32 devices in a mesh: gx: 4 (over y, x), gy: 8 (over z, core).
Axes of the slice: x: 2, y: 2, z: 4, core: 2. Of those that a mesh axis runs over, the one named last changes fastest.
Arguments:
- initial_state: float32 [3, 128, 24576], P(None, 'gx', 'gy'), may hold values from -6 to 6
- beam_dir: float32 [3, 128], P(None, ('gx', 'gy')), may hold values from -4 to 4
- gate_obs: float32 [3, 32, 32, 128], P(None, ('gx', 'gy')), may hold values from -6 to 6
- slot_beam: int32 [32, 32, 128], P(('gx', 'gy')), may hold values from -1 to 3, as said below
- slot_cell: int32 [32, 32, 128], P(('gx', 'gy')), may hold values from 0 to 98303, as said below
Outputs:
- gradient: float32 [3, 128, 24576], P(None, 'gx', 'gy')
The draws below stay inside these ranges and needn't reach their ends.
Inputs may be any that keep to these rules, and one draw needn't show every extreme that they name: `slot_beam`: each of an owner's 4 beams fills exactly 512 slots over all of that owner's lists. In every list the used slots come first. Each owner's list for one common tile is full, so that tile receives 128 used slots from every owner. `slot_cell`: A cell index within the tile, of 32 x 32 x 96 cells with the streamwise index slowest and the vertical fastest; empty slots also hold a valid index.
All inputs are finite; a program needn't handle non-finite values.
Results may differ from the reference program's by a relative error of at most 0.00015.
Values sent between devices are 32-bit elements; how exact they have to be, the bound alone decides.
No kernel may reach another device: no remote copies, remote signals or barrier semaphores. Data moves between devices by JAX's collectives and lax.ppermute only.
A program may use at most 128 MiB of HBM per device.

```python
import jax
import jax.numpy as jnp
from jax import lax

CX = 32
CY = 32
NZ = 96
STEPS = 3
GATES = 512
BEAMS_DEV = 4
CAP = 128
BEAMS = 128
NX = 128
NY = 256
N_GX = 4
N_GY = 8
DEVICES = 32


def slot_layout(key):
    peers = N_GX * N_GY
    half = CAP // 2
    base = jax.random.fold_in(key, 7001)
    favoured = jax.random.randint(jax.random.fold_in(base, 1), (), 0, peers).astype(jnp.int32)
    owner_keys = jax.random.split(jax.random.fold_in(base, 2), peers)

    def one_owner(owner_key):
        key_order, key_shift, key_gates = jax.random.split(owner_key, 3)
        order = jax.random.permutation(key_order, peers).astype(jnp.int32)
        position = jnp.argmax(order == favoured)
        order = order.at[position].set(order[0]).at[0].set(favoured)
        shifts = jax.random.randint(key_shift, (peers // 2,), -half, half + 1).astype(jnp.int32).at[0].set(half)
        counts = jnp.zeros((peers,), jnp.int32).at[order[0::2]].set(half + shifts).at[order[1::2]].set(half - shifts)
        starts = jnp.cumsum(counts) - counts
        slots = jnp.arange(CAP, dtype=jnp.int32)[None, :]
        live = slots < counts[:, None]
        gate = jnp.minimum(starts[:, None] + slots, peers * half - 1)
        gate_order = jax.random.permutation(key_gates, peers * half).astype(jnp.int32)
        return jnp.where(live, gate_order[gate] // GATES, -1).astype(jnp.int32)
    return jax.vmap(one_owner)(owner_keys)


def draw_slot_beam(key, part):
    return slot_layout(key)


def draw_slot_cell(key, part):
    peers = N_GX * N_GY
    return jax.random.randint(jax.random.fold_in(key, 7002), (peers, peers, CAP), 0, CX * CY * NZ).astype(jnp.int32)


def levels(rng, extent, cuts, least, high):
    level = 1.0
    for dim, blocks in cuts:
        draws = jax.random.uniform(jax.random.fold_in(jax.random.fold_in(rng, 6), dim), (blocks,), jnp.float32, least / len(cuts), high / len(cuts))
        level = level * jnp.repeat(jnp.exp(draws), extent[dim] // blocks).reshape((-1,) + (1,) * (len(extent) - 1 - dim))
    return level


def scatter_about(stream_key, shape, spread, reach, shards=(), kind=jnp.bfloat16):
    level = levels(stream_key, shape, shards, -0.22, 0.18) if shards else 1.0
    entries = jax.random.normal(stream_key, shape, jnp.float32) * spread * level
    return jnp.minimum(jnp.maximum(entries, -reach), reach).astype(kind)


def setup_inputs(seed: int = 0) -> dict:
    key_of = jax.random.split(jax.random.key(seed), 6)
    return {
        "initial_state": scatter_about(key_of[0], (3, NX, NY * NZ), 1.0, 6.0, ((1, 4), (2, 8)), jnp.float32),
        "beam_dir": scatter_about(key_of[1], (3, BEAMS), 0.7, 4.0, ((1, 32),), jnp.float32),
        "gate_obs": scatter_about(key_of[2], (STEPS, DEVICES, DEVICES, CAP), 1.0, 6.0, ((1, 32),), jnp.float32),
        "slot_beam": draw_slot_beam(jax.random.fold_in(key_of[5], 71), 0),
        "slot_cell": draw_slot_cell(jax.random.fold_in(key_of[5], 71), 0),
    }


TIME_STEP = 0.2
VISCOSITY = 0.5

def step_core(padded):
    centre = padded[:, 1:-1, NZ:-NZ]
    fore_cell = padded[:, 2:, NZ:-NZ]
    back_cell = padded[:, :-2, NZ:-NZ]
    right_cell = padded[:, 1:-1, 2 * NZ:]
    left_cell = padded[:, 1:-1, :-2 * NZ]
    level = lax.broadcasted_iota(jnp.int32, centre.shape, 2) % NZ
    upper_cell = jnp.where(level < NZ - 1, jnp.roll(centre, -1, axis=2), 0.0)
    lower_cell = jnp.where(level > 0, jnp.roll(centre, 1, axis=2), 0.0)
    laplace = fore_cell + back_cell + right_cell + left_cell + upper_cell + lower_cell - 6.0 * centre
    advect = centre[0:1] * (fore_cell - back_cell) * 0.5
    advect = advect + centre[1:2] * (right_cell - left_cell) * 0.5
    advect = advect + centre[2:3] * (upper_cell - lower_cell) * 0.5
    return centre + TIME_STEP * (VISCOSITY * laplace - advect)

def advance(state):
    return step_core(jnp.pad(state, ((0, 0), (1, 1), (NZ, NZ))))

def reference(initial_state, beam_dir, gate_obs, slot_beam, slot_cell):
    peers = N_GX * N_GY
    row_len = CY * NZ
    owner = jnp.arange(peers, dtype=jnp.int32)[:, None, None]
    tile = jnp.arange(peers, dtype=jnp.int32)[None, :, None]
    x_index = tile // N_GY * CX + slot_cell // row_len
    y_index = tile % N_GY * row_len + slot_cell % row_len
    used = slot_beam >= 0
    beam_ids = jnp.where(used, owner * BEAMS_DEV + slot_beam, peers * BEAMS_DEV).astype(jnp.int32)
    safe_ids = jnp.minimum(beam_ids, peers * BEAMS_DEV - 1)
    slot_dir = jnp.where(used[None], beam_dir[:, safe_ids], 0.0)
    flat_ids = beam_ids.reshape(-1)
    count = peers * BEAMS_DEV + 1

    def beam_mean(values):
        sums = jax.ops.segment_sum(values.reshape(-1), flat_ids, num_segments=count)
        return (sums / GATES)[flat_ids].reshape(values.shape)
    centred = [jnp.where(used, gate_obs[moment] - beam_mean(gate_obs[moment]), 0.0) for moment in range(STEPS)]

    def forcing(state, moment):
        seen = lax.optimization_barrier(jnp.sum(slot_dir * state[:, x_index, y_index], axis=0))
        misfit = jnp.where(used, seen - beam_mean(seen) - centred[moment], 0.0)
        return jnp.zeros_like(state).at[:, x_index, y_index].add(slot_dir * misfit)
    states = [initial_state]
    for moment in range(STEPS):
        states.append(advance(states[-1]))
    adjoint = forcing(states[STEPS], STEPS - 1)
    for moment in range(STEPS - 1, -1, -1):
        unused_out, pull = jax.vjp(advance, states[moment])
        adjoint = pull(adjoint)[0]
        if moment > 0:
            adjoint = adjoint + forcing(states[moment], moment - 1)
    return adjoint
```

```python
import functools

import jax
import jax.numpy as jnp
from jax import lax
from jax.experimental import pallas as pl
from jax.experimental.pallas import tpu as pltpu
from jax.sharding import PartitionSpec as P

NZ = 96
GATES = 512
STEPS = 3
LANES = 128
CX = 32
CY = 32
COLUMNS = CX * CY
RIM = 5
PAD = 8
XH = CX + 2 * PAD
YH = CY + 2 * RIM
PACKED = CX * NZ // LANES
FRIM = 3
FH = CY + 2 * FRIM
FIELDS = 3 * STEPS
BLOCK = 512
F32 = jnp.float32
BF16 = jnp.bfloat16
AXES = ("gx", "gy")
VMEM_LIMIT = 60 * 1024 * 1024


def call(kernel, outs, scratch=(), flops=0):
    return pl.pallas_call(
        kernel,
        out_shape=outs,
        scratch_shapes=list(scratch),
        compiler_params=pltpu.CompilerParams(vmem_limit_bytes=VMEM_LIMIT),
        cost_estimate=pl.CostEstimate(flops=flops, bytes_accessed=1 << 20, transcendentals=0),
    )


def shape(*dims):
    return jax.ShapeDtypeStruct(dims, F32)


def lane_of(rows=8):
    return lax.broadcasted_iota(jnp.int32, (rows, LANES), 1)


def pack(put, block):
    lane = lane_of()
    last = block[24:32]
    for j in range(3):
        tail = pltpu.roll(last, 96 - 32 * j, axis=1)
        put(8 * j, jnp.where(lane < NZ, block[8 * j : 8 * j + 8], tail))


def unpack(rows):
    lane = lane_of()
    last = jnp.zeros((8, LANES), F32)
    parts = []
    for j in range(3):
        piece = rows[8 * j : 8 * j + 8]
        parts.append(jnp.where(lane < NZ, piece, 0.0))
        moved = pltpu.roll(piece, (32 * j - 96) % LANES, axis=1)
        last = jnp.where((lane >= 32 * j) & (lane < 32 * j + 32), moved, last)
    return jnp.concatenate(parts + [last], axis=0)


def column_block(ref, comp, y):
    return ref[comp, :, NZ * y : NZ * y + NZ]


def widen(block):
    return jnp.concatenate([block, jnp.zeros((block.shape[0], LANES - NZ), F32)], axis=1)


def corner_rows(rim):
    rows, out = 0, []
    for comp in range(3):
        for dist in range(1, rim):
            out.append((comp, dist, rows, rim - dist))
            rows += 2 * (rim - dist)
    return out, rows


STATE_CORNERS, STATE_CORNER_ROWS = corner_rows(RIM)
STATE_PIECE = 3 * RIM * PACKED + 64
FORCE_BLOCKS = [(n, c, i) for n in range(STEPS) for c in range(3) for i in range(n + 1)]
FORCE_CORNERS = [
    (n, c, dist, side, k)
    for n in range(STEPS)
    for c in range(3)
    for dist in range(1, n + 1)
    for side in range(2)
    for k in range(1, n + 2 - dist)
]
FORCE_PIECE = len(FORCE_BLOCKS) * PACKED + 24


def prepare_kernel(state, beam_dir, obs, beam, cell, slots, first_rows, last_rows):
    beams = beam_dir.shape[1]
    owned = beam[0]
    used = owned >= 0
    masks = [owned == k for k in range(beams)]

    def spread(values):
        total = jnp.zeros(owned.shape, F32)
        for k in range(beams):
            total = jnp.where(masks[k], values[k], total)
        return total

    slots[:, 0, :] = cell[0].astype(F32)
    slots[:, 1, :] = owned.astype(F32)
    for n in range(STEPS):
        seen = obs[n, 0]
        means = [jnp.sum(jnp.where(m, seen, 0.0), keepdims=True) / GATES for m in masks]
        slots[:, 2 + n, :] = jnp.where(used, seen - spread(means), 0.0)
    for c in range(3):
        slots[:, 5 + c, :] = spread([beam_dir[c : c + 1, k : k + 1] for k in range(beams)])
    for c in range(3):
        first_rows[RIM * c : RIM * c + RIM, :] = state[c, 0:RIM, :]
        last_rows[RIM * c : RIM * c + RIM, :] = state[c, CX - RIM : CX, :]
    first_rows[3 * RIM : 16, :] = jnp.zeros((1, CY * NZ), F32)
    last_rows[3 * RIM : 16, :] = jnp.zeros((1, CY * NZ), F32)


def state_rim_kernel(state, before, after, first_layers, last_layers):
    for out, layer_of in ((first_layers, lambda d: d - 1), (last_layers, lambda d: CY - d)):
        for c in range(3):
            for dist in range(1, RIM + 1):
                base = (c * RIM + dist - 1) * PACKED

                def put(row, rows, base=base, out=out):
                    out[base + row : base + row + 8, :] = rows

                pack(put, widen(column_block(state, c, layer_of(dist))))
        base = 3 * RIM * PACKED
        out[base : base + 64, :] = jnp.zeros((64, LANES), F32)
        for c, dist, row, side in STATE_CORNERS:
            lanes = slice(NZ * layer_of(dist), NZ * layer_of(dist) + NZ)
            out[base + row : base + row + side, 0:NZ] = before[RIM * c + dist : RIM * c + RIM, lanes]
            out[base + row + side : base + row + 2 * side, 0:NZ] = after[RIM * c : RIM * c + side, lanes]


def row_mask(x_place, x_count):
    row = lax.broadcasted_iota(jnp.int32, (XH, LANES), 0)
    lane = lax.broadcasted_iota(jnp.int32, (XH, LANES), 1)
    low = jnp.where(x_place == 0, PAD, 0)
    high = jnp.where(x_place == x_count - 1, PAD + CX, XH)
    return jnp.where((row >= low) & (row < high) & (lane < NZ), 1.0, 0.0).astype(F32)


def layer_mask(y, y_place, y_count):
    outside = ((y < 0) & (y_place == 0)) | ((y >= CY) & (y_place == y_count - 1))
    return jnp.where(outside, 0.0, 1.0).astype(F32)


def next_row(v):
    return pltpu.roll(v, v.shape[0] - 1, axis=0)


def last_row(v):
    return pltpu.roll(v, 1, axis=0)


def next_level(v):
    return pltpu.roll(v, LANES - 1, axis=1)


def last_level(v):
    return pltpu.roll(v, 1, axis=1)


def step_forward(src, dst, low, high, mask, places):
    def layer(i, carry):
        y = i + low
        centre = [src[c, y + RIM] for c in range(3)]
        plus = [0.1 - 0.1 * v for v in centre]
        minus = [0.1 + 0.1 * v for v in centre]
        keep = mask * layer_mask(y, places[2], places[3])
        for c in range(3):
            v = centre[c]
            total = 0.4 * v
            total = total + plus[0] * next_row(v) + minus[0] * last_row(v)
            total = total + plus[1] * src[c, y + RIM + 1] + minus[1] * src[c, y + RIM - 1]
            total = total + plus[2] * next_level(v) + minus[2] * last_level(v)
            dst[c, y + RIM] = total * keep
        return carry

    lax.fori_loop(0, high - low, layer, 0)


def mesh_places():
    return (
        lax.axis_index("gx"),
        lax.axis_size("gx"),
        lax.axis_index("gy"),
        lax.axis_size("gy"),
    )


def slot_columns(slots, row):
    cell = slots[row, 0:1, :]
    x = ((cell + 0.5) * (1.0 / (CY * NZ))).astype(jnp.int32)
    rest = cell.astype(jnp.int32) - x * (CY * NZ)
    y = ((rest.astype(F32) + 0.5) * (1.0 / NZ)).astype(jnp.int32)
    return y * CX + x, rest - y * NZ


def column_hits(columns):
    place = lax.broadcasted_iota(jnp.int32, (COLUMNS, columns.shape[1]), 0)
    return jnp.where(place == columns, 1.0, 0.0).astype(BF16)


def block_places(slots, block):
    rows = [slot_columns(slots, block * (BLOCK // LANES) + r) for r in range(BLOCK // LANES)]
    columns = jnp.concatenate([r[0] for r in rows], axis=1)
    level = jnp.concatenate([r[1] for r in rows], axis=1)
    here = lax.broadcasted_iota(jnp.int32, (NZ, BLOCK), 0) == level
    return column_hits(columns), here


def block_values(slots, block, which):
    rows = [slots[block * (BLOCK // LANES) + r, which : which + 1, :] for r in range(BLOCK // LANES)]
    return jnp.concatenate(rows, axis=1)


def forward_kernel(
    beams, per_row, state, before, after, below, above, slots, seen, sums, s0, s1, s2, s3, table
):
    places = mesh_places()
    mask = row_mask(places[0], places[1])
    s0[...] = jnp.zeros(s0.shape, F32)
    for c in range(3):
        for y in range(CY):
            lanes = slice(NZ * y, NZ * y + NZ)
            s0[c, RIM + y, PAD : PAD + CX, 0:NZ] = state[c, :, lanes]
            s0[c, RIM + y, PAD - RIM : PAD, 0:NZ] = before[RIM * c : RIM * c + RIM, lanes]
            s0[c, RIM + y, PAD + CX : PAD + CX + RIM, 0:NZ] = after[RIM * c : RIM * c + RIM, lanes]
    for piece, layer_of in ((above, lambda d: RIM + CY - 1 + d), (below, lambda d: RIM - d)):
        for c in range(3):
            for dist in range(1, RIM + 1):
                base = (c * RIM + dist - 1) * PACKED
                s0[c, layer_of(dist), PAD : PAD + CX, :] = unpack(piece[base : base + PACKED, :])
        base = 3 * RIM * PACKED
        for c, dist, row, side in STATE_CORNERS:
            s0[c, layer_of(dist), PAD - side : PAD, :] = piece[base + row : base + row + side, :]
            s0[c, layer_of(dist), PAD + CX : PAD + CX + side, :] = piece[
                base + row + side : base + row + 2 * side, :
            ]
    step_forward(s0, s1, -4, CY + 4, mask, places)
    step_forward(s1, s2, -3, CY + 3, mask, places)
    step_forward(s2, s3, 0, CY, mask, places)

    half = FIELDS * NZ
    for n, field in enumerate((s1, s2, s3)):
        for c in range(3):
            tile = field[c, RIM : RIM + CY, PAD : PAD + CX, :].reshape(COLUMNS, LANES)
            turned = tile.T[0:NZ]
            high = turned.astype(BF16)
            base = (3 * n + c) * NZ
            table[base : base + NZ, :] = high
            table[half + base : half + base + NZ, :] = (turned - high.astype(F32)).astype(BF16)

    def gather(block, carry):
        hits, here = block_places(slots, block)
        found = jnp.dot(table[...], hits, preferred_element_type=F32)
        weights = [block_values(slots, block, 5 + c) for c in range(3)]
        for n in range(STEPS):
            total = jnp.zeros((1, BLOCK), F32)
            for c in range(3):
                base = (3 * n + c) * NZ
                both = found[base : base + NZ] + found[half + base : half + base + NZ]
                value = jnp.sum(jnp.where(here, both, 0.0), axis=0, keepdims=True)
                total = total + weights[c] * value
            for r in range(BLOCK // LANES):
                seen[n, pl.ds(block * (BLOCK // LANES) + r, 1), :] = total[:, LANES * r : LANES * r + LANES]
        return carry

    rows = slots.shape[0]
    lax.fori_loop(0, rows * LANES // BLOCK, gather, 0)

    beam = row_beam(beams, per_row, slots)
    lane = lax.broadcasted_iota(jnp.int32, (rows, LANES), 1)
    partial = jnp.zeros((rows, LANES), F32)
    for n in range(STEPS):
        values = seen[n]
        for k in range(per_row):
            one = jnp.sum(jnp.where(beam == k, values, 0.0), axis=1, keepdims=True)
            partial = jnp.where(lane == n * per_row + k, one, partial)
    turned = jnp.concatenate([partial, jnp.zeros((LANES - rows, LANES), F32)], axis=0).T
    per_line = LANES // rows
    sums[...] = jnp.zeros(sums.shape, F32)
    for line in range(STEPS * per_row // per_line):
        total = turned[line * per_line : line * per_line + 1]
        for k in range(1, per_line):
            one = turned[line * per_line + k : line * per_line + k + 1]
            total = total + pltpu.roll(one, rows * k, axis=1)
        sums[:, line : line + 1, :] = jnp.broadcast_to(total[None], (sums.shape[0], 1, LANES))


def row_beam(beams, per_row, slots):
    group = per_row // beams
    lane = lax.broadcasted_iota(jnp.int32, (slots.shape[0], LANES), 1)
    beam = slots[:, 1, :].astype(jnp.int32)
    for g in range(1, group):
        beam = beam + jnp.where(lane >= g * (LANES // group), beams, 0)
    return beam


def force_kernel(beams, per_row, slots, seen, sums, force, first_rows, last_rows, total, weight):
    rows = slots.shape[0]
    per_line = LANES // rows
    lines = jnp.sum(sums[...], axis=0) / GATES
    count = STEPS * per_row
    spread = []
    for k in range(count):
        line = lines[k // per_line : k // per_line + 1]
        spread.append(pltpu.roll(line, (-rows * (k % per_line)) % LANES, axis=1))
    spread.append(jnp.zeros((LANES - count, LANES), F32))
    means = jnp.concatenate(spread, axis=0).T[0:rows]
    beam = row_beam(beams, per_row, slots)
    misfit = []
    for n in range(STEPS):
        mean = jnp.zeros((rows, LANES), F32)
        for k in range(per_row):
            one = means[:, n * per_row + k : n * per_row + k + 1]
            mean = jnp.where(beam == k, one, mean)
        misfit.append(seen[n] - mean - slots[:, 2 + n, :])
    for n in range(STEPS):
        for c in range(3):
            weight[3 * n + c] = slots[:, 5 + c, :] * misfit[n]

    total[...] = jnp.zeros(total.shape, F32)

    def scatter(block, carry):
        hits, here = block_places(slots, block)
        high_rows, low_rows = [], []
        for f in range(FIELDS):
            value = jnp.concatenate(
                [weight[f, pl.ds(block * (BLOCK // LANES) + r, 1), :] for r in range(BLOCK // LANES)],
                axis=1,
            )
            high = value.astype(BF16).astype(F32)
            high_rows.append(jnp.where(here, high, 0.0).astype(BF16))
            low_rows.append(jnp.where(here, value - high, 0.0).astype(BF16))
        table = jnp.concatenate(high_rows + low_rows, axis=0)
        added = lax.dot_general(table, hits, (((1,), (1,)), ((), ())), preferred_element_type=F32)
        for f in range(FIELDS):
            half = FIELDS * NZ
            total[f, 0:NZ, :] += added[NZ * f : NZ * f + NZ] + added[half + NZ * f : half + NZ * f + NZ]
        return carry

    lax.fori_loop(0, rows * LANES // BLOCK, scatter, 0)
    for f in range(FIELDS):
        force[f] = total[f].T.reshape(CY, CX, LANES)
    for out, row_of in ((first_rows, lambda i: i), (last_rows, lambda i: CX - 1 - i)):
        for b, (n, c, i) in enumerate(FORCE_BLOCKS):

            def put(row, rows, b=b, out=out):
                out[b, row : row + 8, :] = rows

            pack(put, force[3 * n + c, :, row_of(i), :])


def rim_rows(piece, which):
    return unpack(piece[which])


def force_rim_kernel(force, before, after, first_layers, last_layers):
    index = {key: b for b, key in enumerate(FORCE_BLOCKS)}
    for out, layer_of in ((first_layers, lambda d: d - 1), (last_layers, lambda d: CY - d)):
        for b, (n, c, i) in enumerate(FORCE_BLOCKS):

            def put(row, rows, b=b, out=out):
                out[b * PACKED + row : b * PACKED + row + 8, :] = rows

            pack(put, force[3 * n + c, layer_of(i + 1)])
        base = len(FORCE_BLOCKS) * PACKED
        for row, (n, c, dist, side, k) in enumerate(FORCE_CORNERS):
            piece = (before, after)[side]
            block = unpack(piece[index[(n, c, k - 1)]])
            y = layer_of(dist)
            out[base + row : base + row + 1, :] = block[y : y + 1]


def backward_kernel(force, before, after, below, above, s0, s1, s2, out, a3, a2, a1, a0):
    places = mesh_places()
    mask = row_mask(places[0], places[1])
    adjoints = (a1, a2, a3)
    for n in range(STEPS):
        adjoints[n][...] = jnp.zeros(adjoints[n].shape, F32)
        for c in range(3):
            adjoints[n][c, FRIM : FRIM + CY, PAD : PAD + CX, :] = force[3 * n + c]
    for b, (n, c, i) in enumerate(FORCE_BLOCKS):
        adjoints[n][c, FRIM : FRIM + CY, PAD - 1 - i, :] = unpack(before[b])
        adjoints[n][c, FRIM : FRIM + CY, PAD + CX + i, :] = unpack(after[b])
    for piece, layer_of in ((above, lambda d: FRIM + CY - 1 + d), (below, lambda d: FRIM - d)):
        for b, (n, c, i) in enumerate(FORCE_BLOCKS):
            adjoints[n][c, layer_of(i + 1), PAD : PAD + CX, :] = unpack(piece[b * PACKED : b * PACKED + PACKED, :])
        base = len(FORCE_BLOCKS) * PACKED
        for row, (n, c, dist, side, k) in enumerate(FORCE_CORNERS):
            x = (PAD - k, PAD + CX - 1 + k)[side]
            adjoints[n][c, layer_of(dist), x : x + 1, :] = piece[base + row : base + row + 1, :]

    def pull(field, source, target, low, high, add):
        def layer(i, carry):
            y = i + low
            v = [field[c, y + RIM] for c in range(3)]
            v_next = [field[c, y + RIM + 1] for c in range(3)]
            v_last = [field[c, y + RIM - 1] for c in range(3)]
            a = [source[c, y + FRIM] for c in range(3)]
            slopes = [
                [next_row(f) - last_row(f) for f in v],
                [n - p for n, p in zip(v_next, v_last)],
                [next_level(f) - last_level(f) for f in v],
            ]
            keep = mask * layer_mask(y, places[2], places[3])
            from_next = [0.1 + 0.1 * f for f in v]
            from_last = [0.1 - 0.1 * f for f in v]
            y_next = 0.1 + 0.1 * v_next[1]
            y_last = 0.1 - 0.1 * v_last[1]
            for c in range(3):
                bend = slopes[c][0] * a[0] + slopes[c][1] * a[1] + slopes[c][2] * a[2]
                total = 0.4 * a[c] - 0.1 * bend
                total = total + next_row(from_next[0] * a[c]) + last_row(from_last[0] * a[c])
                total = total + y_next * source[c, y + FRIM + 1] + y_last * source[c, y + FRIM - 1]
                total = total + next_level(from_next[2] * a[c]) + last_level(from_last[2] * a[c])
                if add:
                    total = total + target[c, y + FRIM]
                target[c, y + FRIM] = total * keep
            return carry

        lax.fori_loop(0, high - low, layer, 0)

    pull(s2, a3, a2, -2, CY + 2, True)
    pull(s1, a2, a1, -1, CY + 1, True)
    pull(s0, a1, a0, 0, CY, False)
    for c in range(3):
        for y in range(CY):
            out[c, :, NZ * y : NZ * y + NZ] = a0[c, FRIM + y, PAD : PAD + CX, 0:NZ]


def shift(values, axis, by):
    count = lax.axis_size(axis)
    return lax.ppermute(values, axis, [(i, i + by) for i in range(count) if 0 <= i + by < count])


def local(initial_state, beam_dir, gate_obs, slot_beam, slot_cell):
    peers, capacity = slot_beam.shape[1:]
    group = LANES // capacity
    beams = beam_dir.shape[1]
    per_row = group * beams
    rows = peers // group
    rim_rows_shape = shape(16, CY * NZ)
    slots, first_rows, last_rows = call(
        prepare_kernel, (shape(peers, 8, capacity), rim_rows_shape, rim_rows_shape)
    )(initial_state, beam_dir, gate_obs, slot_beam, slot_cell)
    after = shift(first_rows, "gx", -1)
    before = shift(last_rows, "gx", 1)
    slots = lax.all_to_all(slots, AXES, split_axis=0, concat_axis=0, tiled=True)
    if group > 1:
        slots = slots.reshape(rows, group, 8, capacity).transpose(0, 2, 1, 3).reshape(rows, 8, LANES)
    piece = shape(STATE_PIECE, LANES)
    first_layers, last_layers = call(state_rim_kernel, (piece, piece))(initial_state, before, after)
    above = shift(first_layers, "gy", -1)
    below = shift(last_layers, "gy", 1)
    lines = -(-STEPS * per_row * rows // LANES // 8) * 8
    field = shape(3, YH, XH, LANES)
    seen, sums, s0, s1, s2 = call(
        functools.partial(forward_kernel, beams, per_row),
        (shape(STEPS, rows, LANES), shape(peers, lines, LANES), field, field, field),
        [pltpu.VMEM(field.shape, F32), pltpu.VMEM((2 * FIELDS * NZ, COLUMNS), BF16)],
    )(initial_state, before, after, below, above, slots)
    sums = lax.all_to_all(sums, AXES, split_axis=0, concat_axis=0, tiled=True)
    rim = shape(len(FORCE_BLOCKS), PACKED, LANES)
    force, first_rows, last_rows = call(
        functools.partial(force_kernel, beams, per_row),
        (shape(FIELDS, CY, CX, LANES), rim, rim),
        [pltpu.VMEM((FIELDS, LANES, COLUMNS), F32), pltpu.VMEM((FIELDS, rows, LANES), F32)],
    )(slots, seen, sums)
    after = shift(first_rows, "gx", -1)
    before = shift(last_rows, "gx", 1)
    piece = shape(FORCE_PIECE, LANES)
    first_layers, last_layers = call(force_rim_kernel, (piece, piece))(force, before, after)
    above = shift(first_layers, "gy", -1)
    below = shift(last_layers, "gy", 1)
    padded = pltpu.VMEM((3, FH, XH, LANES), F32)
    return call(backward_kernel, shape(*initial_state.shape), [padded] * 4)(
        force, before, after, below, above, s0, s1, s2
    )


def solution(mesh):
    in_specs = (
        P(None, "gx", "gy"),
        P(None, ("gx", "gy")),
        P(None, ("gx", "gy"), None, None),
        P(("gx", "gy"), None, None),
        P(("gx", "gy"), None, None),
    )
    out_specs = P(None, "gx", "gy")
    return jax.shard_map(local, mesh=mesh, in_specs=in_specs, out_specs=out_specs, check_vma=False)
```

```python
import functools

import jax
import jax.numpy as jnp
from jax import lax
from jax.experimental import pallas as pl
from jax.experimental.pallas import tpu as pltpu
from jax.sharding import PartitionSpec as P

NZ = 96
GATES = 512
STEPS = 3
LANES = 128
CX = 32
CY = 32
COLUMNS = CX * CY
RIM = 5
PAD = 8
XH = CX + 2 * PAD
YH = CY + 2 * RIM
PACKED = CX * NZ // LANES
FRIM = 3
FH = CY + 2 * FRIM
FIELDS = 3 * STEPS
BLOCK = 512
F32 = jnp.float32
BF16 = jnp.bfloat16
AXES = ("gx", "gy")
MIB = 1024 * 1024


def call(kernel, outs, scratch=(), limit=12, far_in=(), ins=0, far_out=()):
    def specs(count, far):
        spaces = [pl.ANY if i in far else pltpu.VMEM for i in range(count)]
        return [pl.BlockSpec(memory_space=space) for space in spaces]

    single = not isinstance(outs, tuple)
    out_specs = specs(1 if single else len(outs), far_out)
    return pl.pallas_call(
        kernel,
        out_shape=outs,
        in_specs=specs(ins, far_in),
        out_specs=out_specs[0] if single else tuple(out_specs),
        scratch_shapes=list(scratch),
        compiler_params=pltpu.CompilerParams(vmem_limit_bytes=limit * MIB),
    )


def shape(*dims):
    return jax.ShapeDtypeStruct(dims, F32)


def lane_of(rows=8):
    return lax.broadcasted_iota(jnp.int32, (rows, LANES), 1)


def pack(put, block):
    lane = lane_of()
    last = block[24:32]
    for j in range(3):
        tail = pltpu.roll(last, 96 - 32 * j, axis=1)
        put(8 * j, jnp.where(lane < NZ, block[8 * j : 8 * j + 8], tail))


def unpack(rows):
    lane = lane_of()
    last = jnp.zeros((8, LANES), F32)
    parts = []
    for j in range(3):
        piece = rows[8 * j : 8 * j + 8]
        parts.append(jnp.where(lane < NZ, piece, 0.0))
        moved = pltpu.roll(piece, (32 * j - 96) % LANES, axis=1)
        last = jnp.where((lane >= 32 * j) & (lane < 32 * j + 32), moved, last)
    return jnp.concatenate(parts + [last], axis=0)


def column_block(ref, comp, y):
    return ref[comp, :, NZ * y : NZ * y + NZ]


def widen(block):
    return jnp.concatenate([block, jnp.zeros((block.shape[0], LANES - NZ), F32)], axis=1)


def corner_rows(rim):
    rows, out = 0, []
    for comp in range(3):
        for dist in range(1, rim):
            out.append((comp, dist, rows, rim - dist))
            rows += 2 * (rim - dist)
    return out, rows


STATE_CORNERS, STATE_CORNER_ROWS = corner_rows(RIM)
STATE_PIECE = 3 * RIM * PACKED + 64
FORCE_BLOCKS = [(n, c, i) for n in range(STEPS) for c in range(3) for i in range(n + 1)]
FORCE_CORNERS = [
    (n, c, dist, side, k)
    for n in range(STEPS)
    for c in range(3)
    for dist in range(1, n + 1)
    for side in range(2)
    for k in range(1, n + 2 - dist)
]
FORCE_PIECE = len(FORCE_BLOCKS) * PACKED + 24


def prepare_kernel(state, beam_dir, obs, beam, cell, slots, first_rows, last_rows):
    beams = beam_dir.shape[1]
    owned = beam[0]
    used = owned >= 0
    masks = [owned == k for k in range(beams)]

    def spread(values):
        total = jnp.zeros(owned.shape, F32)
        for k in range(beams):
            total = jnp.where(masks[k], values[k], total)
        return total

    slots[:, 0, :] = cell[0].astype(F32)
    slots[:, 1, :] = owned.astype(F32)
    for n in range(STEPS):
        seen = obs[n, 0]
        means = [jnp.sum(jnp.where(m, seen, 0.0), keepdims=True) / GATES for m in masks]
        slots[:, 2 + n, :] = jnp.where(used, seen - spread(means), 0.0)
    for c in range(3):
        slots[:, 5 + c, :] = spread([beam_dir[c : c + 1, k : k + 1] for k in range(beams)])
    for c in range(3):
        first_rows[RIM * c : RIM * c + RIM, :] = state[c, 0:RIM, :]
        last_rows[RIM * c : RIM * c + RIM, :] = state[c, CX - RIM : CX, :]
    first_rows[3 * RIM : 16, :] = jnp.zeros((1, CY * NZ), F32)
    last_rows[3 * RIM : 16, :] = jnp.zeros((1, CY * NZ), F32)


def state_rim_kernel(state, before, after, first_layers, last_layers):
    for out, layer_of in ((first_layers, lambda d: d - 1), (last_layers, lambda d: CY - d)):
        for c in range(3):
            for dist in range(1, RIM + 1):
                base = (c * RIM + dist - 1) * PACKED

                def put(row, rows, base=base, out=out):
                    out[base + row : base + row + 8, :] = rows

                pack(put, widen(column_block(state, c, layer_of(dist))))
        base = 3 * RIM * PACKED
        out[base : base + 64, :] = jnp.zeros((64, LANES), F32)
        for c, dist, row, side in STATE_CORNERS:
            lanes = slice(NZ * layer_of(dist), NZ * layer_of(dist) + NZ)
            out[base + row : base + row + side, 0:NZ] = before[RIM * c + dist : RIM * c + RIM, lanes]
            out[base + row + side : base + row + 2 * side, 0:NZ] = after[RIM * c : RIM * c + side, lanes]


def row_mask(x_place, x_count):
    row = lax.broadcasted_iota(jnp.int32, (XH, LANES), 0)
    lane = lax.broadcasted_iota(jnp.int32, (XH, LANES), 1)
    low = jnp.where(x_place == 0, PAD, 0)
    high = jnp.where(x_place == x_count - 1, PAD + CX, XH)
    return jnp.where((row >= low) & (row < high) & (lane < NZ), 1.0, 0.0).astype(F32)


def layer_mask(y, y_place, y_count):
    outside = ((y < 0) & (y_place == 0)) | ((y >= CY) & (y_place == y_count - 1))
    return jnp.where(outside, 0.0, 1.0).astype(F32)


def next_level(v):
    return pltpu.roll(v, LANES - 1, axis=1)


def last_level(v):
    return pltpu.roll(v, 1, axis=1)


def step_forward(src, dst, low, high, first_row, chunks, mask, places):
    def layer(i, carry):
        y = i + low
        keep = layer_mask(y, places[2], places[3])
        done = []
        for t in range(chunks):
            r = first_row + 8 * t
            here, ahead, behind = pl.ds(r, 8), pl.ds(r + 1, 8), pl.ds(r - 1, 8)
            centre = [src[c, y + RIM, here, :] for c in range(3)]
            scaled = [0.1 * v for v in centre]
            plus = [0.1 - v for v in scaled]
            minus = [0.1 + v for v in scaled]
            inside = mask[here, :] * keep
            for c in range(3):
                v = centre[c]
                total = 0.4 * v + (plus[2] * next_level(v) + minus[2] * last_level(v))
                total = total + (plus[0] * src[c, y + RIM, ahead, :] + minus[0] * src[c, y + RIM, behind, :])
                total = total + (
                    plus[1] * src[c, y + RIM + 1, here, :] + minus[1] * src[c, y + RIM - 1, here, :]
                )
                done.append((c, here, total * inside))
        for c, here, total in done:
            dst[c, y + RIM, here, :] = total
        return carry

    lax.fori_loop(0, high - low, layer, 0, unroll=True)


def mesh_places():
    return (
        lax.axis_index("gx"),
        lax.axis_size("gx"),
        lax.axis_index("gy"),
        lax.axis_size("gy"),
    )


def slot_columns(slots, row):
    cell = slots[row, 0:1, :]
    x = ((cell + 0.5) * (1.0 / (CY * NZ))).astype(jnp.int32)
    rest = cell.astype(jnp.int32) - x * (CY * NZ)
    y = ((rest.astype(F32) + 0.5) * (1.0 / NZ)).astype(jnp.int32)
    return y * CX + x, rest - y * NZ


def column_hits(columns):
    place = lax.broadcasted_iota(jnp.int32, (COLUMNS, columns.shape[1]), 0)
    return jnp.where(place == columns, 1.0, 0.0).astype(BF16)


def block_places(slots, block):
    rows = [slot_columns(slots, block * (BLOCK // LANES) + r) for r in range(BLOCK // LANES)]
    columns = jnp.concatenate([r[0] for r in rows], axis=1)
    level = jnp.concatenate([r[1] for r in rows], axis=1)
    here = lax.broadcasted_iota(jnp.int32, (NZ, BLOCK), 0) == level
    return column_hits(columns), here


def block_values(slots, block, which):
    rows = [slots[block * (BLOCK // LANES) + r, which : which + 1, :] for r in range(BLOCK // LANES)]
    return jnp.concatenate(rows, axis=1)


def forward_kernel(
    beams, per_row, state, before, after, below, above, slots, seen, sums, kept0, kept1, kept2, s0, s1, s2, s3, table, mask, sem
):
    places = mesh_places()
    mask[...] = row_mask(places[0], places[1])
    s0[...] = jnp.zeros(s0.shape, F32)
    for c in range(3):
        for y in range(CY):
            lanes = slice(NZ * y, NZ * y + NZ)
            s0[c, RIM + y, PAD : PAD + CX, 0:NZ] = state[c, :, lanes]
            s0[c, RIM + y, PAD - RIM : PAD, 0:NZ] = before[RIM * c : RIM * c + RIM, lanes]
            s0[c, RIM + y, PAD + CX : PAD + CX + RIM, 0:NZ] = after[RIM * c : RIM * c + RIM, lanes]
    for piece, layer_of in ((above, lambda d: RIM + CY - 1 + d), (below, lambda d: RIM - d)):
        for c in range(3):
            for dist in range(1, RIM + 1):
                base = (c * RIM + dist - 1) * PACKED
                s0[c, layer_of(dist), PAD : PAD + CX, :] = unpack(piece[base : base + PACKED, :])
        base = 3 * RIM * PACKED
        for c, dist, row, side in STATE_CORNERS:
            s0[c, layer_of(dist), PAD - side : PAD, :] = piece[base + row : base + row + side, :]
            s0[c, layer_of(dist), PAD + CX : PAD + CX + side, :] = piece[
                base + row + side : base + row + 2 * side, :
            ]
    keeps = [
        pltpu.make_async_copy(field, kept, sem.at[n])
        for n, (field, kept) in enumerate(((s0, kept0), (s1, kept1), (s2, kept2)))
    ]
    keeps[0].start()
    step_forward(s0, s1, -4, CY + 4, 4, 5, mask, places)
    keeps[1].start()
    step_forward(s1, s2, -3, CY + 3, 4, 5, mask, places)
    keeps[2].start()
    step_forward(s2, s3, 0, CY, PAD, 4, mask, places)

    half = FIELDS * NZ
    for n, field in enumerate((s1, s2, s3)):
        for c in range(3):
            tile = field[c, RIM : RIM + CY, PAD : PAD + CX, :].reshape(COLUMNS, LANES)
            turned = tile.T[0:NZ]
            high = turned.astype(BF16)
            base = (3 * n + c) * NZ
            table[base : base + NZ, :] = high
            table[half + base : half + base + NZ, :] = (turned - high.astype(F32)).astype(BF16)

    def gather(block, carry):
        hits, here = block_places(slots, block)
        found = jnp.dot(table[...], hits, preferred_element_type=F32)
        weights = [block_values(slots, block, 5 + c) for c in range(3)]
        for n in range(STEPS):
            total = jnp.zeros((1, BLOCK), F32)
            for c in range(3):
                base = (3 * n + c) * NZ
                both = found[base : base + NZ] + found[half + base : half + base + NZ]
                value = jnp.sum(jnp.where(here, both, 0.0), axis=0, keepdims=True)
                total = total + weights[c] * value
            for r in range(BLOCK // LANES):
                seen[n, pl.ds(block * (BLOCK // LANES) + r, 1), :] = total[:, LANES * r : LANES * r + LANES]
        return carry

    rows = slots.shape[0]
    lax.fori_loop(0, rows * LANES // BLOCK, gather, 0)

    beam = row_beam(beams, per_row, slots)
    lane = lax.broadcasted_iota(jnp.int32, (rows, LANES), 1)
    partial = jnp.zeros((rows, LANES), F32)
    for n in range(STEPS):
        values = seen[n]
        for k in range(per_row):
            one = jnp.sum(jnp.where(beam == k, values, 0.0), axis=1, keepdims=True)
            partial = jnp.where(lane == n * per_row + k, one, partial)
    turned = jnp.concatenate([partial, jnp.zeros((LANES - rows, LANES), F32)], axis=0).T
    per_line = LANES // rows
    sums[...] = jnp.zeros(sums.shape, F32)
    for line in range(STEPS * per_row // per_line):
        total = turned[line * per_line : line * per_line + 1]
        for k in range(1, per_line):
            one = turned[line * per_line + k : line * per_line + k + 1]
            total = total + pltpu.roll(one, rows * k, axis=1)
        sums[:, line : line + 1, :] = jnp.broadcast_to(total[None], (sums.shape[0], 1, LANES))
    for keep in keeps:
        keep.wait()


def row_beam(beams, per_row, slots):
    group = per_row // beams
    lane = lax.broadcasted_iota(jnp.int32, (slots.shape[0], LANES), 1)
    beam = slots[:, 1, :].astype(jnp.int32)
    for g in range(1, group):
        beam = beam + jnp.where(lane >= g * (LANES // group), beams, 0)
    return beam


def force_kernel(beams, per_row, slots, seen, sums, force, first_rows, last_rows, total, weight):
    rows = slots.shape[0]
    per_line = LANES // rows
    lines = jnp.sum(sums[...], axis=0) / GATES
    count = STEPS * per_row
    spread = []
    for k in range(count):
        line = lines[k // per_line : k // per_line + 1]
        spread.append(pltpu.roll(line, (-rows * (k % per_line)) % LANES, axis=1))
    spread.append(jnp.zeros((LANES - count, LANES), F32))
    means = jnp.concatenate(spread, axis=0).T[0:rows]
    beam = row_beam(beams, per_row, slots)
    misfit = []
    for n in range(STEPS):
        mean = jnp.zeros((rows, LANES), F32)
        for k in range(per_row):
            one = means[:, n * per_row + k : n * per_row + k + 1]
            mean = jnp.where(beam == k, one, mean)
        misfit.append(seen[n] - mean - slots[:, 2 + n, :])
    for n in range(STEPS):
        for c in range(3):
            weight[3 * n + c] = slots[:, 5 + c, :] * misfit[n]

    total[...] = jnp.zeros(total.shape, F32)

    def scatter(block, carry):
        hits, here = block_places(slots, block)
        high_rows, low_rows = [], []
        for f in range(FIELDS):
            value = jnp.concatenate(
                [weight[f, pl.ds(block * (BLOCK // LANES) + r, 1), :] for r in range(BLOCK // LANES)],
                axis=1,
            )
            high = value.astype(BF16).astype(F32)
            high_rows.append(jnp.where(here, high, 0.0).astype(BF16))
            low_rows.append(jnp.where(here, value - high, 0.0).astype(BF16))
        table = jnp.concatenate(high_rows + low_rows, axis=0)
        added = lax.dot_general(table, hits, (((1,), (1,)), ((), ())), preferred_element_type=F32)
        for f in range(FIELDS):
            half = FIELDS * NZ
            total[f, 0:NZ, :] += added[NZ * f : NZ * f + NZ] + added[half + NZ * f : half + NZ * f + NZ]
        return carry

    lax.fori_loop(0, rows * LANES // BLOCK, scatter, 0)
    for f in range(FIELDS):
        force[f] = total[f].T.reshape(CY, CX, LANES)
    for out, row_of in ((first_rows, lambda i: i), (last_rows, lambda i: CX - 1 - i)):
        for b, (n, c, i) in enumerate(FORCE_BLOCKS):

            def put(row, rows, b=b, out=out):
                out[b, row : row + 8, :] = rows

            pack(put, force[3 * n + c, :, row_of(i), :])


def rim_rows(piece, which):
    return unpack(piece[which])


def force_rim_kernel(force, before, after, first_layers, last_layers):
    index = {key: b for b, key in enumerate(FORCE_BLOCKS)}
    for out, layer_of in ((first_layers, lambda d: d - 1), (last_layers, lambda d: CY - d)):
        for b, (n, c, i) in enumerate(FORCE_BLOCKS):

            def put(row, rows, b=b, out=out):
                out[b * PACKED + row : b * PACKED + row + 8, :] = rows

            pack(put, force[3 * n + c, layer_of(i + 1)])
        base = len(FORCE_BLOCKS) * PACKED
        for row, (n, c, dist, side, k) in enumerate(FORCE_CORNERS):
            piece = (before, after)[side]
            block = unpack(piece[index[(n, c, k - 1)]])
            y = layer_of(dist)
            out[base + row : base + row + 1, :] = block[y : y + 1]


def backward_kernel(
    force, before, after, below, above, kept0, kept1, kept2, out, s0, s1, s2, a3, a2, a1, a0, mask, sem
):
    loads = [
        pltpu.make_async_copy(kept, field, sem.at[n])
        for n, (field, kept) in enumerate(((s0, kept0), (s1, kept1), (s2, kept2)))
    ]
    for n in (2, 1, 0):
        loads[n].start()
    places = mesh_places()
    mask[...] = row_mask(places[0], places[1])
    adjoints = (a1, a2, a3)
    for n in range(STEPS):
        adjoints[n][...] = jnp.zeros(adjoints[n].shape, F32)
        for c in range(3):
            adjoints[n][c, FRIM : FRIM + CY, PAD : PAD + CX, :] = force[3 * n + c]
    for b, (n, c, i) in enumerate(FORCE_BLOCKS):
        adjoints[n][c, FRIM : FRIM + CY, PAD - 1 - i, :] = unpack(before[b])
        adjoints[n][c, FRIM : FRIM + CY, PAD + CX + i, :] = unpack(after[b])
    for piece, layer_of in ((above, lambda d: FRIM + CY - 1 + d), (below, lambda d: FRIM - d)):
        for b, (n, c, i) in enumerate(FORCE_BLOCKS):
            adjoints[n][c, layer_of(i + 1), PAD : PAD + CX, :] = unpack(piece[b * PACKED : b * PACKED + PACKED, :])
        base = len(FORCE_BLOCKS) * PACKED
        for row, (n, c, dist, side, k) in enumerate(FORCE_CORNERS):
            x = (PAD - k, PAD + CX - 1 + k)[side]
            adjoints[n][c, layer_of(dist), x : x + 1, :] = piece[base + row : base + row + 1, :]

    def pull(field, source, target, low, high, first_row, chunks, add):
        def layer(i, carry):
            y = i + low
            keep = layer_mask(y, places[2], places[3])
            done = []
            for t in range(chunks):
                r = first_row + 8 * t
                here, ahead, behind = pl.ds(r, 8), pl.ds(r + 1, 8), pl.ds(r - 1, 8)
                v = [field[c, y + RIM, here, :] for c in range(3)]
                v_ahead = [field[c, y + RIM, ahead, :] for c in range(3)]
                v_behind = [field[c, y + RIM, behind, :] for c in range(3)]
                v_next = [field[c, y + RIM + 1, here, :] for c in range(3)]
                v_last = [field[c, y + RIM - 1, here, :] for c in range(3)]
                a = [source[c, y + FRIM, here, :] for c in range(3)]
                scaled = [0.1 * f for f in a]
                bends = [None] * 3
                for d, (up, down) in enumerate(((v_ahead, v_behind), (v_next, v_last), (None, None))):
                    for c in range(3):
                        u, w = (up[c], down[c]) if d < 2 else (next_level(v[c]), last_level(v[c]))
                        part = (u - w) * scaled[c]
                        bends[d] = part if bends[d] is None else bends[d] + part
                x_ahead = 0.1 + 0.1 * v_ahead[0]
                x_behind = 0.1 - 0.1 * v_behind[0]
                y_next = 0.1 + 0.1 * v_next[1]
                y_last = 0.1 - 0.1 * v_last[1]
                inside = mask[here, :] * keep
                for c in range(3):
                    total = 0.4 * a[c] - bends[c]
                    total = total + (
                        x_ahead * source[c, y + FRIM, ahead, :] + x_behind * source[c, y + FRIM, behind, :]
                    )
                    total = total + (
                        y_next * source[c, y + FRIM + 1, here, :] + y_last * source[c, y + FRIM - 1, here, :]
                    )
                    product = v[2] * scaled[c]
                    total = total + (next_level(scaled[c] + product) + last_level(scaled[c] - product))
                    if add:
                        total = total + target[c, y + FRIM, here, :]
                    done.append((c, here, total * inside))
            for c, here, total in done:
                target[c, y + FRIM, here, :] = total
            return carry

        lax.fori_loop(0, high - low, layer, 0, unroll=True)

    loads[2].wait()
    pull(s2, a3, a2, -2, CY + 2, 4, 5, True)
    loads[1].wait()
    pull(s1, a2, a1, -1, CY + 1, 4, 5, True)
    loads[0].wait()
    pull(s0, a1, a0, 0, CY, PAD, 4, False)
    for c in range(3):
        for y in range(CY):
            out[c, :, NZ * y : NZ * y + NZ] = a0[c, FRIM + y, PAD : PAD + CX, 0:NZ]


def shift(values, axis, by):
    count = lax.axis_size(axis)
    return lax.ppermute(values, axis, [(i, i + by) for i in range(count) if 0 <= i + by < count])


def local(initial_state, beam_dir, gate_obs, slot_beam, slot_cell):
    peers, capacity = slot_beam.shape[1:]
    group = LANES // capacity
    beams = beam_dir.shape[1]
    per_row = group * beams
    rows = peers // group
    rim_rows_shape = shape(16, CY * NZ)
    slots, first_rows, last_rows = call(
        prepare_kernel, (shape(peers, 8, capacity), rim_rows_shape, rim_rows_shape), limit=60, ins=5
    )(initial_state, beam_dir, gate_obs, slot_beam, slot_cell)
    after = shift(first_rows, "gx", -1)
    before = shift(last_rows, "gx", 1)
    slots = lax.all_to_all(slots, AXES, split_axis=0, concat_axis=0, tiled=True)
    if group > 1:
        slots = slots.reshape(rows, group, 8, capacity).transpose(0, 2, 1, 3).reshape(rows, 8, LANES)
    piece = shape(STATE_PIECE, LANES)
    first_layers, last_layers = call(state_rim_kernel, (piece, piece), ins=3)(initial_state, before, after)
    above = shift(first_layers, "gy", -1)
    below = shift(last_layers, "gy", 1)
    lines = -(-STEPS * per_row * rows // LANES // 8) * 8
    field = shape(3, YH, XH, LANES)
    mask = pltpu.VMEM((XH, LANES), F32)
    seen, sums, s0, s1, s2 = call(
        functools.partial(forward_kernel, beams, per_row),
        (shape(STEPS, rows, LANES), shape(peers, lines, LANES), field, field, field),
        [pltpu.VMEM(field.shape, F32)] * 4
        + [pltpu.VMEM((2 * FIELDS * NZ, COLUMNS), BF16), mask, pltpu.SemaphoreType.DMA((3,))],
        limit=40,
        ins=6,
        far_out=(2, 3, 4),
    )(initial_state, before, after, below, above, slots)
    sums = lax.all_to_all(sums, AXES, split_axis=0, concat_axis=0, tiled=True)
    rim = shape(len(FORCE_BLOCKS), PACKED, LANES)
    force, first_rows, last_rows = call(
        functools.partial(force_kernel, beams, per_row),
        (shape(FIELDS, CY, CX, LANES), rim, rim),
        [pltpu.VMEM((FIELDS, LANES, COLUMNS), F32), pltpu.VMEM((FIELDS, rows, LANES), F32)],
        limit=40,
        ins=3,
    )(slots, seen, sums)
    after = shift(first_rows, "gx", -1)
    before = shift(last_rows, "gx", 1)
    piece = shape(FORCE_PIECE, LANES)
    first_layers, last_layers = call(force_rim_kernel, (piece, piece), ins=3)(force, before, after)
    above = shift(first_layers, "gy", -1)
    below = shift(last_layers, "gy", 1)
    padded = pltpu.VMEM((3, FH, XH, LANES), F32)
    return call(
        backward_kernel,
        shape(*initial_state.shape),
        [pltpu.VMEM(field.shape, F32)] * 3 + [padded] * 4 + [mask, pltpu.SemaphoreType.DMA((3,))],
        limit=40,
        ins=8,
        far_in=(5, 6, 7),
    )(
        force, before, after, below, above, s0, s1, s2
    )


def solution(mesh):
    in_specs = (
        P(None, "gx", "gy"),
        P(None, ("gx", "gy")),
        P(None, ("gx", "gy"), None, None),
        P(("gx", "gy"), None, None),
        P(("gx", "gy"), None, None),
    )
    out_specs = P(None, "gx", "gy")
    return jax.shard_map(local, mesh=mesh, in_specs=in_specs, out_specs=out_specs, check_vma=False)
```

```python
import functools

import jax
import jax.numpy as jnp
from jax import lax
from jax.experimental import pallas as pl
from jax.experimental.pallas import tpu as pltpu
from jax.sharding import PartitionSpec as P

NZ = 96
GATES = 512
STEPS = 3
LANES = 128
CX = 32
CY = 32
COLUMNS = CX * CY
RIM = 5
PAD = 8
XH = CX + 2 * PAD
YH = CY + 2 * RIM
PACKED = CX * NZ // LANES
FRIM = 3
FH = CY + 2 * FRIM
FIELDS = 3 * STEPS
UNROLL = 4
ROWS = 8
GROUPS = CX // ROWS
GROUP = ROWS * CY
BLOCK = 512
F32 = jnp.float32
BF16 = jnp.bfloat16
AXES = ("gx", "gy")
MIB = 1024 * 1024


def call(kernel, outs, scratch=(), limit=12, far_in=(), ins=0, far_out=(), micros=1):
    def specs(count, far):
        spaces = [pl.ANY if i in far else pltpu.VMEM for i in range(count)]
        return [pl.BlockSpec(memory_space=space) for space in spaces]

    single = not isinstance(outs, tuple)
    out_specs = specs(1 if single else len(outs), far_out)
    return pl.pallas_call(
        kernel,
        out_shape=outs,
        in_specs=specs(ins, far_in),
        out_specs=out_specs[0] if single else tuple(out_specs),
        scratch_shapes=list(scratch),
        compiler_params=pltpu.CompilerParams(vmem_limit_bytes=limit * MIB),
        cost_estimate=pl.CostEstimate(flops=0, bytes_accessed=micros * 3_000_000, transcendentals=0),
    )


def shape(*dims):
    return jax.ShapeDtypeStruct(dims, F32)


def lane_of(rows=8):
    return lax.broadcasted_iota(jnp.int32, (rows, LANES), 1)


def pack(put, block):
    lane = lane_of()
    last = block[24:32]
    for j in range(3):
        tail = pltpu.roll(last, 96 - 32 * j, axis=1)
        put(8 * j, jnp.where(lane < NZ, block[8 * j : 8 * j + 8], tail))


def unpack(rows):
    lane = lane_of()
    last = jnp.zeros((8, LANES), F32)
    parts = []
    for j in range(3):
        piece = rows[8 * j : 8 * j + 8]
        parts.append(jnp.where(lane < NZ, piece, 0.0))
        moved = pltpu.roll(piece, (32 * j - 96) % LANES, axis=1)
        last = jnp.where((lane >= 32 * j) & (lane < 32 * j + 32), moved, last)
    return jnp.concatenate(parts + [last], axis=0)


def column_block(ref, comp, y):
    return ref[comp, :, NZ * y : NZ * y + NZ]


def widen(block):
    return jnp.concatenate([block, jnp.zeros((block.shape[0], LANES - NZ), F32)], axis=1)


def corner_rows(rim):
    rows, out = 0, []
    for comp in range(3):
        for dist in range(1, rim):
            out.append((comp, dist, rows, rim - dist))
            rows += 2 * (rim - dist)
    return out, rows


STATE_CORNERS, STATE_CORNER_ROWS = corner_rows(RIM)
STATE_PIECE = 3 * RIM * PACKED + 64
FORCE_BLOCKS = [(n, c, i) for n in range(STEPS) for c in range(3) for i in range(n + 1)]
FORCE_CORNERS = [
    (n, c, dist, side, k)
    for n in range(STEPS)
    for c in range(3)
    for dist in range(1, n + 1)
    for side in range(2)
    for k in range(1, n + 2 - dist)
]
FORCE_PIECE = len(FORCE_BLOCKS) * PACKED + 24


def prepare_kernel(state, beam_dir, obs, beam, cell, slots, first_rows, last_rows):
    beams = beam_dir.shape[1]
    owned = beam[0]
    used = owned >= 0
    masks = [owned == k for k in range(beams)]

    def spread(values):
        total = jnp.zeros(owned.shape, F32)
        for k in range(beams):
            total = jnp.where(masks[k], values[k], total)
        return total

    slots[:, 0, :] = cell[0].astype(F32)
    slots[:, 1, :] = owned.astype(F32)
    for n in range(STEPS):
        seen = obs[n, 0]
        means = [jnp.sum(jnp.where(m, seen, 0.0), keepdims=True) / GATES for m in masks]
        slots[:, 2 + n, :] = jnp.where(used, seen - spread(means), 0.0)
    for c in range(3):
        slots[:, 5 + c, :] = spread([beam_dir[c : c + 1, k : k + 1] for k in range(beams)])
    for c in range(3):
        first_rows[RIM * c : RIM * c + RIM, :] = state[c, 0:RIM, :]
        last_rows[RIM * c : RIM * c + RIM, :] = state[c, CX - RIM : CX, :]
    first_rows[3 * RIM : 16, :] = jnp.zeros((1, CY * NZ), F32)
    last_rows[3 * RIM : 16, :] = jnp.zeros((1, CY * NZ), F32)


def state_rim_kernel(state, before, after, first_layers, last_layers):
    for out, layer_of in ((first_layers, lambda d: d - 1), (last_layers, lambda d: CY - d)):
        for c in range(3):
            for dist in range(1, RIM + 1):
                base = (c * RIM + dist - 1) * PACKED

                def put(row, rows, base=base, out=out):
                    out[base + row : base + row + 8, :] = rows

                pack(put, widen(column_block(state, c, layer_of(dist))))
        base = 3 * RIM * PACKED
        out[base : base + 64, :] = jnp.zeros((64, LANES), F32)
        for c, dist, row, side in STATE_CORNERS:
            lanes = slice(NZ * layer_of(dist), NZ * layer_of(dist) + NZ)
            out[base + row : base + row + side, 0:NZ] = before[RIM * c + dist : RIM * c + RIM, lanes]
            out[base + row + side : base + row + 2 * side, 0:NZ] = after[RIM * c : RIM * c + side, lanes]


def row_mask(x_place, x_count):
    row = lax.broadcasted_iota(jnp.int32, (XH, LANES), 0)
    lane = lax.broadcasted_iota(jnp.int32, (XH, LANES), 1)
    low = jnp.where(x_place == 0, PAD, 0)
    high = jnp.where(x_place == x_count - 1, PAD + CX, XH)
    return jnp.where((row >= low) & (row < high) & (lane < NZ), 1.0, 0.0).astype(F32)


def layer_mask(y, y_place, y_count):
    outside = ((y < 0) & (y_place == 0)) | ((y >= CY) & (y_place == y_count - 1))
    return jnp.where(outside, 0.0, 1.0).astype(F32)


def next_level(v):
    return pltpu.roll(v, LANES - 1, axis=1)


def last_level(v):
    return pltpu.roll(v, 1, axis=1)


def step_forward(src, dst, low, high, first_row, chunks, mask, places):
    def layer(i, carry):
        y = i + low
        keep = layer_mask(y, places[2], places[3])
        done = []
        for t in range(chunks):
            r = first_row + 8 * t
            here, ahead, behind = pl.ds(r, 8), pl.ds(r + 1, 8), pl.ds(r - 1, 8)
            centre = [src[c, y + RIM, here, :] for c in range(3)]
            scaled = [0.1 * v for v in centre]
            plus = [0.1 - v for v in scaled]
            minus = [0.1 + v for v in scaled]
            inside = mask[here, :] * keep
            for c in range(3):
                v = centre[c]
                total = 0.4 * v + (plus[2] * next_level(v) + minus[2] * last_level(v))
                total = total + (plus[0] * src[c, y + RIM, ahead, :] + minus[0] * src[c, y + RIM, behind, :])
                total = total + (
                    plus[1] * src[c, y + RIM + 1, here, :] + minus[1] * src[c, y + RIM - 1, here, :]
                )
                done.append((c, here, total * inside))
        for c, here, total in done:
            dst[c, y + RIM, here, :] = total
        return carry

    lax.fori_loop(0, high - low, layer, 0, unroll=UNROLL)


def mesh_places():
    return (
        lax.axis_index("gx"),
        lax.axis_size("gx"),
        lax.axis_index("gy"),
        lax.axis_size("gy"),
    )


def slot_columns(slots, row):
    cell = slots[row, 0:1, :]
    x = ((cell + 0.5) * (1.0 / (CY * NZ))).astype(jnp.int32)
    rest = cell.astype(jnp.int32) - x * (CY * NZ)
    y = ((rest.astype(F32) + 0.5) * (1.0 / NZ)).astype(jnp.int32)
    high = x // ROWS
    return high * (GROUP - ROWS) + y * ROWS + x, rest - y * NZ


def column_hits(columns, count=COLUMNS):
    place = lax.broadcasted_iota(jnp.int32, (count, columns.shape[1]), 0)
    return jnp.where(place == columns, 1.0, 0.0).astype(BF16)


def block_places(slots, block):
    rows = [slot_columns(slots, block * (BLOCK // LANES) + r) for r in range(BLOCK // LANES)]
    columns = jnp.concatenate([r[0] for r in rows], axis=1)
    level = jnp.concatenate([r[1] for r in rows], axis=1)
    here = lax.broadcasted_iota(jnp.int32, (NZ, BLOCK), 0) == level
    return columns, here


def block_values(slots, block, which):
    rows = [slots[block * (BLOCK // LANES) + r, which : which + 1, :] for r in range(BLOCK // LANES)]
    return jnp.concatenate(rows, axis=1)


def forward_kernel(
    beams, per_row, state, before, after, below, above, slots, seen, sums, kept0, kept1, kept2, s0, s1, s2, s3, table, mask, sem
):
    places = mesh_places()
    mask[...] = row_mask(places[0], places[1])
    s0[...] = jnp.zeros(s0.shape, F32)
    for c in range(3):
        for y in range(CY):
            lanes = slice(NZ * y, NZ * y + NZ)
            s0[c, RIM + y, PAD : PAD + CX, 0:NZ] = state[c, :, lanes]
            s0[c, RIM + y, PAD - RIM : PAD, 0:NZ] = before[RIM * c : RIM * c + RIM, lanes]
            s0[c, RIM + y, PAD + CX : PAD + CX + RIM, 0:NZ] = after[RIM * c : RIM * c + RIM, lanes]
    for piece, layer_of in ((above, lambda d: RIM + CY - 1 + d), (below, lambda d: RIM - d)):
        for c in range(3):
            for dist in range(1, RIM + 1):
                base = (c * RIM + dist - 1) * PACKED
                s0[c, layer_of(dist), PAD : PAD + CX, :] = unpack(piece[base : base + PACKED, :])
        base = 3 * RIM * PACKED
        for c, dist, row, side in STATE_CORNERS:
            s0[c, layer_of(dist), PAD - side : PAD, :] = piece[base + row : base + row + side, :]
            s0[c, layer_of(dist), PAD + CX : PAD + CX + side, :] = piece[
                base + row + side : base + row + 2 * side, :
            ]
    keeps = [
        pltpu.make_async_copy(field, kept, sem.at[n])
        for n, (field, kept) in enumerate(((s0, kept0), (s1, kept1), (s2, kept2)))
    ]
    keeps[0].start()
    step_forward(s0, s1, -4, CY + 4, 4, 5, mask, places)
    keeps[1].start()
    step_forward(s1, s2, -3, CY + 3, 4, 5, mask, places)
    keeps[2].start()
    step_forward(s2, s3, 0, CY, PAD, 4, mask, places)

    half = FIELDS * NZ
    for n, field in enumerate((s1, s2, s3)):
        for c in range(3):
            base = (3 * n + c) * NZ
            for g in range(GROUPS):
                rows = field[c, RIM : RIM + CY, PAD + ROWS * g : PAD + ROWS * g + ROWS, :]
                turned = rows.reshape(GROUP, LANES).T[0:NZ]
                high = turned.astype(BF16)
                span = slice(GROUP * g, GROUP * g + GROUP)
                table[base : base + NZ, span] = high
                table[half + base : half + base + NZ, span] = (turned - high.astype(F32)).astype(BF16)

    def gather(block, carry):
        columns, here = block_places(slots, block)
        found = jnp.dot(table[...], column_hits(columns), preferred_element_type=F32)
        weights = [block_values(slots, block, 5 + c) for c in range(3)]
        for n in range(STEPS):
            total = jnp.zeros((1, BLOCK), F32)
            for c in range(3):
                base = (3 * n + c) * NZ
                both = found[base : base + NZ] + found[half + base : half + base + NZ]
                value = jnp.sum(jnp.where(here, both, 0.0), axis=0, keepdims=True)
                total = total + weights[c] * value
            for r in range(BLOCK // LANES):
                seen[n, pl.ds(block * (BLOCK // LANES) + r, 1), :] = total[:, LANES * r : LANES * r + LANES]
        return carry

    rows = slots.shape[0]
    lax.fori_loop(0, rows * LANES // BLOCK, gather, 0)

    beam = row_beam(beams, per_row, slots)
    lane = lax.broadcasted_iota(jnp.int32, (rows, LANES), 1)
    partial = jnp.zeros((rows, LANES), F32)
    for n in range(STEPS):
        values = seen[n]
        for k in range(per_row):
            one = jnp.sum(jnp.where(beam == k, values, 0.0), axis=1, keepdims=True)
            partial = jnp.where(lane == n * per_row + k, one, partial)
    turned = jnp.concatenate([partial, jnp.zeros((LANES - rows, LANES), F32)], axis=0).T
    per_line = LANES // rows
    sums[...] = jnp.zeros(sums.shape, F32)
    for line in range(STEPS * per_row // per_line):
        total = turned[line * per_line : line * per_line + 1]
        for k in range(1, per_line):
            one = turned[line * per_line + k : line * per_line + k + 1]
            total = total + pltpu.roll(one, rows * k, axis=1)
        sums[:, line : line + 1, :] = jnp.broadcast_to(total[None], (sums.shape[0], 1, LANES))
    for keep in keeps:
        keep.wait()


def row_beam(beams, per_row, slots):
    group = per_row // beams
    lane = lax.broadcasted_iota(jnp.int32, (slots.shape[0], LANES), 1)
    beam = slots[:, 1, :].astype(jnp.int32)
    for g in range(1, group):
        beam = beam + jnp.where(lane >= g * (LANES // group), beams, 0)
    return beam


def scatter_slots(groups, slots, weight, total, force):
    total[...] = jnp.zeros(total.shape, F32)

    def scatter(block, carry):
        columns, here = block_places(slots, block)
        hits = jnp.concatenate([column_hits(columns - GROUP * g, GROUP) for g in groups], axis=0)
        high_rows, low_rows = [], []
        for f in range(FIELDS):
            value = jnp.concatenate(
                [weight[f, pl.ds(block * (BLOCK // LANES) + r, 1), :] for r in range(BLOCK // LANES)],
                axis=1,
            )
            high = value.astype(BF16).astype(F32)
            high_rows.append(jnp.where(here, high, 0.0).astype(BF16))
            low_rows.append(jnp.where(here, value - high, 0.0).astype(BF16))
        table = jnp.concatenate(high_rows + low_rows, axis=0)
        added = lax.dot_general(table, hits, (((1,), (1,)), ((), ())), preferred_element_type=F32)
        half = FIELDS * NZ
        for f in range(FIELDS):
            total[f, 0:NZ, :] += added[NZ * f : NZ * f + NZ] + added[half + NZ * f : half + NZ * f + NZ]
        return carry

    lax.fori_loop(0, slots.shape[0] * LANES // BLOCK, scatter, 0)
    for f in range(FIELDS):
        for k in range(len(groups)):
            force[f, k] = total[f, :, GROUP * k : GROUP * k + GROUP].T.reshape(CY, ROWS, LANES)


def outer_force_kernel(beams, per_row, slots, seen, sums, force, weight, first_rows, last_rows, total):
    rows = slots.shape[0]
    per_line = LANES // rows
    lines = jnp.sum(sums[...], axis=0) / GATES
    count = STEPS * per_row
    spread = []
    for k in range(count):
        line = lines[k // per_line : k // per_line + 1]
        spread.append(pltpu.roll(line, (-rows * (k % per_line)) % LANES, axis=1))
    spread.append(jnp.zeros((LANES - count, LANES), F32))
    means = jnp.concatenate(spread, axis=0).T[0:rows]
    beam = row_beam(beams, per_row, slots)
    for n in range(STEPS):
        mean = jnp.zeros((rows, LANES), F32)
        for k in range(per_row):
            one = means[:, n * per_row + k : n * per_row + k + 1]
            mean = jnp.where(beam == k, one, mean)
        misfit = seen[n] - mean - slots[:, 2 + n, :]
        for c in range(3):
            weight[3 * n + c] = slots[:, 5 + c, :] * misfit
    scatter_slots((0, GROUPS - 1), slots, weight, total, force)
    for out, k, row_of in ((first_rows, 0, lambda i: i), (last_rows, 1, lambda i: ROWS - 1 - i)):
        for b, (n, c, i) in enumerate(FORCE_BLOCKS):

            def put(row, rows, b=b, out=out):
                out[b, row : row + 8, :] = rows

            pack(put, force[3 * n + c, k, :, row_of(i), :])


def inner_force_kernel(slots, weight, force, total):
    scatter_slots((1, 2), slots, weight, total, force)


def force_rim_kernel(outer, inner, before, after, first_layers, last_layers):
    index = {key: b for b, key in enumerate(FORCE_BLOCKS)}
    for out, layer_of in ((first_layers, lambda d: d - 1), (last_layers, lambda d: CY - d)):
        for b, (n, c, i) in enumerate(FORCE_BLOCKS):

            def put(row, rows, b=b, out=out):
                out[b * PACKED + row : b * PACKED + row + 8, :] = rows

            f, y = 3 * n + c, layer_of(i + 1)
            pack(put, jnp.concatenate([outer[f, 0, y], inner[f, 0, y], inner[f, 1, y], outer[f, 1, y]], axis=0))
        base = len(FORCE_BLOCKS) * PACKED
        for row, (n, c, dist, side, k) in enumerate(FORCE_CORNERS):
            piece = (before, after)[side]
            block = unpack(piece[index[(n, c, k - 1)]])
            y = layer_of(dist)
            out[base + row : base + row + 1, :] = block[y : y + 1]


def backward_kernel(
    outer, inner, before, after, below, above, kept0, kept1, kept2, out, s0, s1, s2, a3, a2, a1, a0, mask, sem
):
    loads = [
        pltpu.make_async_copy(kept, field, sem.at[n])
        for n, (field, kept) in enumerate(((s0, kept0), (s1, kept1), (s2, kept2)))
    ]
    for n in (2, 1, 0):
        loads[n].start()
    places = mesh_places()
    mask[...] = row_mask(places[0], places[1])
    adjoints = (a1, a2, a3)
    for n in range(STEPS):
        adjoints[n][...] = jnp.zeros(adjoints[n].shape, F32)
        for c in range(3):
            for g, (part, k) in enumerate(((outer, 0), (inner, 0), (inner, 1), (outer, 1))):
                row = PAD + ROWS * g
                adjoints[n][c, FRIM : FRIM + CY, row : row + ROWS, :] = part[3 * n + c, k]
    for b, (n, c, i) in enumerate(FORCE_BLOCKS):
        adjoints[n][c, FRIM : FRIM + CY, PAD - 1 - i, :] = unpack(before[b])
        adjoints[n][c, FRIM : FRIM + CY, PAD + CX + i, :] = unpack(after[b])
    for piece, layer_of in ((above, lambda d: FRIM + CY - 1 + d), (below, lambda d: FRIM - d)):
        for b, (n, c, i) in enumerate(FORCE_BLOCKS):
            adjoints[n][c, layer_of(i + 1), PAD : PAD + CX, :] = unpack(piece[b * PACKED : b * PACKED + PACKED, :])
        base = len(FORCE_BLOCKS) * PACKED
        for row, (n, c, dist, side, k) in enumerate(FORCE_CORNERS):
            x = (PAD - k, PAD + CX - 1 + k)[side]
            adjoints[n][c, layer_of(dist), x : x + 1, :] = piece[base + row : base + row + 1, :]

    def pull(field, source, target, low, high, first_row, chunks, add):
        def layer(i, carry):
            y = i + low
            keep = layer_mask(y, places[2], places[3])
            done = []
            for t in range(chunks):
                r = first_row + 8 * t
                here, ahead, behind = pl.ds(r, 8), pl.ds(r + 1, 8), pl.ds(r - 1, 8)
                v = [field[c, y + RIM, here, :] for c in range(3)]
                v_ahead = [field[c, y + RIM, ahead, :] for c in range(3)]
                v_behind = [field[c, y + RIM, behind, :] for c in range(3)]
                v_next = [field[c, y + RIM + 1, here, :] for c in range(3)]
                v_last = [field[c, y + RIM - 1, here, :] for c in range(3)]
                a = [source[c, y + FRIM, here, :] for c in range(3)]
                scaled = [0.1 * f for f in a]
                bends = [None] * 3
                for d, (up, down) in enumerate(((v_ahead, v_behind), (v_next, v_last), (None, None))):
                    for c in range(3):
                        u, w = (up[c], down[c]) if d < 2 else (next_level(v[c]), last_level(v[c]))
                        part = (u - w) * scaled[c]
                        bends[d] = part if bends[d] is None else bends[d] + part
                x_ahead = 0.1 + 0.1 * v_ahead[0]
                x_behind = 0.1 - 0.1 * v_behind[0]
                y_next = 0.1 + 0.1 * v_next[1]
                y_last = 0.1 - 0.1 * v_last[1]
                inside = mask[here, :] * keep
                for c in range(3):
                    total = 0.4 * a[c] - bends[c]
                    total = total + (
                        x_ahead * source[c, y + FRIM, ahead, :] + x_behind * source[c, y + FRIM, behind, :]
                    )
                    total = total + (
                        y_next * source[c, y + FRIM + 1, here, :] + y_last * source[c, y + FRIM - 1, here, :]
                    )
                    product = v[2] * scaled[c]
                    total = total + (next_level(scaled[c] + product) + last_level(scaled[c] - product))
                    if add:
                        total = total + target[c, y + FRIM, here, :]
                    done.append((c, here, total * inside))
            for c, here, total in done:
                target[c, y + FRIM, here, :] = total
            return carry

        lax.fori_loop(0, high - low, layer, 0, unroll=UNROLL)

    loads[2].wait()
    pull(s2, a3, a2, -2, CY + 2, 4, 5, True)
    loads[1].wait()
    pull(s1, a2, a1, -1, CY + 1, 4, 5, True)
    loads[0].wait()
    pull(s0, a1, a0, 0, CY, PAD, 4, False)
    for c in range(3):
        for y in range(CY):
            out[c, :, NZ * y : NZ * y + NZ] = a0[c, FRIM + y, PAD : PAD + CX, 0:NZ]


def shift(values, axis, by):
    count = lax.axis_size(axis)
    return lax.ppermute(values, axis, [(i, i + by) for i in range(count) if 0 <= i + by < count])


def local(initial_state, beam_dir, gate_obs, slot_beam, slot_cell):
    peers, capacity = slot_beam.shape[1:]
    group = LANES // capacity
    beams = beam_dir.shape[1]
    per_row = group * beams
    rows = peers // group
    rim_rows_shape = shape(16, CY * NZ)
    slots, first_rows, last_rows = call(
        prepare_kernel, (shape(peers, 8, capacity), rim_rows_shape, rim_rows_shape), limit=60, ins=5
    )(initial_state, beam_dir, gate_obs, slot_beam, slot_cell)
    after = shift(first_rows, "gx", -1)
    before = shift(last_rows, "gx", 1)
    slots = lax.all_to_all(slots, AXES, split_axis=0, concat_axis=0, tiled=True)
    if group > 1:
        slots = slots.reshape(rows, group, 8, capacity).transpose(0, 2, 1, 3).reshape(rows, 8, LANES)
    piece = shape(STATE_PIECE, LANES)
    first_layers, last_layers = call(state_rim_kernel, (piece, piece), ins=3)(initial_state, before, after)
    above = shift(first_layers, "gy", -1)
    below = shift(last_layers, "gy", 1)
    lines = -(-STEPS * per_row * rows // LANES // 8) * 8
    field = shape(3, YH, XH, LANES)
    mask = pltpu.VMEM((XH, LANES), F32)
    seen, sums, s0, s1, s2 = call(
        functools.partial(forward_kernel, beams, per_row),
        (shape(STEPS, rows, LANES), shape(peers, lines, LANES), field, field, field),
        [pltpu.VMEM(field.shape, F32)] * 4
        + [pltpu.VMEM((2 * FIELDS * NZ, COLUMNS), BF16), mask, pltpu.SemaphoreType.DMA((3,))],
        limit=40,
        ins=6,
        far_out=(2, 3, 4),
    )(initial_state, before, after, below, above, slots)
    sums = lax.all_to_all(sums, AXES, split_axis=0, concat_axis=0, tiled=True)
    rim = shape(len(FORCE_BLOCKS), PACKED, LANES)
    part = shape(FIELDS, 2, CY, ROWS, LANES)
    total = pltpu.VMEM((FIELDS, LANES, 2 * GROUP), F32)
    outer, weight, first_rows, last_rows = call(
        functools.partial(outer_force_kernel, beams, per_row),
        (part, shape(FIELDS, rows, LANES), rim, rim),
        [total],
        limit=40,
        ins=3,
    )(slots, seen, sums)
    after = shift(first_rows, "gx", -1)
    before = shift(last_rows, "gx", 1)
    inner = call(inner_force_kernel, part, [total], limit=40, ins=2, micros=9)(slots, weight)
    piece = shape(FORCE_PIECE, LANES)
    first_layers, last_layers = call(force_rim_kernel, (piece, piece), ins=4)(outer, inner, before, after)
    above = shift(first_layers, "gy", -1)
    below = shift(last_layers, "gy", 1)
    padded = pltpu.VMEM((3, FH, XH, LANES), F32)
    return call(
        backward_kernel,
        shape(*initial_state.shape),
        [pltpu.VMEM(field.shape, F32)] * 3 + [padded] * 4 + [mask, pltpu.SemaphoreType.DMA((3,))],
        limit=40,
        ins=9,
        far_in=(6, 7, 8),
    )(
        outer, inner, before, after, below, above, s0, s1, s2
    )


def solution(mesh):
    in_specs = (
        P(None, "gx", "gy"),
        P(None, ("gx", "gy")),
        P(None, ("gx", "gy"), None, None),
        P(("gx", "gy"), None, None),
        P(("gx", "gy"), None, None),
    )
    out_specs = P(None, "gx", "gy")
    return jax.shard_map(local, mesh=mesh, in_specs=in_specs, out_specs=out_specs, check_vma=False)
```

```python
import functools

import jax
import jax.numpy as jnp
from jax import lax
from jax.experimental import pallas as pl
from jax.experimental.pallas import tpu as pltpu
from jax.sharding import PartitionSpec as P

NZ = 96
GATES = 512
STEPS = 3
LANES = 128
CX = 32
CY = 32
COLUMNS = CX * CY
RIM = 5
PAD = 8
XH = CX + 2 * PAD
YH = CY + 2 * RIM
PACKED = CX * NZ // LANES
FRIM = 3
FH = CY + 2 * FRIM
FIELDS = 3 * STEPS
UNROLL = 4
ROWS = 8
GROUPS = CX // ROWS
GROUP = ROWS * CY
BLOCK = 512
F32 = jnp.float32
BF16 = jnp.bfloat16
AXES = ("gx", "gy")
MIB = 1024 * 1024


def call(kernel, outs, scratch=(), limit=12, far_in=(), ins=0, far_out=(), micros=1):
    def specs(count, far):
        spaces = [pl.ANY if i in far else pltpu.VMEM for i in range(count)]
        return [pl.BlockSpec(memory_space=space) for space in spaces]

    single = not isinstance(outs, tuple)
    out_specs = specs(1 if single else len(outs), far_out)
    return pl.pallas_call(
        kernel,
        out_shape=outs,
        in_specs=specs(ins, far_in),
        out_specs=out_specs[0] if single else tuple(out_specs),
        scratch_shapes=list(scratch),
        compiler_params=pltpu.CompilerParams(vmem_limit_bytes=limit * MIB),
        cost_estimate=pl.CostEstimate(flops=0, bytes_accessed=micros * 3_000_000, transcendentals=0),
    )


def shape(*dims):
    return jax.ShapeDtypeStruct(dims, F32)


def lane_of(rows=8):
    return lax.broadcasted_iota(jnp.int32, (rows, LANES), 1)


def pack(put, block):
    lane = lane_of()
    last = block[24:32]
    for j in range(3):
        tail = pltpu.roll(last, 96 - 32 * j, axis=1)
        put(8 * j, jnp.where(lane < NZ, block[8 * j : 8 * j + 8], tail))


def unpack(rows):
    lane = lane_of()
    last = jnp.zeros((8, LANES), F32)
    parts = []
    for j in range(3):
        piece = rows[8 * j : 8 * j + 8]
        parts.append(jnp.where(lane < NZ, piece, 0.0))
        moved = pltpu.roll(piece, (32 * j - 96) % LANES, axis=1)
        last = jnp.where((lane >= 32 * j) & (lane < 32 * j + 32), moved, last)
    return jnp.concatenate(parts + [last], axis=0)


def is_odd(axis):
    return lax.axis_index(axis) % 2 == 1


def to_partners(axis, first, last, near, far):
    odd = is_odd(axis)
    near[...] = jnp.where(odd, first[...], last[...])
    far[...] = jnp.where(odd, last[...], first[...])


def from_partners(axis, near, far, behind, ahead):
    odd = is_odd(axis)
    behind[...] = jnp.where(odd, near[...], far[...])
    ahead[...] = jnp.where(odd, far[...], near[...])


def corner_rows(rim):
    rows, out = 0, []
    for comp in range(3):
        for dist in range(1, rim):
            out.append((comp, dist, rows, rim - dist))
            rows += 2 * (rim - dist)
    return out, rows


STATE_CORNERS, STATE_CORNER_ROWS = corner_rows(RIM)
STATE_PIECE = 3 * RIM * PACKED + 64
FORCE_BLOCKS = [(n, c, i) for n in range(STEPS) for c in range(3) for i in range(n + 1)]
FORCE_CORNERS = [
    (n, c, dist, side, k)
    for n in range(STEPS)
    for c in range(3)
    for dist in range(1, n + 1)
    for side in range(2)
    for k in range(1, n + 2 - dist)
]
FORCE_PIECE = len(FORCE_BLOCKS) * PACKED + 24


def prepare_kernel(state, beam_dir, obs, beam, cell, slots, near, far, first_rows, last_rows):
    for c in range(3):
        first_rows[RIM * c : RIM * c + RIM, :] = state[c, 0:RIM, :]
        last_rows[RIM * c : RIM * c + RIM, :] = state[c, CX - RIM : CX, :]
    first_rows[3 * RIM : 16, :] = jnp.zeros((1, CY * NZ), F32)
    last_rows[3 * RIM : 16, :] = jnp.zeros((1, CY * NZ), F32)
    to_partners("gx", first_rows, last_rows, near, far)
    beams = beam_dir.shape[1]
    owned = beam[0]
    used = owned >= 0
    masks = [owned == k for k in range(beams)]

    def spread(values):
        total = jnp.zeros(owned.shape, F32)
        for k in range(beams):
            total = jnp.where(masks[k], values[k], total)
        return total

    slots[:, 0, :] = cell[0].astype(F32)
    slots[:, 1, :] = owned.astype(F32)
    for n in range(STEPS):
        seen = obs[n, 0]
        means = [jnp.sum(jnp.where(m, seen, 0.0), keepdims=True) / GATES for m in masks]
        slots[:, 2 + n, :] = jnp.where(used, seen - spread(means), 0.0)
    for c in range(3):
        slots[:, 5 + c, :] = spread([beam_dir[c : c + 1, k : k + 1] for k in range(beams)])


def layout_kernel(state, wide, first_layers, last_layers):
    wide[...] = jnp.zeros(wide.shape, F32)
    for c in range(3):
        for y in range(CY):
            wide[c, RIM + y, PAD : PAD + CX, 0:NZ] = state[c, :, NZ * y : NZ * y + NZ]
    for out, layer_of in ((first_layers, lambda d: d - 1), (last_layers, lambda d: CY - d)):
        for c in range(3):
            for dist in range(1, RIM + 1):
                base = (c * RIM + dist - 1) * PACKED

                def put(row, rows, base=base, out=out):
                    out[base + row : base + row + 8, :] = rows

                pack(put, wide[c, RIM + layer_of(dist), PAD : PAD + CX, :])


def state_corner_kernel(bulk_first, bulk_last, x_near, x_far, near, far, first, last, before, after):
    from_partners("gx", x_near, x_far, before, after)
    base = 3 * RIM * PACKED
    for bulk, out, layer_of in (
        (bulk_first, first, lambda d: d - 1),
        (bulk_last, last, lambda d: CY - d),
    ):
        out[0:base, :] = bulk[...]
        out[base : base + 64, :] = jnp.zeros((64, LANES), F32)
        for c, dist, row, side in STATE_CORNERS:
            lanes = slice(NZ * layer_of(dist), NZ * layer_of(dist) + NZ)
            out[base + row : base + row + side, 0:NZ] = before[RIM * c + dist : RIM * c + RIM, lanes]
            out[base + row + side : base + row + 2 * side, 0:NZ] = after[RIM * c : RIM * c + side, lanes]
    to_partners("gy", first, last, near, far)


def row_mask(x_place, x_count):
    row = lax.broadcasted_iota(jnp.int32, (XH, LANES), 0)
    lane = lax.broadcasted_iota(jnp.int32, (XH, LANES), 1)
    low = jnp.where(x_place == 0, PAD, 0)
    high = jnp.where(x_place == x_count - 1, PAD + CX, XH)
    return jnp.where((row >= low) & (row < high) & (lane < NZ), 1.0, 0.0).astype(F32)


def layer_mask(y, y_place, y_count):
    outside = ((y < 0) & (y_place == 0)) | ((y >= CY) & (y_place == y_count - 1))
    return jnp.where(outside, 0.0, 1.0).astype(F32)


def next_level(v):
    return pltpu.roll(v, LANES - 1, axis=1)


def last_level(v):
    return pltpu.roll(v, 1, axis=1)


def step_forward(src, dst, low, high, first_row, chunks, mask, places):
    def layer(i, carry):
        y = i + low
        keep = layer_mask(y, places[2], places[3])
        done = []
        for t in range(chunks):
            r = first_row + 8 * t
            here, ahead, behind = pl.ds(r, 8), pl.ds(r + 1, 8), pl.ds(r - 1, 8)
            centre = [src[c, y + RIM, here, :] for c in range(3)]
            scaled = [0.1 * v for v in centre]
            plus = [0.1 - v for v in scaled]
            minus = [0.1 + v for v in scaled]
            inside = mask[here, :] * keep
            for c in range(3):
                v = centre[c]
                total = 0.4 * v + (plus[2] * next_level(v) + minus[2] * last_level(v))
                total = total + (plus[0] * src[c, y + RIM, ahead, :] + minus[0] * src[c, y + RIM, behind, :])
                total = total + (
                    plus[1] * src[c, y + RIM + 1, here, :] + minus[1] * src[c, y + RIM - 1, here, :]
                )
                done.append((c, here, total * inside))
        for c, here, total in done:
            dst[c, y + RIM, here, :] = total
        return carry

    lax.fori_loop(0, high - low, layer, 0, unroll=UNROLL)


def mesh_places():
    return (
        lax.axis_index("gx"),
        lax.axis_size("gx"),
        lax.axis_index("gy"),
        lax.axis_size("gy"),
    )


def slot_columns(slots, row):
    cell = slots[row, 0:1, :]
    x = ((cell + 0.5) * (1.0 / (CY * NZ))).astype(jnp.int32)
    rest = cell.astype(jnp.int32) - x * (CY * NZ)
    y = ((rest.astype(F32) + 0.5) * (1.0 / NZ)).astype(jnp.int32)
    high = x // ROWS
    return high * (GROUP - ROWS) + y * ROWS + x, rest - y * NZ


def column_hits(columns, count=COLUMNS):
    place = lax.broadcasted_iota(jnp.int32, (count, columns.shape[1]), 0)
    return jnp.where(place == columns, 1.0, 0.0).astype(BF16)


def block_places(slots, block):
    rows = [slot_columns(slots, block * (BLOCK // LANES) + r) for r in range(BLOCK // LANES)]
    columns = jnp.concatenate([r[0] for r in rows], axis=1)
    level = jnp.concatenate([r[1] for r in rows], axis=1)
    here = lax.broadcasted_iota(jnp.int32, (NZ, BLOCK), 0) == level
    return columns, here


def block_values(slots, block, which):
    rows = [slots[block * (BLOCK // LANES) + r, which : which + 1, :] for r in range(BLOCK // LANES)]
    return jnp.concatenate(rows, axis=1)


def forward_kernel(
    beams,
    per_row,
    wide,
    x_near,
    x_far,
    y_near,
    y_far,
    slots,
    seen,
    sums,
    s0,
    s1,
    s2,
    s3,
    table,
    mask,
    below,
    above,
    before,
    after,
):
    places = mesh_places()
    from_partners("gx", x_near, x_far, before, after)
    mask[...] = row_mask(places[0], places[1])
    from_partners("gy", y_near, y_far, below, above)
    s0[...] = wide[...]
    for c in range(3):
        for y in range(CY):
            lanes = slice(NZ * y, NZ * y + NZ)
            s0[c, RIM + y, PAD - RIM : PAD, 0:NZ] = before[RIM * c : RIM * c + RIM, lanes]
            s0[c, RIM + y, PAD + CX : PAD + CX + RIM, 0:NZ] = after[RIM * c : RIM * c + RIM, lanes]
    for piece, layer_of in ((above, lambda d: RIM + CY - 1 + d), (below, lambda d: RIM - d)):
        for c in range(3):
            for dist in range(1, RIM + 1):
                base = (c * RIM + dist - 1) * PACKED
                s0[c, layer_of(dist), PAD : PAD + CX, :] = unpack(piece[base : base + PACKED, :])
        base = 3 * RIM * PACKED
        for c, dist, row, side in STATE_CORNERS:
            s0[c, layer_of(dist), PAD - side : PAD, :] = piece[base + row : base + row + side, :]
            s0[c, layer_of(dist), PAD + CX : PAD + CX + side, :] = piece[
                base + row + side : base + row + 2 * side, :
            ]
    step_forward(s0, s1, -4, CY + 4, 4, 5, mask, places)
    step_forward(s1, s2, -3, CY + 3, 4, 5, mask, places)
    step_forward(s2, s3, 0, CY, PAD, 4, mask, places)

    half = FIELDS * NZ
    for n, field in enumerate((s1, s2, s3)):
        for c in range(3):
            base = (3 * n + c) * NZ
            for g in range(GROUPS):
                rows = field[c, RIM : RIM + CY, PAD + ROWS * g : PAD + ROWS * g + ROWS, :]
                turned = rows.reshape(GROUP, LANES).T[0:NZ]
                high = turned.astype(BF16)
                span = slice(GROUP * g, GROUP * g + GROUP)
                table[base : base + NZ, span] = high
                table[half + base : half + base + NZ, span] = (turned - high.astype(F32)).astype(BF16)

    def gather(block, carry):
        columns, here = block_places(slots, block)
        found = jnp.dot(table[...], column_hits(columns), preferred_element_type=F32)
        weights = [block_values(slots, block, 5 + c) for c in range(3)]
        for n in range(STEPS):
            total = jnp.zeros((1, BLOCK), F32)
            for c in range(3):
                base = (3 * n + c) * NZ
                both = found[base : base + NZ] + found[half + base : half + base + NZ]
                value = jnp.sum(jnp.where(here, both, 0.0), axis=0, keepdims=True)
                total = total + weights[c] * value
            for r in range(BLOCK // LANES):
                seen[n, pl.ds(block * (BLOCK // LANES) + r, 1), :] = total[:, LANES * r : LANES * r + LANES]
        return carry

    rows = slots.shape[0]
    lax.fori_loop(0, rows * LANES // BLOCK, gather, 0)

    beam = row_beam(beams, per_row, slots)
    lane = lax.broadcasted_iota(jnp.int32, (rows, LANES), 1)
    partial = jnp.zeros((rows, LANES), F32)
    for n in range(STEPS):
        values = seen[n]
        for k in range(per_row):
            one = jnp.sum(jnp.where(beam == k, values, 0.0), axis=1, keepdims=True)
            partial = jnp.where(lane == n * per_row + k, one, partial)
    turned = jnp.concatenate([partial, jnp.zeros((LANES - rows, LANES), F32)], axis=0).T
    per_line = LANES // rows
    sums[...] = jnp.zeros(sums.shape, F32)
    for line in range(STEPS * per_row // per_line):
        total = turned[line * per_line : line * per_line + 1]
        for k in range(1, per_line):
            one = turned[line * per_line + k : line * per_line + k + 1]
            total = total + pltpu.roll(one, rows * k, axis=1)
        sums[:, line : line + 1, :] = jnp.broadcast_to(total[None], (sums.shape[0], 1, LANES))


def row_beam(beams, per_row, slots):
    group = per_row // beams
    lane = lax.broadcasted_iota(jnp.int32, (slots.shape[0], LANES), 1)
    beam = slots[:, 1, :].astype(jnp.int32)
    for g in range(1, group):
        beam = beam + jnp.where(lane >= g * (LANES // group), beams, 0)
    return beam


def scatter_slots(groups, slots, weight, total, force):
    total[...] = jnp.zeros(total.shape, F32)

    def scatter(block, carry):
        columns, here = block_places(slots, block)
        hits = jnp.concatenate([column_hits(columns - GROUP * g, GROUP) for g in groups], axis=0)
        high_rows, low_rows = [], []
        for f in range(FIELDS):
            value = jnp.concatenate(
                [weight[f, pl.ds(block * (BLOCK // LANES) + r, 1), :] for r in range(BLOCK // LANES)],
                axis=1,
            )
            high = value.astype(BF16).astype(F32)
            high_rows.append(jnp.where(here, high, 0.0).astype(BF16))
            low_rows.append(jnp.where(here, value - high, 0.0).astype(BF16))
        table = jnp.concatenate(high_rows + low_rows, axis=0)
        added = lax.dot_general(table, hits, (((1,), (1,)), ((), ())), preferred_element_type=F32)
        half = FIELDS * NZ
        for f in range(FIELDS):
            total[f, 0:NZ, :] += added[NZ * f : NZ * f + NZ] + added[half + NZ * f : half + NZ * f + NZ]
        return carry

    lax.fori_loop(0, slots.shape[0] * LANES // BLOCK, scatter, 0)
    for f in range(FIELDS):
        for k in range(len(groups)):
            force[f, k] = total[f, :, GROUP * k : GROUP * k + GROUP].T.reshape(CY, ROWS, LANES)


def outer_force_kernel(
    beams, per_row, slots, seen, sums, force, weight, near, far, first_rows, last_rows, total
):
    rows = slots.shape[0]
    per_line = LANES // rows
    lines = jnp.sum(sums[...], axis=0) / GATES
    count = STEPS * per_row
    spread = []
    for k in range(count):
        line = lines[k // per_line : k // per_line + 1]
        spread.append(pltpu.roll(line, (-rows * (k % per_line)) % LANES, axis=1))
    spread.append(jnp.zeros((LANES - count, LANES), F32))
    means = jnp.concatenate(spread, axis=0).T[0:rows]
    beam = row_beam(beams, per_row, slots)
    for n in range(STEPS):
        mean = jnp.zeros((rows, LANES), F32)
        for k in range(per_row):
            one = means[:, n * per_row + k : n * per_row + k + 1]
            mean = jnp.where(beam == k, one, mean)
        misfit = seen[n] - mean - slots[:, 2 + n, :]
        for c in range(3):
            weight[3 * n + c] = slots[:, 5 + c, :] * misfit
    scatter_slots((0, GROUPS - 1), slots, weight, total, force)
    for out, k, row_of in ((first_rows, 0, lambda i: i), (last_rows, 1, lambda i: ROWS - 1 - i)):
        for b, (n, c, i) in enumerate(FORCE_BLOCKS):

            def put(row, rows, b=b, out=out):
                out[b, row : row + 8, :] = rows

            pack(put, force[3 * n + c, k, :, row_of(i), :])
    to_partners("gx", first_rows, last_rows, near, far)


def inner_force_kernel(slots, weight, force, total):
    scatter_slots((1, 2), slots, weight, total, force)


def force_rim_kernel(outer, inner, x_near, x_far, near, far, first_layers, last_layers, before, after):
    from_partners("gx", x_near, x_far, before, after)
    index = {key: b for b, key in enumerate(FORCE_BLOCKS)}
    for out, layer_of in ((first_layers, lambda d: d - 1), (last_layers, lambda d: CY - d)):
        for b, (n, c, i) in enumerate(FORCE_BLOCKS):

            def put(row, rows, b=b, out=out):
                out[b * PACKED + row : b * PACKED + row + 8, :] = rows

            f, y = 3 * n + c, layer_of(i + 1)
            pack(put, jnp.concatenate([outer[f, 0, y], inner[f, 0, y], inner[f, 1, y], outer[f, 1, y]], axis=0))
        base = len(FORCE_BLOCKS) * PACKED
        for row, (n, c, dist, side, k) in enumerate(FORCE_CORNERS):
            piece = (before, after)[side]
            block = unpack(piece[index[(n, c, k - 1)]])
            y = layer_of(dist)
            out[base + row : base + row + 1, :] = block[y : y + 1]
    to_partners("gy", first_layers, last_layers, near, far)


def backward_kernel(
    outer,
    inner,
    x_near,
    x_far,
    y_near,
    y_far,
    s0,
    s1,
    s2,
    out,
    a3,
    a2,
    a1,
    a0,
    mask,
    below,
    above,
    before,
    after,
):
    from_partners("gx", x_near, x_far, before, after)
    from_partners("gy", y_near, y_far, below, above)
    places = mesh_places()
    mask[...] = row_mask(places[0], places[1])
    adjoints = (a1, a2, a3)
    for n in range(STEPS):
        adjoints[n][...] = jnp.zeros(adjoints[n].shape, F32)
        for c in range(3):
            for g, (part, k) in enumerate(((outer, 0), (inner, 0), (inner, 1), (outer, 1))):
                row = PAD + ROWS * g
                adjoints[n][c, FRIM : FRIM + CY, row : row + ROWS, :] = part[3 * n + c, k]
    for b, (n, c, i) in enumerate(FORCE_BLOCKS):
        adjoints[n][c, FRIM : FRIM + CY, PAD - 1 - i, :] = unpack(before[b])
        adjoints[n][c, FRIM : FRIM + CY, PAD + CX + i, :] = unpack(after[b])
    for piece, layer_of in ((above, lambda d: FRIM + CY - 1 + d), (below, lambda d: FRIM - d)):
        for b, (n, c, i) in enumerate(FORCE_BLOCKS):
            adjoints[n][c, layer_of(i + 1), PAD : PAD + CX, :] = unpack(piece[b * PACKED : b * PACKED + PACKED, :])
        base = len(FORCE_BLOCKS) * PACKED
        for row, (n, c, dist, side, k) in enumerate(FORCE_CORNERS):
            x = (PAD - k, PAD + CX - 1 + k)[side]
            adjoints[n][c, layer_of(dist), x : x + 1, :] = piece[base + row : base + row + 1, :]

    def pull(field, source, target, low, high, first_row, chunks, add):
        def layer(i, carry):
            y = i + low
            keep = layer_mask(y, places[2], places[3])
            done = []
            for t in range(chunks):
                r = first_row + 8 * t
                here, ahead, behind = pl.ds(r, 8), pl.ds(r + 1, 8), pl.ds(r - 1, 8)
                v = [field[c, y + RIM, here, :] for c in range(3)]
                v_ahead = [field[c, y + RIM, ahead, :] for c in range(3)]
                v_behind = [field[c, y + RIM, behind, :] for c in range(3)]
                v_next = [field[c, y + RIM + 1, here, :] for c in range(3)]
                v_last = [field[c, y + RIM - 1, here, :] for c in range(3)]
                a = [source[c, y + FRIM, here, :] for c in range(3)]
                scaled = [0.1 * f for f in a]
                bends = [None] * 3
                for d, (up, down) in enumerate(((v_ahead, v_behind), (v_next, v_last), (None, None))):
                    for c in range(3):
                        u, w = (up[c], down[c]) if d < 2 else (next_level(v[c]), last_level(v[c]))
                        part = (u - w) * scaled[c]
                        bends[d] = part if bends[d] is None else bends[d] + part
                x_ahead = 0.1 + 0.1 * v_ahead[0]
                x_behind = 0.1 - 0.1 * v_behind[0]
                y_next = 0.1 + 0.1 * v_next[1]
                y_last = 0.1 - 0.1 * v_last[1]
                inside = mask[here, :] * keep
                for c in range(3):
                    total = 0.4 * a[c] - bends[c]
                    total = total + (
                        x_ahead * source[c, y + FRIM, ahead, :] + x_behind * source[c, y + FRIM, behind, :]
                    )
                    total = total + (
                        y_next * source[c, y + FRIM + 1, here, :] + y_last * source[c, y + FRIM - 1, here, :]
                    )
                    product = v[2] * scaled[c]
                    total = total + (next_level(scaled[c] + product) + last_level(scaled[c] - product))
                    if add:
                        total = total + target[c, y + FRIM, here, :]
                    done.append((c, here, total * inside))
            for c, here, total in done:
                target[c, y + FRIM, here, :] = total
            return carry

        lax.fori_loop(0, high - low, layer, 0, unroll=UNROLL)

    pull(s2, a3, a2, -2, CY + 2, 4, 5, True)
    pull(s1, a2, a1, -1, CY + 1, 4, 5, True)
    pull(s0, a1, a0, 0, CY, PAD, 4, False)
    for c in range(3):
        for y in range(CY):
            out[c, :, NZ * y : NZ * y + NZ] = a0[c, FRIM + y, PAD : PAD + CX, 0:NZ]


def swap(near, far, axis):
    def pairs(start):
        lows = range(start, lax.axis_size(axis) - 1, 2)
        return [(i, i + 1) for i in lows] + [(i + 1, i) for i in lows]

    return lax.ppermute(near, axis, pairs(0)), lax.ppermute(far, axis, pairs(1))


def local(initial_state, beam_dir, gate_obs, slot_beam, slot_cell):
    peers, capacity = slot_beam.shape[1:]
    group = LANES // capacity
    beams = beam_dir.shape[1]
    per_row = group * beams
    rows = peers // group
    x_rim = (16, CY * NZ)
    slots, near, far = call(
        prepare_kernel,
        (shape(peers, 8, capacity), shape(*x_rim), shape(*x_rim)),
        [pltpu.VMEM(x_rim, F32)] * 2,
        limit=60,
        ins=5,
    )(initial_state, beam_dir, gate_obs, slot_beam, slot_cell)
    x_near, x_far = swap(near, far, "gx")
    slots = lax.all_to_all(slots, AXES, split_axis=0, concat_axis=0, tiled=True)
    if group > 1:
        slots = slots.reshape(rows, group, 8, capacity).transpose(0, 2, 1, 3).reshape(rows, 8, LANES)
    field = shape(3, YH, XH, LANES)
    bulk = shape(3 * RIM * PACKED, LANES)
    wide, bulk_first, bulk_last = call(layout_kernel, (field, bulk, bulk), ins=1, micros=2)(initial_state)
    y_rim = (STATE_PIECE, LANES)
    near, far = call(
        state_corner_kernel,
        (shape(*y_rim), shape(*y_rim)),
        [pltpu.VMEM(y_rim, F32)] * 2 + [pltpu.VMEM(x_rim, F32)] * 2,
        ins=4,
    )(bulk_first, bulk_last, x_near, x_far)
    y_near, y_far = swap(near, far, "gy")
    lines = -(-STEPS * per_row * rows // LANES // 8) * 8
    mask = pltpu.VMEM((XH, LANES), F32)
    seen, sums, s0, s1, s2 = call(
        functools.partial(forward_kernel, beams, per_row),
        (shape(STEPS, rows, LANES), shape(peers, lines, LANES), field, field, field),
        [pltpu.VMEM(field.shape, F32), pltpu.VMEM((2 * FIELDS * NZ, COLUMNS), BF16), mask]
        + [pltpu.VMEM(y_rim, F32)] * 2
        + [pltpu.VMEM(x_rim, F32)] * 2,
        limit=32,
        ins=6,
    )(wide, x_near, x_far, y_near, y_far, slots)
    sums = lax.all_to_all(sums, AXES, split_axis=0, concat_axis=0, tiled=True)
    x_rim = (len(FORCE_BLOCKS), PACKED, LANES)
    part = shape(FIELDS, 2, CY, ROWS, LANES)
    total = pltpu.VMEM((FIELDS, LANES, 2 * GROUP), F32)
    outer, weight, near, far = call(
        functools.partial(outer_force_kernel, beams, per_row),
        (part, shape(FIELDS, rows, LANES), shape(*x_rim), shape(*x_rim)),
        [pltpu.VMEM(x_rim, F32)] * 2 + [total],
        limit=24,
        ins=3,
    )(slots, seen, sums)
    x_near, x_far = swap(near, far, "gx")
    inner = call(inner_force_kernel, part, [total], limit=24, ins=2, micros=9)(slots, weight)
    y_rim = (FORCE_PIECE, LANES)
    near, far = call(
        force_rim_kernel,
        (shape(*y_rim), shape(*y_rim)),
        [pltpu.VMEM(y_rim, F32)] * 2 + [pltpu.VMEM(x_rim, F32)] * 2,
        ins=4,
    )(outer, inner, x_near, x_far)
    y_near, y_far = swap(near, far, "gy")
    return call(
        backward_kernel,
        shape(*initial_state.shape),
        [pltpu.VMEM((3, FH, XH, LANES), F32)] * 4
        + [mask]
        + [pltpu.VMEM(y_rim, F32)] * 2
        + [pltpu.VMEM(x_rim, F32)] * 2,
        limit=32,
        ins=9,
    )(outer, inner, x_near, x_far, y_near, y_far, s0, s1, s2)


def solution(mesh):
    in_specs = (
        P(None, "gx", "gy"),
        P(None, ("gx", "gy")),
        P(None, ("gx", "gy"), None, None),
        P(("gx", "gy"), None, None),
        P(("gx", "gy"), None, None),
    )
    out_specs = P(None, "gx", "gy")
    return jax.shard_map(local, mesh=mesh, in_specs=in_specs, out_specs=out_specs, check_vma=False)
```

```python
import functools

import jax
import jax.numpy as jnp
from jax import lax
from jax.experimental import pallas as pl
from jax.experimental.pallas import tpu as pltpu
from jax.sharding import PartitionSpec as P

NZ = 96
GATES = 512
STEPS = 3
LANES = 128
CX = 32
CY = 32
COLUMNS = CX * CY
RIM = 5
PAD = 8
XH = CX + 2 * PAD
YH = CY + 2 * RIM
PACKED = CX * NZ // LANES
FRIM = 3
FH = CY + 2 * FRIM
FIELDS = 3 * STEPS
UNROLL = 4
ROWS = 8
GROUPS = CX // ROWS
GROUP = ROWS * CY
BLOCK = 256
BLOCK_ROWS = BLOCK // LANES
TOGETHER = 4
WORK = 128
F32 = jnp.float32
BF16 = jnp.bfloat16
AXES = ("gx", "gy")
MIB = 1024 * 1024


def call(kernel, outs, scratch=(), limit=12, ins=0, scalar_in=(), scalar_out=(), micros=1):
    def specs(count, scalar):
        spaces = [pltpu.SMEM if i in scalar else pltpu.VMEM for i in range(count)]
        return [pl.BlockSpec(memory_space=space) for space in spaces]

    single = not isinstance(outs, tuple)
    out_specs = specs(1 if single else len(outs), scalar_out)
    return pl.pallas_call(
        kernel,
        out_shape=outs,
        in_specs=specs(ins, scalar_in),
        out_specs=out_specs[0] if single else tuple(out_specs),
        scratch_shapes=list(scratch),
        compiler_params=pltpu.CompilerParams(vmem_limit_bytes=limit * MIB),
        cost_estimate=pl.CostEstimate(flops=0, bytes_accessed=micros * 3_000_000, transcendentals=0),
    )


def shape(*dims):
    return jax.ShapeDtypeStruct(dims, F32)


def lane_of(rows=8):
    return lax.broadcasted_iota(jnp.int32, (rows, LANES), 1)


def pack(put, block):
    lane = lane_of()
    last = block[24:32]
    for j in range(3):
        tail = pltpu.roll(last, 96 - 32 * j, axis=1)
        put(8 * j, jnp.where(lane < NZ, block[8 * j : 8 * j + 8], tail))


def unpack(rows):
    lane = lane_of()
    last = jnp.zeros((8, LANES), F32)
    parts = []
    for j in range(3):
        piece = rows[8 * j : 8 * j + 8]
        parts.append(jnp.where(lane < NZ, piece, 0.0))
        moved = pltpu.roll(piece, (32 * j - 96) % LANES, axis=1)
        last = jnp.where((lane >= 32 * j) & (lane < 32 * j + 32), moved, last)
    return jnp.concatenate(parts + [last], axis=0)


def is_odd(axis):
    return lax.axis_index(axis) % 2 == 1


def to_partners(axis, first, last, near, far):
    odd = is_odd(axis)
    near[...] = jnp.where(odd, first[...], last[...])
    far[...] = jnp.where(odd, last[...], first[...])


def from_partners(axis, near, far, behind, ahead):
    odd = is_odd(axis)
    behind[...] = jnp.where(odd, near[...], far[...])
    ahead[...] = jnp.where(odd, far[...], near[...])


def corner_rows(rim):
    rows, out = 0, []
    for comp in range(3):
        for dist in range(1, rim):
            out.append((comp, dist, rows, rim - dist))
            rows += 2 * (rim - dist)
    return out, rows


STATE_CORNERS, STATE_CORNER_ROWS = corner_rows(RIM)
STATE_PIECE = 3 * RIM * PACKED + 64
FORCE_BLOCKS = [(n, c, i) for n in range(STEPS) for c in range(3) for i in range(n + 1)]
FORCE_CORNERS = [
    (n, c, dist, side, k)
    for n in range(STEPS)
    for c in range(3)
    for dist in range(1, n + 1)
    for side in range(2)
    for k in range(1, n + 2 - dist)
]
FORCE_PIECE = len(FORCE_BLOCKS) * PACKED + 24


def state_rows_kernel(state, near, far, first_rows, last_rows):
    for c in range(3):
        first_rows[RIM * c : RIM * c + RIM, :] = state[c, 0:RIM, :]
        last_rows[RIM * c : RIM * c + RIM, :] = state[c, CX - RIM : CX, :]
    first_rows[3 * RIM : 16, :] = jnp.zeros((1, CY * NZ), F32)
    last_rows[3 * RIM : 16, :] = jnp.zeros((1, CY * NZ), F32)
    to_partners("gx", first_rows, last_rows, near, far)


def arrange_kernel(beam_dir, obs, beam, cell, slots, values, places):
    beams = beam_dir.shape[1]
    owned = beam[0]
    lists, capacity = owned.shape
    used = owned >= 0
    masks = [owned == k for k in range(beams)]

    def spread(parts):
        total = jnp.zeros(owned.shape, F32)
        for k in range(beams):
            total = jnp.where(masks[k], parts[k], total)
        return total

    cells = cell[0].astype(F32)
    values[:, 0, :] = cells + 1.0
    values[:, 1, :] = owned.astype(F32)
    for n in range(STEPS):
        seen = obs[n, 0]
        means = [jnp.sum(jnp.where(m, seen, 0.0), keepdims=True) / GATES for m in masks]
        values[:, 2 + n, :] = jnp.where(used, seen - spread(means), 0.0)
    for c in range(3):
        values[:, 5 + c, :] = spread([beam_dir[c : c + 1, k : k + 1] for k in range(beams)])

    group = ((cells + 0.5) * (1.0 / (GROUP * NZ))).astype(jnp.int32)
    row = lax.broadcasted_iota(jnp.int32, (capacity, capacity), 0)
    column = lax.broadcasted_iota(jnp.int32, (capacity, capacity), 1)
    ahead = jnp.where(row <= column, 1.0, 0.0).astype(BF16)
    ones = [jnp.where(used & (group == g), 1.0, 0.0) for g in range(GROUPS)]
    counts = [jnp.sum(o, axis=1, keepdims=True) for o in ones]
    place = jnp.full(owned.shape, -1.0, F32)
    end = jnp.zeros((lists, 1), F32)
    left = counts[0] + counts[1] + counts[2] + counts[3]
    for g in range(GROUPS):
        start = jnp.minimum(jnp.maximum(float(capacity // GROUPS * g), end), capacity - left)
        upto = jnp.dot(ones[g].astype(BF16), ahead, preferred_element_type=F32)
        place = jnp.where(ones[g] > 0.5, start + upto - 1.0, place)
        end = start + counts[g]
        left = left - counts[g]
    places[...] = place.astype(jnp.int32)

    def move(i, carry):
        full = values[i]
        high = full.astype(BF16).astype(F32)
        mid = (full - high).astype(BF16).astype(F32)
        low = full - high - mid
        three = jnp.concatenate([high, mid, low], axis=0).astype(BF16)
        hits = jnp.where(row == places[pl.ds(i, 1), :], 1.0, 0.0).astype(BF16)
        moved = lax.dot_general(three, hits, (((1,), (1,)), ((), ())), preferred_element_type=F32)
        slots[i] = moved[0:8] + moved[8:16] + moved[16:24]
        return carry

    lax.fori_loop(0, lists, move, 0, unroll=8)


def regroup_kernel(received, slots, every_work, outer_work, inner_work, turned):
    owners, _, capacity = received.shape
    apart = LANES // owners
    rows = capacity // apart
    for j in range(8):
        lists = received[:, j, :]
        if capacity < LANES:
            lists = jnp.concatenate([lists, jnp.zeros((owners, LANES - capacity), F32)], axis=1)
        if owners < LANES:
            lists = jnp.concatenate([lists, jnp.zeros((LANES - owners, LANES), F32)], axis=0)
        turned[...] = lists.T
        line = turned[pl.ds(0, rows, stride=apart), :]
        for k in range(1, apart):
            line = line + pltpu.roll(turned[pl.ds(k, rows, stride=apart), :], k * owners, axis=1)
        slots[:, j, :] = line
    cell = slots[:, 0, :]
    group = ((cell - 0.5) * (1.0 / (GROUP * NZ))).astype(jnp.int32).astype(F32)
    low = jnp.where(cell > 0.5, group, float(GROUPS))
    high = jnp.where(cell > 0.5, group, -1.0)
    counts = [jnp.int32(0)] * 3
    works = (every_work, outer_work, inner_work)
    for block in range(rows // BLOCK_ROWS):
        span = slice(block * BLOCK_ROWS, block * BLOCK_ROWS + BLOCK_ROWS)
        first = jnp.min(low[span]).astype(jnp.int32)
        last = jnp.max(high[span]).astype(jnp.int32)
        for g in range(GROUPS):
            hit = ((first <= g) & (last >= g)).astype(jnp.int32)
            for w in (0, 1 if g in (0, GROUPS - 1) else 2):
                works[w][counts[w]] = block * GROUPS + g
                counts[w] = counts[w] + hit
    for w in range(3):
        for k in range(TOGETHER):
            works[w][counts[w] + k] = 0
        works[w][WORK - 1] = counts[w]


def layout_kernel(state, wide, first_layers, last_layers):
    wide[...] = jnp.zeros(wide.shape, F32)
    for c in range(3):
        for y in range(CY):
            wide[c, RIM + y, PAD : PAD + CX, 0:NZ] = state[c, :, NZ * y : NZ * y + NZ]
    for out, layer_of in ((first_layers, lambda d: d - 1), (last_layers, lambda d: CY - d)):
        for c in range(3):
            for dist in range(1, RIM + 1):
                base = (c * RIM + dist - 1) * PACKED

                def put(row, rows, base=base, out=out):
                    out[base + row : base + row + 8, :] = rows

                pack(put, wide[c, RIM + layer_of(dist), PAD : PAD + CX, :])


def state_corner_kernel(bulk_first, bulk_last, x_near, x_far, near, far, first, last, before, after):
    from_partners("gx", x_near, x_far, before, after)
    base = 3 * RIM * PACKED
    for bulk, out, layer_of in (
        (bulk_first, first, lambda d: d - 1),
        (bulk_last, last, lambda d: CY - d),
    ):
        out[0:base, :] = bulk[...]
        out[base : base + 64, :] = jnp.zeros((64, LANES), F32)
        for c, dist, row, side in STATE_CORNERS:
            lanes = slice(NZ * layer_of(dist), NZ * layer_of(dist) + NZ)
            out[base + row : base + row + side, 0:NZ] = before[RIM * c + dist : RIM * c + RIM, lanes]
            out[base + row + side : base + row + 2 * side, 0:NZ] = after[RIM * c : RIM * c + side, lanes]
    to_partners("gy", first, last, near, far)


def row_mask(x_place, x_count):
    row = lax.broadcasted_iota(jnp.int32, (XH, LANES), 0)
    lane = lax.broadcasted_iota(jnp.int32, (XH, LANES), 1)
    low = jnp.where(x_place == 0, PAD, 0)
    high = jnp.where(x_place == x_count - 1, PAD + CX, XH)
    return jnp.where((row >= low) & (row < high) & (lane < NZ), 1.0, 0.0).astype(F32)


def layer_mask(y, y_place, y_count):
    outside = ((y < 0) & (y_place == 0)) | ((y >= CY) & (y_place == y_count - 1))
    return jnp.where(outside, 0.0, 1.0).astype(F32)


def next_level(v):
    return pltpu.roll(v, LANES - 1, axis=1)


def last_level(v):
    return pltpu.roll(v, 1, axis=1)


def step_forward(src, dst, low, high, first_row, chunks, mask, places):
    def layer(i, carry):
        y = i + low
        keep = layer_mask(y, places[2], places[3])
        done = []
        for t in range(chunks):
            r = first_row + 8 * t
            here, ahead, behind = pl.ds(r, 8), pl.ds(r + 1, 8), pl.ds(r - 1, 8)
            centre = [src[c, y + RIM, here, :] for c in range(3)]
            scaled = [0.1 * v for v in centre]
            plus = [0.1 - v for v in scaled]
            minus = [0.1 + v for v in scaled]
            inside = mask[here, :] * keep
            for c in range(3):
                v = centre[c]
                total = 0.4 * v + (plus[2] * next_level(v) + minus[2] * last_level(v))
                total = total + (plus[0] * src[c, y + RIM, ahead, :] + minus[0] * src[c, y + RIM, behind, :])
                total = total + (
                    plus[1] * src[c, y + RIM + 1, here, :] + minus[1] * src[c, y + RIM - 1, here, :]
                )
                done.append((c, here, total * inside))
        for c, here, total in done:
            dst[c, y + RIM, here, :] = total
        return carry

    lax.fori_loop(0, high - low, layer, 0, unroll=UNROLL)


def mesh_places():
    return (
        lax.axis_index("gx"),
        lax.axis_size("gx"),
        lax.axis_index("gy"),
        lax.axis_size("gy"),
    )


def slot_columns(slots, row):
    cell = slots[row, 0:1, :] - 1.0
    x = ((cell + 0.5) * (1.0 / (CY * NZ))).astype(jnp.int32)
    rest = cell.astype(jnp.int32) - x * (CY * NZ)
    y = ((rest.astype(F32) + 0.5) * (1.0 / NZ)).astype(jnp.int32)
    high = x // ROWS
    return high * (GROUP - ROWS) + y * ROWS + x, rest - y * NZ


def column_hits(columns):
    place = lax.broadcasted_iota(jnp.int32, (GROUP, columns.shape[1]), 0)
    return jnp.where(place == columns, 1.0, 0.0).astype(BF16)


def block_places(slots, block):
    rows = [slot_columns(slots, block * BLOCK_ROWS + r) for r in range(BLOCK_ROWS)]
    columns = jnp.concatenate([r[0] for r in rows], axis=1)
    level = jnp.concatenate([r[1] for r in rows], axis=1)
    here = lax.broadcasted_iota(jnp.int32, (NZ, BLOCK), 0) == level
    return columns, here


def block_values(slots, block, which):
    rows = [slots[block * BLOCK_ROWS + r, which : which + 1, :] for r in range(BLOCK_ROWS)]
    return jnp.concatenate(rows, axis=1)


def each_product(work, together, body):
    count = work[WORK - 1]

    def some(i, carry):
        for k in range(together):
            item = i * together + k
            code = work[item]
            group = code & (GROUPS - 1)
            offset = jnp.where(item < count, group * GROUP, -(1 << 20))
            body(lax.shift_right_logical(code, GROUPS // 2), group, offset)
        return carry

    lax.fori_loop(0, lax.shift_right_logical(count + together - 1, together // 2), some, 0)


def fold(owners, line):
    reach = LANES // 2
    while reach >= owners:
        line = line + pltpu.roll(line, reach, axis=1)
        reach //= 2
    return line


def forward_kernel(
    beams,
    work,
    wide,
    x_near,
    x_far,
    y_near,
    y_far,
    slots,
    seen,
    sums,
    s0,
    s1,
    s2,
    s3,
    table,
    mask,
    below,
    above,
    before,
    after,
):
    places = mesh_places()
    from_partners("gx", x_near, x_far, before, after)
    mask[...] = row_mask(places[0], places[1])
    from_partners("gy", y_near, y_far, below, above)
    s0[...] = wide[...]
    for c in range(3):
        for y in range(CY):
            lanes = slice(NZ * y, NZ * y + NZ)
            s0[c, RIM + y, PAD - RIM : PAD, 0:NZ] = before[RIM * c : RIM * c + RIM, lanes]
            s0[c, RIM + y, PAD + CX : PAD + CX + RIM, 0:NZ] = after[RIM * c : RIM * c + RIM, lanes]
    for piece, layer_of in ((above, lambda d: RIM + CY - 1 + d), (below, lambda d: RIM - d)):
        for c in range(3):
            for dist in range(1, RIM + 1):
                base = (c * RIM + dist - 1) * PACKED
                s0[c, layer_of(dist), PAD : PAD + CX, :] = unpack(piece[base : base + PACKED, :])
        base = 3 * RIM * PACKED
        for c, dist, row, side in STATE_CORNERS:
            s0[c, layer_of(dist), PAD - side : PAD, :] = piece[base + row : base + row + side, :]
            s0[c, layer_of(dist), PAD + CX : PAD + CX + side, :] = piece[
                base + row + side : base + row + 2 * side, :
            ]
    step_forward(s0, s1, -4, CY + 4, 4, 5, mask, places)
    step_forward(s1, s2, -3, CY + 3, 4, 5, mask, places)
    step_forward(s2, s3, 0, CY, PAD, 4, mask, places)

    half = FIELDS * NZ
    for n, field in enumerate((s1, s2, s3)):
        for c in range(3):
            base = (3 * n + c) * NZ
            for g in range(GROUPS):
                rows = field[c, RIM : RIM + CY, PAD + ROWS * g : PAD + ROWS * g + ROWS, :]
                turned = rows.reshape(GROUP, LANES).T[0:NZ]
                high = turned.astype(BF16)
                table[g, base : base + NZ, :] = high
                table[g, half + base : half + base + NZ, :] = (turned - high.astype(F32)).astype(BF16)

    seen[...] = jnp.zeros(seen.shape, F32)

    def gather(block, group, offset):
        columns, here = block_places(slots, block)
        found = jnp.dot(table[group], column_hits(columns - offset), preferred_element_type=F32)
        weights = [block_values(slots, block, 5 + c) for c in range(3)]
        for n in range(STEPS):
            total = jnp.zeros((1, BLOCK), F32)
            for c in range(3):
                base = (3 * n + c) * NZ
                both = found[base : base + NZ] + found[half + base : half + base + NZ]
                value = jnp.sum(jnp.where(here, both, 0.0), axis=0, keepdims=True)
                total = total + weights[c] * value
            for r in range(BLOCK_ROWS):
                seen[n, pl.ds(block * BLOCK_ROWS + r, 1), :] += total[:, LANES * r : LANES * r + LANES]

    each_product(work, TOGETHER, gather)

    owners = sums.shape[0]
    apart = LANES // owners
    beam = slots[:, 1, :].astype(jnp.int32)
    lane = lax.broadcasted_iota(jnp.int32, (1, LANES), 1)
    lines = [jnp.zeros((1, LANES), F32)] * (STEPS * beams // apart)
    for n in range(STEPS):
        for k in range(beams):
            one = fold(owners, jnp.sum(jnp.where(beam == k, seen[n], 0.0), axis=0, keepdims=True))
            line, place = divmod(n * beams + k, apart)
            here = (lane >= place * owners) & (lane < place * owners + owners)
            lines[line] = jnp.where(here, one, lines[line])
    sums[...] = jnp.zeros(sums.shape, F32)
    for line, total in enumerate(lines):
        sums[:, line : line + 1, :] = jnp.broadcast_to(total[None], (owners, 1, LANES))


def scatter_slots(part_of, together, work, slots, weight, total, force):
    total[...] = jnp.zeros(total.shape, F32)
    half = FIELDS * NZ

    def scatter(block, group, offset):
        columns, here = block_places(slots, block)
        high_rows, low_rows = [], []
        for f in range(FIELDS):
            value = jnp.concatenate(
                [weight[f, pl.ds(block * BLOCK_ROWS + r, 1), :] for r in range(BLOCK_ROWS)], axis=1
            )
            high = value.astype(BF16).astype(F32)
            high_rows.append(jnp.where(here, high, 0.0).astype(BF16))
            low_rows.append(jnp.where(here, value - high, 0.0).astype(BF16))
        table = jnp.concatenate(high_rows + low_rows, axis=0)
        hits = column_hits(columns - offset)
        added = lax.dot_general(table, hits, (((1,), (1,)), ((), ())), preferred_element_type=F32)
        part = part_of(group)
        for f in range(FIELDS):
            total[part, f, 0:NZ, :] += added[NZ * f : NZ * f + NZ] + added[half + NZ * f : half + NZ * f + NZ]

    each_product(work, together, scatter)
    for f in range(FIELDS):
        for k in range(2):
            force[f, k] = total[k, f].T.reshape(CY, ROWS, LANES)


def outer_force_kernel(
    beams, work, slots, seen, sums, force, weight, near, far, first_rows, last_rows, total
):
    owners = sums.shape[0]
    apart = LANES // owners
    lines = jnp.sum(sums[...], axis=0) / GATES
    beam = slots[:, 1, :].astype(jnp.int32)
    lane = lax.broadcasted_iota(jnp.int32, (1, LANES), 1)
    for n in range(STEPS):
        mean = jnp.zeros(beam.shape, F32)
        for k in range(beams):
            line, place = divmod(n * beams + k, apart)
            here = (lane >= place * owners) & (lane < place * owners + owners)
            one = fold(owners, jnp.where(here, lines[line : line + 1], 0.0))
            mean = jnp.where(beam == k, one, mean)
        misfit = seen[n] - mean - slots[:, 2 + n, :]
        for c in range(3):
            weight[3 * n + c] = slots[:, 5 + c, :] * misfit
    scatter_slots(lambda g: (g == GROUPS - 1).astype(jnp.int32), 2, work, slots, weight, total, force)
    for out, k, row_of in ((first_rows, 0, lambda i: i), (last_rows, 1, lambda i: ROWS - 1 - i)):
        for b, (n, c, i) in enumerate(FORCE_BLOCKS):

            def put(row, rows, b=b, out=out):
                out[b, row : row + 8, :] = rows

            pack(put, force[3 * n + c, k, :, row_of(i), :])
    to_partners("gx", first_rows, last_rows, near, far)


def inner_force_kernel(work, slots, weight, force, total):
    scatter_slots(lambda g: (g == 2).astype(jnp.int32), TOGETHER, work, slots, weight, total, force)


def force_rim_kernel(outer, inner, x_near, x_far, near, far, first_layers, last_layers, before, after):
    from_partners("gx", x_near, x_far, before, after)
    index = {key: b for b, key in enumerate(FORCE_BLOCKS)}
    for out, layer_of in ((first_layers, lambda d: d - 1), (last_layers, lambda d: CY - d)):
        for b, (n, c, i) in enumerate(FORCE_BLOCKS):

            def put(row, rows, b=b, out=out):
                out[b * PACKED + row : b * PACKED + row + 8, :] = rows

            f, y = 3 * n + c, layer_of(i + 1)
            pack(put, jnp.concatenate([outer[f, 0, y], inner[f, 0, y], inner[f, 1, y], outer[f, 1, y]], axis=0))
        base = len(FORCE_BLOCKS) * PACKED
        for row, (n, c, dist, side, k) in enumerate(FORCE_CORNERS):
            piece = (before, after)[side]
            block = unpack(piece[index[(n, c, k - 1)]])
            y = layer_of(dist)
            out[base + row : base + row + 1, :] = block[y : y + 1]
    to_partners("gy", first_layers, last_layers, near, far)


def backward_kernel(
    outer,
    inner,
    x_near,
    x_far,
    y_near,
    y_far,
    s0,
    s1,
    s2,
    out,
    a3,
    a2,
    a1,
    a0,
    mask,
    below,
    above,
    before,
    after,
):
    from_partners("gx", x_near, x_far, before, after)
    from_partners("gy", y_near, y_far, below, above)
    places = mesh_places()
    mask[...] = row_mask(places[0], places[1])
    adjoints = (a1, a2, a3)
    for n in range(STEPS):
        adjoints[n][...] = jnp.zeros(adjoints[n].shape, F32)
        for c in range(3):
            for g, (part, k) in enumerate(((outer, 0), (inner, 0), (inner, 1), (outer, 1))):
                row = PAD + ROWS * g
                adjoints[n][c, FRIM : FRIM + CY, row : row + ROWS, :] = part[3 * n + c, k]
    for b, (n, c, i) in enumerate(FORCE_BLOCKS):
        adjoints[n][c, FRIM : FRIM + CY, PAD - 1 - i, :] = unpack(before[b])
        adjoints[n][c, FRIM : FRIM + CY, PAD + CX + i, :] = unpack(after[b])
    for piece, layer_of in ((above, lambda d: FRIM + CY - 1 + d), (below, lambda d: FRIM - d)):
        for b, (n, c, i) in enumerate(FORCE_BLOCKS):
            adjoints[n][c, layer_of(i + 1), PAD : PAD + CX, :] = unpack(piece[b * PACKED : b * PACKED + PACKED, :])
        base = len(FORCE_BLOCKS) * PACKED
        for row, (n, c, dist, side, k) in enumerate(FORCE_CORNERS):
            x = (PAD - k, PAD + CX - 1 + k)[side]
            adjoints[n][c, layer_of(dist), x : x + 1, :] = piece[base + row : base + row + 1, :]

    def pull(field, source, target, low, high, first_row, chunks, add):
        def layer(i, carry):
            y = i + low
            keep = layer_mask(y, places[2], places[3])
            done = []
            for t in range(chunks):
                r = first_row + 8 * t
                here, ahead, behind = pl.ds(r, 8), pl.ds(r + 1, 8), pl.ds(r - 1, 8)
                v = [field[c, y + RIM, here, :] for c in range(3)]
                v_ahead = [field[c, y + RIM, ahead, :] for c in range(3)]
                v_behind = [field[c, y + RIM, behind, :] for c in range(3)]
                v_next = [field[c, y + RIM + 1, here, :] for c in range(3)]
                v_last = [field[c, y + RIM - 1, here, :] for c in range(3)]
                a = [source[c, y + FRIM, here, :] for c in range(3)]
                scaled = [0.1 * f for f in a]
                bends = [None] * 3
                for d, (up, down) in enumerate(((v_ahead, v_behind), (v_next, v_last), (None, None))):
                    for c in range(3):
                        u, w = (up[c], down[c]) if d < 2 else (next_level(v[c]), last_level(v[c]))
                        part = (u - w) * scaled[c]
                        bends[d] = part if bends[d] is None else bends[d] + part
                x_ahead = 0.1 + 0.1 * v_ahead[0]
                x_behind = 0.1 - 0.1 * v_behind[0]
                y_next = 0.1 + 0.1 * v_next[1]
                y_last = 0.1 - 0.1 * v_last[1]
                inside = mask[here, :] * keep
                for c in range(3):
                    total = 0.4 * a[c] - bends[c]
                    total = total + (
                        x_ahead * source[c, y + FRIM, ahead, :] + x_behind * source[c, y + FRIM, behind, :]
                    )
                    total = total + (
                        y_next * source[c, y + FRIM + 1, here, :] + y_last * source[c, y + FRIM - 1, here, :]
                    )
                    product = v[2] * scaled[c]
                    total = total + (next_level(scaled[c] + product) + last_level(scaled[c] - product))
                    if add:
                        total = total + target[c, y + FRIM, here, :]
                    done.append((c, here, total * inside))
            for c, here, total in done:
                target[c, y + FRIM, here, :] = total
            return carry

        lax.fori_loop(0, high - low, layer, 0, unroll=UNROLL)

    pull(s2, a3, a2, -2, CY + 2, 4, 5, True)
    pull(s1, a2, a1, -1, CY + 1, 4, 5, True)
    pull(s0, a1, a0, 0, CY, PAD, 4, False)
    for c in range(3):
        for y in range(CY):
            out[c, :, NZ * y : NZ * y + NZ] = a0[c, FRIM + y, PAD : PAD + CX, 0:NZ]


def swap(near, far, axis):
    def pairs(start):
        lows = range(start, lax.axis_size(axis) - 1, 2)
        return [(i, i + 1) for i in lows] + [(i + 1, i) for i in lows]

    return lax.ppermute(near, axis, pairs(0)), lax.ppermute(far, axis, pairs(1))


def local(initial_state, beam_dir, gate_obs, slot_beam, slot_cell):
    peers, capacity = slot_beam.shape[1:]
    beams = beam_dir.shape[1]
    rows = peers * capacity // LANES
    x_rim = (16, CY * NZ)
    near, far = call(
        state_rows_kernel, (shape(*x_rim), shape(*x_rim)), [pltpu.VMEM(x_rim, F32)] * 2, limit=60, ins=1
    )(initial_state)
    x_near, x_far = swap(near, far, "gx")
    lists = (peers, 8, capacity)
    slots = call(
        arrange_kernel,
        shape(*lists),
        [pltpu.VMEM(lists, F32), pltpu.VMEM((peers, capacity), jnp.int32)],
        limit=60,
        ins=4,
    )(beam_dir, gate_obs, slot_beam, slot_cell)
    slots = lax.all_to_all(slots, AXES, split_axis=0, concat_axis=0, tiled=True)
    work = jax.ShapeDtypeStruct((WORK,), jnp.int32)
    slots, every_work, outer_work, inner_work = call(
        regroup_kernel,
        (shape(rows, 8, LANES), work, work, work),
        [pltpu.VMEM((LANES, LANES), F32)],
        ins=1,
        scalar_out=(1, 2, 3),
        micros=2,
    )(slots)
    field = shape(3, YH, XH, LANES)
    bulk = shape(3 * RIM * PACKED, LANES)
    wide, bulk_first, bulk_last = call(layout_kernel, (field, bulk, bulk), ins=1, micros=2)(initial_state)
    y_rim = (STATE_PIECE, LANES)
    near, far = call(
        state_corner_kernel,
        (shape(*y_rim), shape(*y_rim)),
        [pltpu.VMEM(y_rim, F32)] * 2 + [pltpu.VMEM(x_rim, F32)] * 2,
        ins=4,
    )(bulk_first, bulk_last, x_near, x_far)
    y_near, y_far = swap(near, far, "gy")
    lines = -(-STEPS * beams * peers // LANES // 8) * 8
    mask = pltpu.VMEM((XH, LANES), F32)
    seen, sums, s0, s1, s2 = call(
        functools.partial(forward_kernel, beams),
        (shape(STEPS, rows, LANES), shape(peers, lines, LANES), field, field, field),
        [pltpu.VMEM(field.shape, F32), pltpu.VMEM((GROUPS, 2 * FIELDS * NZ, GROUP), BF16), mask]
        + [pltpu.VMEM(y_rim, F32)] * 2
        + [pltpu.VMEM(x_rim, F32)] * 2,
        limit=32,
        ins=7,
        scalar_in=(0,),
    )(every_work, wide, x_near, x_far, y_near, y_far, slots)
    sums = lax.all_to_all(sums, AXES, split_axis=0, concat_axis=0, tiled=True)
    x_rim = (len(FORCE_BLOCKS), PACKED, LANES)
    part = shape(FIELDS, 2, CY, ROWS, LANES)
    total = pltpu.VMEM((2, FIELDS, LANES, GROUP), F32)
    outer, weight, near, far = call(
        functools.partial(outer_force_kernel, beams),
        (part, shape(FIELDS, rows, LANES), shape(*x_rim), shape(*x_rim)),
        [pltpu.VMEM(x_rim, F32)] * 2 + [total],
        limit=24,
        ins=4,
        scalar_in=(0,),
    )(outer_work, slots, seen, sums)
    x_near, x_far = swap(near, far, "gx")
    inner = call(inner_force_kernel, part, [total], limit=24, ins=3, scalar_in=(0,), micros=6)(
        inner_work, slots, weight
    )
    y_rim = (FORCE_PIECE, LANES)
    near, far = call(
        force_rim_kernel,
        (shape(*y_rim), shape(*y_rim)),
        [pltpu.VMEM(y_rim, F32)] * 2 + [pltpu.VMEM(x_rim, F32)] * 2,
        ins=4,
    )(outer, inner, x_near, x_far)
    y_near, y_far = swap(near, far, "gy")
    return call(
        backward_kernel,
        shape(*initial_state.shape),
        [pltpu.VMEM((3, FH, XH, LANES), F32)] * 4
        + [mask]
        + [pltpu.VMEM(y_rim, F32)] * 2
        + [pltpu.VMEM(x_rim, F32)] * 2,
        limit=32,
        ins=9,
    )(outer, inner, x_near, x_far, y_near, y_far, s0, s1, s2)


def solution(mesh):
    in_specs = (
        P(None, "gx", "gy"),
        P(None, ("gx", "gy")),
        P(None, ("gx", "gy"), None, None),
        P(("gx", "gy"), None, None),
        P(("gx", "gy"), None, None),
    )
    out_specs = P(None, "gx", "gy")
    return jax.shard_map(local, mesh=mesh, in_specs=in_specs, out_specs=out_specs, check_vma=False)
```

```python
import functools

import jax
import jax.numpy as jnp
from jax import lax
from jax.experimental import pallas as pl
from jax.experimental.pallas import tpu as pltpu
from jax.sharding import PartitionSpec as P

NZ = 96
GATES = 512
STEPS = 3
LANES = 128
CX = 32
CY = 32
COLUMNS = CX * CY
RIM = 5
PAD = 8
XH = CX + 2 * PAD
YH = CY + 2 * RIM
PACKED = CX * NZ // LANES
FRIM = 3
FH = CY + 2 * FRIM
EDGE = 4
FIELDS = 3 * STEPS
UNROLL = 8
ROWS = 8
GROUPS = CX // ROWS
GROUP = ROWS * CY
BLOCK = 256
BLOCK_ROWS = BLOCK // LANES
TOGETHER = 4
WORK = 128
F32 = jnp.float32
BF16 = jnp.bfloat16
AXES = ("gx", "gy")
MIB = 1024 * 1024


def call(kernel, outs, scratch=(), limit=12, ins=0, scalar_in=(), scalar_out=(), micros=1):
    def specs(count, scalar):
        spaces = [pltpu.SMEM if i in scalar else pltpu.VMEM for i in range(count)]
        return [pl.BlockSpec(memory_space=space) for space in spaces]

    single = not isinstance(outs, tuple)
    out_specs = specs(1 if single else len(outs), scalar_out)
    return pl.pallas_call(
        kernel,
        out_shape=outs,
        in_specs=specs(ins, scalar_in),
        out_specs=out_specs[0] if single else tuple(out_specs),
        scratch_shapes=list(scratch),
        compiler_params=pltpu.CompilerParams(vmem_limit_bytes=limit * MIB),
        cost_estimate=pl.CostEstimate(flops=0, bytes_accessed=micros * 3_000_000, transcendentals=0),
    )


def shape(*dims):
    return jax.ShapeDtypeStruct(dims, F32)


def lane_of(rows=8):
    return lax.broadcasted_iota(jnp.int32, (rows, LANES), 1)


def pack(put, block):
    lane = lane_of()
    last = block[24:32]
    for j in range(3):
        tail = pltpu.roll(last, 96 - 32 * j, axis=1)
        put(8 * j, jnp.where(lane < NZ, block[8 * j : 8 * j + 8], tail))


def unpack(rows):
    lane = lane_of()
    last = jnp.zeros((8, LANES), F32)
    parts = []
    for j in range(3):
        piece = rows[8 * j : 8 * j + 8]
        parts.append(jnp.where(lane < NZ, piece, 0.0))
        moved = pltpu.roll(piece, (32 * j - 96) % LANES, axis=1)
        last = jnp.where((lane >= 32 * j) & (lane < 32 * j + 32), moved, last)
    return jnp.concatenate(parts + [last], axis=0)


def is_odd(axis):
    return lax.axis_index(axis) % 2 == 1


def to_partners(axis, first, last, near, far):
    odd = is_odd(axis)
    near[...] = jnp.where(odd, first[...], last[...])
    far[...] = jnp.where(odd, last[...], first[...])


def from_partners(axis, near, far, behind, ahead):
    odd = is_odd(axis)
    behind[...] = jnp.where(odd, near[...], far[...])
    ahead[...] = jnp.where(odd, far[...], near[...])


def corner_rows(rim):
    rows, out = 0, []
    for comp in range(3):
        for dist in range(1, rim):
            out.append((comp, dist, rows, rim - dist))
            rows += 2 * (rim - dist)
    return out, rows


STATE_CORNERS, STATE_CORNER_ROWS = corner_rows(RIM)
STATE_PIECE = 3 * RIM * PACKED + 64
FORCE_BLOCKS = [(n, c, i) for n in range(STEPS) for c in range(3) for i in range(n + 1)]
FORCE_CORNERS = [
    (n, c, dist, side, k)
    for n in range(STEPS)
    for c in range(3)
    for dist in range(1, n + 1)
    for side in range(2)
    for k in range(1, n + 2 - dist)
]
FORCE_PIECE = len(FORCE_BLOCKS) * PACKED + 24


def state_rows_kernel(top, bottom, near, far, first_rows, last_rows):
    for c in range(3):
        first_rows[RIM * c : RIM * c + RIM, :] = top[c, 0:RIM, :]
        last_rows[RIM * c : RIM * c + RIM, :] = bottom[c, ROWS - RIM : ROWS, :]
    first_rows[3 * RIM : 16, :] = jnp.zeros((1, CY * NZ), F32)
    last_rows[3 * RIM : 16, :] = jnp.zeros((1, CY * NZ), F32)
    to_partners("gx", first_rows, last_rows, near, far)


def arrange_kernel(beam_dir, obs, beam, cell, slots, values, places):
    beams = beam_dir.shape[1]
    owned = beam[0]
    lists, capacity = owned.shape
    used = owned >= 0
    masks = [owned == k for k in range(beams)]

    def spread(parts):
        total = jnp.zeros(owned.shape, F32)
        for k in range(beams):
            total = jnp.where(masks[k], parts[k], total)
        return total

    cells = cell[0].astype(F32)
    values[:, 0, :] = cells + 1.0
    values[:, 1, :] = owned.astype(F32)
    for n in range(STEPS):
        seen = obs[n, 0]
        means = [jnp.sum(jnp.where(m, seen, 0.0), keepdims=True) / GATES for m in masks]
        values[:, 2 + n, :] = jnp.where(used, seen - spread(means), 0.0)
    for c in range(3):
        values[:, 5 + c, :] = spread([beam_dir[c : c + 1, k : k + 1] for k in range(beams)])

    group = ((cells + 0.5) * (1.0 / (GROUP * NZ))).astype(jnp.int32)
    row = lax.broadcasted_iota(jnp.int32, (capacity, capacity), 0)
    column = lax.broadcasted_iota(jnp.int32, (capacity, capacity), 1)
    ahead = jnp.where(row <= column, 1.0, 0.0).astype(BF16)
    ones = [jnp.where(used & (group == g), 1.0, 0.0) for g in range(GROUPS)]
    counts = [jnp.sum(o, axis=1, keepdims=True) for o in ones]
    place = jnp.full(owned.shape, -1.0, F32)
    end = jnp.zeros((lists, 1), F32)
    left = counts[0] + counts[1] + counts[2] + counts[3]
    for g in range(GROUPS):
        start = jnp.minimum(jnp.maximum(float(capacity // GROUPS * g), end), capacity - left)
        upto = jnp.dot(ones[g].astype(BF16), ahead, preferred_element_type=F32)
        place = jnp.where(ones[g] > 0.5, start + upto - 1.0, place)
        end = start + counts[g]
        left = left - counts[g]
    places[...] = place.astype(jnp.int32)

    def move(i, carry):
        full = values[i]
        high = full.astype(BF16).astype(F32)
        mid = (full - high).astype(BF16).astype(F32)
        low = full - high - mid
        three = jnp.concatenate([high, mid, low], axis=0).astype(BF16)
        hits = jnp.where(row == places[pl.ds(i, 1), :], 1.0, 0.0).astype(BF16)
        moved = lax.dot_general(three, hits, (((1,), (1,)), ((), ())), preferred_element_type=F32)
        slots[i] = moved[0:8] + moved[8:16] + moved[16:24]
        return carry

    lax.fori_loop(0, lists, move, 0, unroll=8)


def regroup_kernel(received, slots, every_work, outer_work, inner_work, turned):
    owners, _, capacity = received.shape
    apart = LANES // owners
    rows = capacity // apart
    for j in range(8):
        lists = received[:, j, :]
        if capacity < LANES:
            lists = jnp.concatenate([lists, jnp.zeros((owners, LANES - capacity), F32)], axis=1)
        if owners < LANES:
            lists = jnp.concatenate([lists, jnp.zeros((LANES - owners, LANES), F32)], axis=0)
        turned[...] = lists.T
        line = turned[pl.ds(0, rows, stride=apart), :]
        for k in range(1, apart):
            line = line + pltpu.roll(turned[pl.ds(k, rows, stride=apart), :], k * owners, axis=1)
        slots[:, j, :] = line
    cell = slots[:, 0, :]
    group = ((cell - 0.5) * (1.0 / (GROUP * NZ))).astype(jnp.int32).astype(F32)
    low = jnp.where(cell > 0.5, group, float(GROUPS))
    high = jnp.where(cell > 0.5, group, -1.0)
    counts = [jnp.int32(0)] * 3
    works = (every_work, outer_work, inner_work)
    for block in range(rows // BLOCK_ROWS):
        span = slice(block * BLOCK_ROWS, block * BLOCK_ROWS + BLOCK_ROWS)
        first = jnp.min(low[span]).astype(jnp.int32)
        last = jnp.max(high[span]).astype(jnp.int32)
        for g in range(GROUPS):
            hit = ((first <= g) & (last >= g)).astype(jnp.int32)
            for w in (0, 1 if g in (0, GROUPS - 1) else 2):
                works[w][counts[w]] = block * GROUPS + g
                counts[w] = counts[w] + hit
    for w in range(3):
        for k in range(TOGETHER):
            works[w][counts[w] + k] = 0
        works[w][WORK - 1] = counts[w]


def state_layers_kernel(state, first_layers, last_layers):
    blank = jnp.zeros((CX, LANES - NZ), F32)
    for out, layer_of in ((first_layers, lambda d: d - 1), (last_layers, lambda d: CY - d)):
        for c in range(3):
            for dist in range(1, RIM + 1):
                base = (c * RIM + dist - 1) * PACKED
                y = layer_of(dist)

                def put(row, rows, base=base, out=out):
                    out[base + row : base + row + 8, :] = rows

                pack(put, jnp.concatenate([state[c, :, NZ * y : NZ * y + NZ], blank], axis=1))


def state_corner_kernel(bulk_first, bulk_last, x_near, x_far, near, far, first, last, before, after):
    from_partners("gx", x_near, x_far, before, after)
    base = 3 * RIM * PACKED
    for bulk, out, layer_of in (
        (bulk_first, first, lambda d: d - 1),
        (bulk_last, last, lambda d: CY - d),
    ):
        out[0:base, :] = bulk[...]
        out[base : base + 64, :] = jnp.zeros((64, LANES), F32)
        for c, dist, row, side in STATE_CORNERS:
            lanes = slice(NZ * layer_of(dist), NZ * layer_of(dist) + NZ)
            out[base + row : base + row + side, 0:NZ] = before[RIM * c + dist : RIM * c + RIM, lanes]
            out[base + row + side : base + row + 2 * side, 0:NZ] = after[RIM * c : RIM * c + side, lanes]
    to_partners("gy", first, last, near, far)


def row_mask(x_place, x_count):
    row = lax.broadcasted_iota(jnp.int32, (XH, LANES), 0)
    lane = lax.broadcasted_iota(jnp.int32, (XH, LANES), 1)
    low = jnp.where(x_place == 0, PAD, 0)
    high = jnp.where(x_place == x_count - 1, PAD + CX, XH)
    return jnp.where((row >= low) & (row < high) & (lane < NZ), 1.0, 0.0).astype(F32)


def layer_mask(y, y_place, y_count):
    outside = ((y < 0) & (y_place == 0)) | ((y >= CY) & (y_place == y_count - 1))
    return jnp.where(outside, 0.0, 1.0).astype(F32)


def next_level(v):
    return pltpu.roll(v, LANES - 1, axis=1)


def last_level(v):
    return pltpu.roll(v, 1, axis=1)


def step_forward(src, dst, low, high, first_row, chunks, mask, places):
    def layer(i, carry):
        y = i + low
        keep = layer_mask(y, places[2], places[3])
        done = []
        for t in range(chunks):
            r = first_row + 8 * t
            here, ahead, behind = pl.ds(r, 8), pl.ds(r + 1, 8), pl.ds(r - 1, 8)
            centre = [src[c, y + RIM, here, :] for c in range(3)]
            scaled = [0.1 * v for v in centre]
            plus = [0.1 - v for v in scaled]
            minus = [0.1 + v for v in scaled]
            inside = mask[here, :] * keep
            for c in range(3):
                v = centre[c]
                total = 0.4 * v + (plus[2] * next_level(v) + minus[2] * last_level(v))
                total = total + (plus[0] * src[c, y + RIM, ahead, :] + minus[0] * src[c, y + RIM, behind, :])
                total = total + (
                    plus[1] * src[c, y + RIM + 1, here, :] + minus[1] * src[c, y + RIM - 1, here, :]
                )
                done.append((c, here, total * inside))
        for c, here, total in done:
            dst[c, y + RIM, here, :] = total
        return carry

    lax.fori_loop(0, high - low, layer, 0, unroll=UNROLL)


def mesh_places():
    return (
        lax.axis_index("gx"),
        lax.axis_size("gx"),
        lax.axis_index("gy"),
        lax.axis_size("gy"),
    )


def slot_columns(slots, row):
    cell = slots[row, 0:1, :] - 1.0
    x = ((cell + 0.5) * (1.0 / (CY * NZ))).astype(jnp.int32)
    rest = cell.astype(jnp.int32) - x * (CY * NZ)
    y = ((rest.astype(F32) + 0.5) * (1.0 / NZ)).astype(jnp.int32)
    high = x // ROWS
    return high * (GROUP - ROWS) + y * ROWS + x, rest - y * NZ


def column_hits(columns):
    place = lax.broadcasted_iota(jnp.int32, (GROUP, columns.shape[1]), 0)
    return jnp.where(place == columns, 1.0, 0.0).astype(BF16)


def block_places(slots, block):
    rows = [slot_columns(slots, block * BLOCK_ROWS + r) for r in range(BLOCK_ROWS)]
    columns = jnp.concatenate([r[0] for r in rows], axis=1)
    level = jnp.concatenate([r[1] for r in rows], axis=1)
    here = lax.broadcasted_iota(jnp.int32, (NZ, BLOCK), 0) == level
    return columns, here


def block_values(slots, block, which):
    rows = [slots[block * BLOCK_ROWS + r, which : which + 1, :] for r in range(BLOCK_ROWS)]
    return jnp.concatenate(rows, axis=1)


def each_product(work, together, body):
    count = work[WORK - 1]

    def some(i, carry):
        for k in range(together):
            item = i * together + k
            code = work[item]
            group = code & (GROUPS - 1)
            offset = jnp.where(item < count, group * GROUP, -(1 << 20))
            body(lax.shift_right_logical(code, GROUPS // 2), group, offset)
        return carry

    lax.fori_loop(0, lax.shift_right_logical(count + together - 1, together // 2), some, 0)


def fold(owners, line):
    reach = LANES // 2
    while reach >= owners:
        line = line + pltpu.roll(line, reach, axis=1)
        reach //= 2
    return line


def forward_kernel(
    beams,
    work,
    state,
    x_near,
    x_far,
    y_near,
    y_far,
    slots,
    seen,
    sums,
    s0,
    s1,
    s2,
    s3,
    table,
    mask,
    below,
    above,
    before,
    after,
):
    places = mesh_places()
    from_partners("gx", x_near, x_far, before, after)
    mask[...] = row_mask(places[0], places[1])
    from_partners("gy", y_near, y_far, below, above)
    s0[...] = jnp.zeros(s0.shape, F32)
    for c in range(3):
        for y in range(CY):
            lanes = slice(NZ * y, NZ * y + NZ)
            s0[c, RIM + y, PAD : PAD + CX, 0:NZ] = state[c, :, lanes]
            s0[c, RIM + y, PAD - RIM : PAD, 0:NZ] = before[RIM * c : RIM * c + RIM, lanes]
            s0[c, RIM + y, PAD + CX : PAD + CX + RIM, 0:NZ] = after[RIM * c : RIM * c + RIM, lanes]
    for piece, layer_of in ((above, lambda d: RIM + CY - 1 + d), (below, lambda d: RIM - d)):
        for c in range(3):
            for dist in range(1, RIM + 1):
                base = (c * RIM + dist - 1) * PACKED
                s0[c, layer_of(dist), PAD : PAD + CX, :] = unpack(piece[base : base + PACKED, :])
        base = 3 * RIM * PACKED
        for c, dist, row, side in STATE_CORNERS:
            s0[c, layer_of(dist), PAD - side : PAD, :] = piece[base + row : base + row + side, :]
            s0[c, layer_of(dist), PAD + CX : PAD + CX + side, :] = piece[
                base + row + side : base + row + 2 * side, :
            ]
    step_forward(s0, s1, -4, CY + 4, 4, 5, mask, places)
    step_forward(s1, s2, -3, CY + 3, 4, 5, mask, places)
    step_forward(s2, s3, 0, CY, PAD, 4, mask, places)

    half = FIELDS * NZ
    for n, field in enumerate((s1, s2, s3)):
        for c in range(3):
            base = (3 * n + c) * NZ
            for g in range(GROUPS):
                rows = field[c, RIM : RIM + CY, PAD + ROWS * g : PAD + ROWS * g + ROWS, :]
                turned = rows.reshape(GROUP, LANES).T[0:NZ]
                high = turned.astype(BF16)
                table[g, base : base + NZ, :] = high
                table[g, half + base : half + base + NZ, :] = (turned - high.astype(F32)).astype(BF16)

    seen[...] = jnp.zeros(seen.shape, F32)

    def gather(block, group, offset):
        columns, here = block_places(slots, block)
        found = jnp.dot(table[group], column_hits(columns - offset), preferred_element_type=F32)
        weights = [block_values(slots, block, 5 + c) for c in range(3)]
        for n in range(STEPS):
            total = jnp.zeros((1, BLOCK), F32)
            for c in range(3):
                base = (3 * n + c) * NZ
                both = found[base : base + NZ] + found[half + base : half + base + NZ]
                value = jnp.sum(jnp.where(here, both, 0.0), axis=0, keepdims=True)
                total = total + weights[c] * value
            for r in range(BLOCK_ROWS):
                seen[n, pl.ds(block * BLOCK_ROWS + r, 1), :] += total[:, LANES * r : LANES * r + LANES]

    each_product(work, TOGETHER, gather)

    owners = sums.shape[0]
    apart = LANES // owners
    beam = slots[:, 1, :].astype(jnp.int32)
    lane = lax.broadcasted_iota(jnp.int32, (1, LANES), 1)
    lines = [jnp.zeros((1, LANES), F32)] * (STEPS * beams // apart)
    for n in range(STEPS):
        for k in range(beams):
            one = fold(owners, jnp.sum(jnp.where(beam == k, seen[n], 0.0), axis=0, keepdims=True))
            line, place = divmod(n * beams + k, apart)
            here = (lane >= place * owners) & (lane < place * owners + owners)
            lines[line] = jnp.where(here, one, lines[line])
    for line, total in enumerate(lines):
        span = slice(LANES * line, LANES * line + LANES)
        sums[:, :, span] = jnp.broadcast_to(total[None], (owners, 1, LANES))


def scatter_slots(part_of, together, work, slots, weight, total, force):
    total[...] = jnp.zeros(total.shape, F32)
    half = FIELDS * NZ

    def scatter(block, group, offset):
        columns, here = block_places(slots, block)
        high_rows, low_rows = [], []
        for f in range(FIELDS):
            value = jnp.concatenate(
                [weight[f, pl.ds(block * BLOCK_ROWS + r, 1), :] for r in range(BLOCK_ROWS)], axis=1
            )
            high = value.astype(BF16).astype(F32)
            high_rows.append(jnp.where(here, high, 0.0).astype(BF16))
            low_rows.append(jnp.where(here, value - high, 0.0).astype(BF16))
        table = jnp.concatenate(high_rows + low_rows, axis=0)
        hits = column_hits(columns - offset)
        added = lax.dot_general(table, hits, (((1,), (1,)), ((), ())), preferred_element_type=F32)
        part = part_of(group)
        for f in range(FIELDS):
            total[part, f, 0:NZ, :] += added[NZ * f : NZ * f + NZ] + added[half + NZ * f : half + NZ * f + NZ]

    each_product(work, together, scatter)
    for f in range(FIELDS):
        for k in range(2):
            force[f, k] = total[k, f].T.reshape(CY, ROWS, LANES)


def outer_force_kernel(
    beams, work, slots, seen, sums, force, weight, near, far, first_rows, last_rows, total
):
    owners = sums.shape[0]
    apart = LANES // owners
    lines = jnp.sum(sums[...], axis=0) / GATES
    beam = slots[:, 1, :].astype(jnp.int32)
    lane = lax.broadcasted_iota(jnp.int32, (1, LANES), 1)
    for n in range(STEPS):
        mean = jnp.zeros(beam.shape, F32)
        for k in range(beams):
            line, place = divmod(n * beams + k, apart)
            here = (lane >= place * owners) & (lane < place * owners + owners)
            one = fold(owners, jnp.where(here, lines[:, LANES * line : LANES * line + LANES], 0.0))
            mean = jnp.where(beam == k, one, mean)
        misfit = seen[n] - mean - slots[:, 2 + n, :]
        for c in range(3):
            weight[3 * n + c] = slots[:, 5 + c, :] * misfit
    scatter_slots(lambda g: (g == GROUPS - 1).astype(jnp.int32), 2, work, slots, weight, total, force)
    for out, k, row_of in ((first_rows, 0, lambda i: i), (last_rows, 1, lambda i: ROWS - 1 - i)):
        for b, (n, c, i) in enumerate(FORCE_BLOCKS):

            def put(row, rows, b=b, out=out):
                out[b, row : row + 8, :] = rows

            pack(put, force[3 * n + c, k, :, row_of(i), :])
    to_partners("gx", first_rows, last_rows, near, far)


def inner_force_kernel(work, slots, weight, force, total):
    scatter_slots(lambda g: (g == 2).astype(jnp.int32), TOGETHER, work, slots, weight, total, force)


def force_rim_kernel(outer, inner, x_near, x_far, near, far, first_layers, last_layers, before, after):
    from_partners("gx", x_near, x_far, before, after)
    index = {key: b for b, key in enumerate(FORCE_BLOCKS)}
    for out, layer_of in ((first_layers, lambda d: d - 1), (last_layers, lambda d: CY - d)):
        for b, (n, c, i) in enumerate(FORCE_BLOCKS):

            def put(row, rows, b=b, out=out):
                out[b * PACKED + row : b * PACKED + row + 8, :] = rows

            f, y = 3 * n + c, layer_of(i + 1)
            pack(put, jnp.concatenate([outer[f, 0, y], inner[f, 0, y], inner[f, 1, y], outer[f, 1, y]], axis=0))
        base = len(FORCE_BLOCKS) * PACKED
        for row, (n, c, dist, side, k) in enumerate(FORCE_CORNERS):
            piece = (before, after)[side]
            block = unpack(piece[index[(n, c, k - 1)]])
            y = layer_of(dist)
            out[base + row : base + row + 1, :] = block[y : y + 1]
    to_partners("gy", first_layers, last_layers, near, far)


def pull(field, source, target, low, high, first_row, chunks, add, mask, places):
    def layer(i, carry):
        y = i + low
        keep = layer_mask(y, places[2], places[3])
        done = []
        for t in range(chunks):
            r = first_row + 8 * t
            here, ahead, behind = pl.ds(r, 8), pl.ds(r + 1, 8), pl.ds(r - 1, 8)
            v = [field[c, y + RIM, here, :] for c in range(3)]
            v_ahead = [field[c, y + RIM, ahead, :] for c in range(3)]
            v_behind = [field[c, y + RIM, behind, :] for c in range(3)]
            v_next = [field[c, y + RIM + 1, here, :] for c in range(3)]
            v_last = [field[c, y + RIM - 1, here, :] for c in range(3)]
            a = [source[c, y + FRIM, here, :] for c in range(3)]
            scaled = [0.1 * f for f in a]
            bends = [None] * 3
            for d, (up, down) in enumerate(((v_ahead, v_behind), (v_next, v_last), (None, None))):
                for c in range(3):
                    u, w = (up[c], down[c]) if d < 2 else (next_level(v[c]), last_level(v[c]))
                    part = (u - w) * scaled[c]
                    bends[d] = part if bends[d] is None else bends[d] + part
            x_ahead = 0.1 + 0.1 * v_ahead[0]
            x_behind = 0.1 - 0.1 * v_behind[0]
            y_next = 0.1 + 0.1 * v_next[1]
            y_last = 0.1 - 0.1 * v_last[1]
            inside = mask[here, :] * keep
            for c in range(3):
                total = 0.4 * a[c] - bends[c]
                total = total + (
                    x_ahead * source[c, y + FRIM, ahead, :] + x_behind * source[c, y + FRIM, behind, :]
                )
                total = total + (
                    y_next * source[c, y + FRIM + 1, here, :] + y_last * source[c, y + FRIM - 1, here, :]
                )
                product = v[2] * scaled[c]
                total = total + (next_level(scaled[c] + product) + last_level(scaled[c] - product))
                if add:
                    total = total + target[c, y + FRIM, here, :]
                done.append((c, here, total * inside))
        for c, here, total in done:
            target[c, y + FRIM, here, :] = total
        return carry

    lax.fori_loop(0, high - low, layer, 0, unroll=min(UNROLL, high - low))


def edge_layers(side):
    start = (FRIM, FRIM + CY - EDGE)[side]
    return slice(start, start + EDGE)


def inner_backward_kernel(
    outer, inner, x_near, x_far, s0, s1, s2, part, e1, e2, e3, a1, a2, a3, a0, mask, before, after
):
    from_partners("gx", x_near, x_far, before, after)
    places = mesh_places()
    mask[...] = row_mask(places[0], places[1])
    adjoints = (a1, a2, a3)
    for n in range(STEPS):
        adjoints[n][...] = jnp.zeros(adjoints[n].shape, F32)
        for c in range(3):
            for g, (force, k) in enumerate(((outer, 0), (inner, 0), (inner, 1), (outer, 1))):
                row = PAD + ROWS * g
                adjoints[n][c, FRIM : FRIM + CY, row : row + ROWS, :] = force[3 * n + c, k]
    for b, (n, c, i) in enumerate(FORCE_BLOCKS):
        adjoints[n][c, FRIM : FRIM + CY, PAD - 1 - i, :] = unpack(before[b])
        adjoints[n][c, FRIM : FRIM + CY, PAD + CX + i, :] = unpack(after[b])
    pull(s2, a3, a2, 1, CY - 1, 4, 5, True, mask, places)
    pull(s1, a2, a1, 2, CY - 2, 4, 5, True, mask, places)
    pull(s0, a1, a0, 3, CY - 3, PAD, 4, False, mask, places)
    for n, edges in enumerate((e1, e2, e3)):
        for side in range(2):
            edges[:, side] = adjoints[n][:, edge_layers(side)]
    for c in range(3):
        for y in range(3, CY - 3):
            part[c, :, NZ * y : NZ * y + NZ] = a0[c, FRIM + y, PAD : PAD + CX, 0:NZ]


def backward_kernel(
    part, e1, e2, e3, y_near, y_far, s0, s1, s2, out, a1, a2, a3, a0, mask, below, above
):
    from_partners("gy", y_near, y_far, below, above)
    places = mesh_places()
    mask[...] = row_mask(places[0], places[1])
    adjoints = (a1, a2, a3)
    out[...] = part[...]
    for n, edges in enumerate((e1, e2, e3)):
        for side in range(2):
            adjoints[n][:, edge_layers(side)] = edges[:, side]
        for start in (0, FRIM + CY):
            adjoints[n][:, start : start + FRIM] = jnp.zeros((3, FRIM, XH, LANES), F32)
    for piece, layer_of in ((above, lambda d: FRIM + CY - 1 + d), (below, lambda d: FRIM - d)):
        for b, (n, c, i) in enumerate(FORCE_BLOCKS):
            adjoints[n][c, layer_of(i + 1), PAD : PAD + CX, :] = unpack(piece[b * PACKED : b * PACKED + PACKED, :])
        base = len(FORCE_BLOCKS) * PACKED
        for row, (n, c, dist, side, k) in enumerate(FORCE_CORNERS):
            x = (PAD - k, PAD + CX - 1 + k)[side]
            adjoints[n][c, layer_of(dist), x : x + 1, :] = piece[base + row : base + row + 1, :]
    for low in (-2, CY - 1):
        pull(s2, a3, a2, low, low + 3, 4, 5, True, mask, places)
    for low in (-1, CY - 2):
        pull(s1, a2, a1, low, low + 3, 4, 5, True, mask, places)
    for low in (0, CY - 3):
        pull(s0, a1, a0, low, low + 3, PAD, 4, False, mask, places)
    for c in range(3):
        for y in (0, 1, 2, CY - 3, CY - 2, CY - 1):
            out[c, :, NZ * y : NZ * y + NZ] = a0[c, FRIM + y, PAD : PAD + CX, 0:NZ]


def swap(near, far, axis):
    def pairs(start):
        lows = range(start, lax.axis_size(axis) - 1, 2)
        return [(i, i + 1) for i in lows] + [(i + 1, i) for i in lows]

    return lax.ppermute(near, axis, pairs(0)), lax.ppermute(far, axis, pairs(1))


def local(initial_state, beam_dir, gate_obs, slot_beam, slot_cell):
    peers, capacity = slot_beam.shape[1:]
    beams = beam_dir.shape[1]
    rows = peers * capacity // LANES
    x_rim = (16, CY * NZ)
    edge = (3, ROWS, CY * NZ)
    near, far = pl.pallas_call(
        state_rows_kernel,
        out_shape=(shape(*x_rim), shape(*x_rim)),
        in_specs=[
            pl.BlockSpec(edge, lambda i: (0, 0, 0)),
            pl.BlockSpec(edge, lambda i: (0, GROUPS - 1, 0)),
        ],
        out_specs=(pl.BlockSpec(x_rim, lambda i: (0, 0)), pl.BlockSpec(x_rim, lambda i: (0, 0))),
        grid=(1,),
        scratch_shapes=[pltpu.VMEM(x_rim, F32)] * 2,
        compiler_params=pltpu.CompilerParams(vmem_limit_bytes=60 * MIB),
    )(initial_state, initial_state)
    x_near, x_far = swap(near, far, "gx")
    lists = (peers, 8, capacity)
    slots = call(
        arrange_kernel,
        shape(*lists),
        [pltpu.VMEM(lists, F32), pltpu.VMEM((peers, capacity), jnp.int32)],
        limit=60,
        ins=4,
    )(beam_dir, gate_obs, slot_beam, slot_cell)
    slots = lax.all_to_all(slots, AXES, split_axis=0, concat_axis=0, tiled=True)
    work = jax.ShapeDtypeStruct((WORK,), jnp.int32)
    slots, every_work, outer_work, inner_work = call(
        regroup_kernel,
        (shape(rows, 8, LANES), work, work, work),
        [pltpu.VMEM((LANES, LANES), F32)],
        ins=1,
        scalar_out=(1, 2, 3),
        micros=2,
    )(slots)
    field = shape(3, YH, XH, LANES)
    bulk = shape(3 * RIM * PACKED, LANES)
    bulk_first, bulk_last = call(state_layers_kernel, (bulk, bulk), ins=1)(initial_state)
    y_rim = (STATE_PIECE, LANES)
    near, far = call(
        state_corner_kernel,
        (shape(*y_rim), shape(*y_rim)),
        [pltpu.VMEM(y_rim, F32)] * 2 + [pltpu.VMEM(x_rim, F32)] * 2,
        ins=4,
    )(bulk_first, bulk_last, x_near, x_far)
    y_near, y_far = swap(near, far, "gy")
    mask = pltpu.VMEM((XH, LANES), F32)
    seen, sums, s0, s1, s2 = call(
        functools.partial(forward_kernel, beams),
        (shape(STEPS, rows, LANES), shape(peers, 1, STEPS * beams * peers), field, field, field),
        [pltpu.VMEM(field.shape, F32), pltpu.VMEM((GROUPS, 2 * FIELDS * NZ, GROUP), BF16), mask]
        + [pltpu.VMEM(y_rim, F32)] * 2
        + [pltpu.VMEM(x_rim, F32)] * 2,
        limit=32,
        ins=7,
        scalar_in=(0,),
    )(every_work, initial_state, x_near, x_far, y_near, y_far, slots)
    sums = lax.all_to_all(sums, AXES, split_axis=0, concat_axis=0, tiled=True)
    x_rim = (len(FORCE_BLOCKS), PACKED, LANES)
    part = shape(FIELDS, 2, CY, ROWS, LANES)
    total = pltpu.VMEM((2, FIELDS, LANES, GROUP), F32)
    outer, weight, near, far = call(
        functools.partial(outer_force_kernel, beams),
        (part, shape(FIELDS, rows, LANES), shape(*x_rim), shape(*x_rim)),
        [pltpu.VMEM(x_rim, F32)] * 2 + [total],
        limit=24,
        ins=4,
        scalar_in=(0,),
    )(outer_work, slots, seen, sums)
    x_near, x_far = swap(near, far, "gx")
    inner = call(inner_force_kernel, part, [total], limit=24, ins=3, scalar_in=(0,), micros=6)(
        inner_work, slots, weight
    )
    y_rim = (FORCE_PIECE, LANES)
    near, far = call(
        force_rim_kernel,
        (shape(*y_rim), shape(*y_rim)),
        [pltpu.VMEM(y_rim, F32)] * 2 + [pltpu.VMEM(x_rim, F32)] * 2,
        ins=4,
    )(outer, inner, x_near, x_far)
    y_near, y_far = swap(near, far, "gy")
    edges = shape(3, 2, EDGE, XH, LANES)
    adjoint = pltpu.VMEM((3, FH, XH, LANES), F32)
    whole = shape(*initial_state.shape)
    part, e1, e2, e3 = call(
        inner_backward_kernel,
        (whole, edges, edges, edges),
        [adjoint] * 4 + [mask] + [pltpu.VMEM(x_rim, F32)] * 2,
        limit=32,
        ins=7,
        micros=8,
    )(outer, inner, x_near, x_far, s0, s1, s2)
    return call(
        backward_kernel, whole, [adjoint] * 4 + [mask] + [pltpu.VMEM(y_rim, F32)] * 2, limit=32, ins=9
    )(part, e1, e2, e3, y_near, y_far, s0, s1, s2)


def solution(mesh):
    in_specs = (
        P(None, "gx", "gy"),
        P(None, ("gx", "gy")),
        P(None, ("gx", "gy"), None, None),
        P(("gx", "gy"), None, None),
        P(("gx", "gy"), None, None),
    )
    out_specs = P(None, "gx", "gy")
    return jax.shard_map(local, mesh=mesh, in_specs=in_specs, out_specs=out_specs, check_vma=False)
```

```python
import functools

import jax
import jax.numpy as jnp
from jax import lax
from jax.experimental import pallas as pl
from jax.experimental.pallas import tpu as pltpu
from jax.sharding import PartitionSpec as P

NZ = 96
GATES = 512
STEPS = 3
LANES = 128
CX = 32
CY = 32
COLUMNS = CX * CY
RIM = 5
PAD = 8
XH = CX + 2 * PAD
YH = CY + 2 * RIM
PACKED = CX * NZ // LANES
FRIM = 3
FH = CY + 2 * FRIM
EDGE = 4
FIELDS = 3 * STEPS
UNROLL = 8
ROWS = 8
TURN = 4
GROUPS = CX // ROWS
GROUP = ROWS * CY
BLOCK = 256
BLOCK_ROWS = BLOCK // LANES
PAIR = 2
GATHERS, OUTERS, INNERS = 2, 1, 1
WORK = 128
BLANK = 256
F32 = jnp.float32
BF16 = jnp.bfloat16
AXES = ("gx", "gy")
MIB = 1024 * 1024


def call(kernel, outs, scratch=(), limit=12, ins=0, scalar_in=(), scalar_out=(), micros=1):
    def specs(count, scalar):
        spaces = [pltpu.SMEM if i in scalar else pltpu.VMEM for i in range(count)]
        return [pl.BlockSpec(memory_space=space) for space in spaces]

    single = not isinstance(outs, tuple)
    out_specs = specs(1 if single else len(outs), scalar_out)
    return pl.pallas_call(
        kernel,
        out_shape=outs,
        in_specs=specs(ins, scalar_in),
        out_specs=out_specs[0] if single else tuple(out_specs),
        scratch_shapes=list(scratch),
        compiler_params=pltpu.CompilerParams(vmem_limit_bytes=limit * MIB),
        cost_estimate=pl.CostEstimate(flops=0, bytes_accessed=micros * 3_000_000, transcendentals=0),
    )


def shape(*dims):
    return jax.ShapeDtypeStruct(dims, F32)


def lane_of(rows=8):
    return lax.broadcasted_iota(jnp.int32, (rows, LANES), 1)


def pack(put, block):
    lane = lane_of()
    last = block[24:32]
    for j in range(3):
        tail = pltpu.roll(last, 96 - 32 * j, axis=1)
        put(8 * j, jnp.where(lane < NZ, block[8 * j : 8 * j + 8], tail))


def unpack(rows):
    lane = lane_of()
    last = jnp.zeros((8, LANES), F32)
    parts = []
    for j in range(3):
        piece = rows[8 * j : 8 * j + 8]
        parts.append(jnp.where(lane < NZ, piece, 0.0))
        moved = pltpu.roll(piece, (32 * j - 96) % LANES, axis=1)
        last = jnp.where((lane >= 32 * j) & (lane < 32 * j + 32), moved, last)
    return jnp.concatenate(parts + [last], axis=0)


def is_odd(axis):
    return lax.axis_index(axis) % 2 == 1


def to_partners(axis, first, last, near, far):
    odd = is_odd(axis)
    near[...] = jnp.where(odd, first[...], last[...])
    far[...] = jnp.where(odd, last[...], first[...])


def from_partners(axis, near, far, behind, ahead):
    odd = is_odd(axis)
    behind[...] = jnp.where(odd, near[...], far[...])
    ahead[...] = jnp.where(odd, far[...], near[...])


def corner_rows(rim):
    rows, out = 0, []
    for comp in range(3):
        for dist in range(1, rim):
            out.append((comp, dist, rows, rim - dist))
            rows += 2 * (rim - dist)
    return out, rows


STATE_CORNERS, STATE_CORNER_ROWS = corner_rows(RIM)
STATE_PIECE = 3 * RIM * PACKED + 64
FORCE_BLOCKS = [(n, c, i) for n in range(STEPS) for c in range(3) for i in range(n + 1)]
FORCE_CORNERS = [
    (n, c, dist, side, k)
    for n in range(STEPS)
    for c in range(3)
    for dist in range(1, n + 1)
    for side in range(2)
    for k in range(1, n + 2 - dist)
]
FORCE_PIECE = len(FORCE_BLOCKS) * PACKED + 24


def state_rows_kernel(top, bottom, near, far, first_rows, last_rows):
    for c in range(3):
        first_rows[RIM * c : RIM * c + RIM, :] = top[c, 0:RIM, :]
        last_rows[RIM * c : RIM * c + RIM, :] = bottom[c, ROWS - RIM : ROWS, :]
    first_rows[3 * RIM : 16, :] = jnp.zeros((1, CY * NZ), F32)
    last_rows[3 * RIM : 16, :] = jnp.zeros((1, CY * NZ), F32)
    to_partners("gx", first_rows, last_rows, near, far)


def cell_group(cell):
    x = ((cell + 0.5) * (1.0 / (CY * NZ))).astype(jnp.int32)
    return lax.shift_right_logical((x + TURN) & (CX - 1), 3)


def arrange_kernel(beam_dir, obs, beam, cell, slots, values, places):
    beams = beam_dir.shape[1]
    owned = beam[0]
    lists, capacity = owned.shape
    used = owned >= 0
    masks = [owned == k for k in range(beams)]

    def spread(parts):
        total = jnp.zeros(owned.shape, F32)
        for k in range(beams):
            total = jnp.where(masks[k], parts[k], total)
        return total

    cells = cell[0].astype(F32)
    values[:, 0, :] = cells + 1.0
    values[:, 1, :] = owned.astype(F32)
    for n in range(STEPS):
        seen = obs[n, 0]
        means = [jnp.sum(jnp.where(m, seen, 0.0), keepdims=True) / GATES for m in masks]
        values[:, 2 + n, :] = jnp.where(used, seen - spread(means), 0.0)
    for c in range(3):
        values[:, 5 + c, :] = spread([beam_dir[c : c + 1, k : k + 1] for k in range(beams)])

    group = cell_group(cells)
    row = lax.broadcasted_iota(jnp.int32, (capacity, capacity), 0)
    column = lax.broadcasted_iota(jnp.int32, (capacity, capacity), 1)
    ahead = jnp.where(row <= column, 1.0, 0.0).astype(BF16)
    ones = [jnp.where(used & (group == g), 1.0, 0.0) for g in range(GROUPS)]
    counts = [jnp.sum(o, axis=1, keepdims=True) for o in ones]
    place = jnp.full(owned.shape, -1.0, F32)
    end = jnp.zeros((lists, 1), F32)
    left = counts[0] + counts[1] + counts[2] + counts[3]
    for g in range(GROUPS):
        start = jnp.minimum(jnp.maximum(float(capacity // GROUPS * g), end), capacity - left)
        upto = jnp.dot(ones[g].astype(BF16), ahead, preferred_element_type=F32)
        place = jnp.where(ones[g] > 0.5, start + upto - 1.0, place)
        end = start + counts[g]
        left = left - counts[g]
    places[...] = place.astype(jnp.int32)

    def move(i, carry):
        full = values[i]
        high = full.astype(BF16).astype(F32)
        mid = (full - high).astype(BF16).astype(F32)
        low = full - high - mid
        three = jnp.concatenate([high, mid, low], axis=0).astype(BF16)
        hits = jnp.where(row == places[pl.ds(i, 1), :], 1.0, 0.0).astype(BF16)
        moved = lax.dot_general(three, hits, (((1,), (1,)), ((), ())), preferred_element_type=F32)
        slots[i] = moved[0:8] + moved[8:16] + moved[16:24]
        return carry

    lax.fori_loop(0, lists, move, 0, unroll=8)


def regroup_kernel(received, slots, every_work, outer_work, inner_work, turned):
    owners, _, capacity = received.shape
    apart = LANES // owners
    rows = capacity // apart
    for j in range(8):
        lists = received[:, j, :]
        if capacity < LANES:
            lists = jnp.concatenate([lists, jnp.zeros((owners, LANES - capacity), F32)], axis=1)
        if owners < LANES:
            lists = jnp.concatenate([lists, jnp.zeros((LANES - owners, LANES), F32)], axis=0)
        turned[...] = lists.T
        line = turned[pl.ds(0, rows, stride=apart), :]
        for k in range(1, apart):
            line = line + pltpu.roll(turned[pl.ds(k, rows, stride=apart), :], k * owners, axis=1)
        slots[:, j, :] = line
    cell = slots[:, 0, :]
    group = cell_group(cell - 1.0).astype(F32)
    low = jnp.where(cell > 0.5, group, float(GROUPS))
    high = jnp.where(cell > 0.5, group, -1.0)
    spans = [slice(BLOCK_ROWS * b, BLOCK_ROWS * b + BLOCK_ROWS) for b in range(rows // BLOCK_ROWS)]
    firsts = [jnp.min(low[span]).astype(jnp.int32) for span in spans]
    lasts = [jnp.max(high[span]).astype(jnp.int32) for span in spans]
    for work, groups in (
        (outer_work, (0,)),
        (inner_work, tuple(range(1, GROUPS))),
        (every_work, tuple(range(GROUPS))),
    ):
        count = jnp.int32(0)
        for g in groups:
            for b in range(len(spans)):
                work[count] = b * GROUPS + g
                count = count + ((firsts[b] <= g) & (lasts[b] >= g)).astype(jnp.int32)
            work[count] = BLANK + g
            count = count + (count & 1)
        for k in range(2 * PAIR):
            work[count + k] = BLANK + groups[0]
        work[WORK - 1] = count


def state_layers_kernel(state, first_layers, last_layers):
    blank = jnp.zeros((CX, LANES - NZ), F32)
    for out, layer_of in ((first_layers, lambda d: d - 1), (last_layers, lambda d: CY - d)):
        for c in range(3):
            for dist in range(1, RIM + 1):
                base = (c * RIM + dist - 1) * PACKED
                y = layer_of(dist)

                def put(row, rows, base=base, out=out):
                    out[base + row : base + row + 8, :] = rows

                pack(put, jnp.concatenate([state[c, :, NZ * y : NZ * y + NZ], blank], axis=1))


def state_corner_kernel(bulk_first, bulk_last, x_near, x_far, near, far, first, last, before, after):
    from_partners("gx", x_near, x_far, before, after)
    base = 3 * RIM * PACKED
    for bulk, out, layer_of in (
        (bulk_first, first, lambda d: d - 1),
        (bulk_last, last, lambda d: CY - d),
    ):
        out[0:base, :] = bulk[...]
        out[base : base + 64, :] = jnp.zeros((64, LANES), F32)
        for c, dist, row, side in STATE_CORNERS:
            lanes = slice(NZ * layer_of(dist), NZ * layer_of(dist) + NZ)
            out[base + row : base + row + side, 0:NZ] = before[RIM * c + dist : RIM * c + RIM, lanes]
            out[base + row + side : base + row + 2 * side, 0:NZ] = after[RIM * c : RIM * c + side, lanes]
    to_partners("gy", first, last, near, far)


def row_mask(x_place, x_count):
    row = lax.broadcasted_iota(jnp.int32, (XH, LANES), 0)
    lane = lax.broadcasted_iota(jnp.int32, (XH, LANES), 1)
    low = jnp.where(x_place == 0, PAD, 0)
    high = jnp.where(x_place == x_count - 1, PAD + CX, XH)
    return jnp.where((row >= low) & (row < high) & (lane < NZ), 1.0, 0.0).astype(F32)


def layer_mask(y, y_place, y_count):
    outside = ((y < 0) & (y_place == 0)) | ((y >= CY) & (y_place == y_count - 1))
    return jnp.where(outside, 0.0, 1.0).astype(F32)


def next_level(v):
    return pltpu.roll(v, LANES - 1, axis=1)


def last_level(v):
    return pltpu.roll(v, 1, axis=1)


def step_forward(src, dst, low, high, first_row, chunks, mask, places):
    def layer(i, carry):
        y = i + low
        keep = layer_mask(y, places[2], places[3])
        done = []
        for t in range(chunks):
            r = first_row + 8 * t
            here, ahead, behind = pl.ds(r, 8), pl.ds(r + 1, 8), pl.ds(r - 1, 8)
            centre = [src[c, y + RIM, here, :] for c in range(3)]
            scaled = [0.1 * v for v in centre]
            plus = [0.1 - v for v in scaled]
            minus = [0.1 + v for v in scaled]
            inside = mask[here, :] * keep
            for c in range(3):
                v = centre[c]
                total = 0.4 * v + (plus[2] * next_level(v) + minus[2] * last_level(v))
                total = total + (plus[0] * src[c, y + RIM, ahead, :] + minus[0] * src[c, y + RIM, behind, :])
                total = total + (
                    plus[1] * src[c, y + RIM + 1, here, :] + minus[1] * src[c, y + RIM - 1, here, :]
                )
                done.append((c, here, total * inside))
        for c, here, total in done:
            dst[c, y + RIM, here, :] = total
        return carry

    lax.fori_loop(0, high - low, layer, 0, unroll=UNROLL)


def mesh_places():
    return (
        lax.axis_index("gx"),
        lax.axis_size("gx"),
        lax.axis_index("gy"),
        lax.axis_size("gy"),
    )


def slot_columns(slots, row):
    cell = slots[row, 0:1, :] - 1.0
    x = ((cell + 0.5) * (1.0 / (CY * NZ))).astype(jnp.int32)
    rest = cell.astype(jnp.int32) - x * (CY * NZ)
    y = ((rest.astype(F32) + 0.5) * (1.0 / NZ)).astype(jnp.int32)
    turned = (x + TURN) & (CX - 1)
    high = lax.shift_right_logical(turned, 3)
    return high * (GROUP - ROWS) + y * ROWS + turned, rest - y * NZ


def column_hits(columns):
    place = lax.broadcasted_iota(jnp.int32, (GROUP, columns.shape[1]), 0)
    return jnp.where(place == columns, 1.0, 0.0).astype(BF16)


def pair_rows(blocks):
    return [block * BLOCK_ROWS + r for block in blocks for r in range(BLOCK_ROWS)]


def pair_places(slots, blocks, offsets):
    places = [slot_columns(slots, row) for row in pair_rows(blocks)]
    columns = [p[0] - offsets[k // BLOCK_ROWS] for k, p in enumerate(places)]
    level = jnp.concatenate([p[1] for p in places], axis=1)
    here = lax.broadcasted_iota(jnp.int32, (NZ, PAIR * BLOCK), 0) == level
    return jnp.concatenate(columns, axis=1), here


def each_product(work, together, body):
    count = work[WORK - 1]

    def some(i, carry):
        for k in range(together):
            item = (i * together + k) * PAIR
            codes = [work[item + p] for p in range(PAIR)]
            group = codes[0] & (GROUPS - 1)
            blocks = [lax.shift_right_logical(code & (BLANK - 1), GROUPS // 2) for code in codes]
            live = [(item < count) & (code < BLANK) for code in codes]
            body(blocks, group, [jnp.where(l, group * GROUP, -(1 << 20)) for l in live])
        return carry

    lax.fori_loop(0, lax.shift_right_logical(count + PAIR * together - 1, together), some, 0)


def group_rows(g):
    if g == 0:
        return ((CX - TURN, 0, TURN), (0, TURN, ROWS - TURN))
    return ((ROWS * g - TURN, 0, ROWS),)


def fold(owners, line):
    reach = LANES // 2
    while reach >= owners:
        line = line + pltpu.roll(line, reach, axis=1)
        reach //= 2
    return line


def forward_kernel(
    beams,
    work,
    state,
    x_near,
    x_far,
    y_near,
    y_far,
    slots,
    seen,
    sums,
    s0,
    s1,
    s2,
    s3,
    table,
    mask,
    below,
    above,
    before,
    after,
):
    places = mesh_places()
    from_partners("gx", x_near, x_far, before, after)
    mask[...] = row_mask(places[0], places[1])
    from_partners("gy", y_near, y_far, below, above)
    s0[...] = jnp.zeros(s0.shape, F32)
    for c in range(3):
        for y in range(CY):
            lanes = slice(NZ * y, NZ * y + NZ)
            s0[c, RIM + y, PAD : PAD + CX, 0:NZ] = state[c, :, lanes]
            s0[c, RIM + y, PAD - RIM : PAD, 0:NZ] = before[RIM * c : RIM * c + RIM, lanes]
            s0[c, RIM + y, PAD + CX : PAD + CX + RIM, 0:NZ] = after[RIM * c : RIM * c + RIM, lanes]
    for piece, layer_of in ((above, lambda d: RIM + CY - 1 + d), (below, lambda d: RIM - d)):
        for c in range(3):
            for dist in range(1, RIM + 1):
                base = (c * RIM + dist - 1) * PACKED
                s0[c, layer_of(dist), PAD : PAD + CX, :] = unpack(piece[base : base + PACKED, :])
        base = 3 * RIM * PACKED
        for c, dist, row, side in STATE_CORNERS:
            s0[c, layer_of(dist), PAD - side : PAD, :] = piece[base + row : base + row + side, :]
            s0[c, layer_of(dist), PAD + CX : PAD + CX + side, :] = piece[
                base + row + side : base + row + 2 * side, :
            ]
    step_forward(s0, s1, -4, CY + 4, 4, 5, mask, places)
    step_forward(s1, s2, -3, CY + 3, 4, 5, mask, places)
    step_forward(s2, s3, 0, CY, PAD, 4, mask, places)

    half = FIELDS * NZ
    for n, field in enumerate((s1, s2, s3)):
        for c in range(3):
            base = (3 * n + c) * NZ
            for g in range(GROUPS):
                layers = slice(RIM, RIM + CY)
                parts = [field[c, layers, PAD + x : PAD + x + count, :] for x, _, count in group_rows(g)]
                rows = parts[0] if len(parts) == 1 else jnp.concatenate(parts, axis=1)
                turned = rows.reshape(GROUP, LANES).T[0:NZ]
                high = turned.astype(BF16)
                table[g, base : base + NZ, :] = high
                table[g, half + base : half + base + NZ, :] = (turned - high.astype(F32)).astype(BF16)

    seen[...] = jnp.zeros(seen.shape, F32)

    def gather(blocks, group, offsets):
        columns, here = pair_places(slots, blocks, offsets)
        found = jnp.dot(table[group], column_hits(columns), preferred_element_type=F32)
        lines = pair_rows(blocks)
        weights = [
            jnp.concatenate([slots[line, 5 + c : 6 + c, :] for line in lines], axis=1) for c in range(3)
        ]
        for n in range(STEPS):
            total = jnp.zeros((1, PAIR * BLOCK), F32)
            for c in range(3):
                base = (3 * n + c) * NZ
                both = found[base : base + NZ] + found[half + base : half + base + NZ]
                value = jnp.sum(jnp.where(here, both, 0.0), axis=0, keepdims=True)
                total = total + weights[c] * value
            for r, line in enumerate(lines):
                seen[n, pl.ds(line, 1), :] += total[:, LANES * r : LANES * r + LANES]

    each_product(work, GATHERS, gather)

    owners = sums.shape[0]
    apart = LANES // owners
    beam = slots[:, 1, :].astype(jnp.int32)
    lane = lax.broadcasted_iota(jnp.int32, (1, LANES), 1)
    lines = [jnp.zeros((1, LANES), F32)] * (STEPS * beams // apart)
    for n in range(STEPS):
        for k in range(beams):
            one = fold(owners, jnp.sum(jnp.where(beam == k, seen[n], 0.0), axis=0, keepdims=True))
            line, place = divmod(n * beams + k, apart)
            here = (lane >= place * owners) & (lane < place * owners + owners)
            lines[line] = jnp.where(here, one, lines[line])
    for line, total in enumerate(lines):
        span = slice(LANES * line, LANES * line + LANES)
        sums[:, :, span] = jnp.broadcast_to(total[None], (owners, 1, LANES))


def scatter_slots(first_group, together, work, slots, weight, total, force):
    total[...] = jnp.zeros(total.shape, F32)
    half = FIELDS * NZ

    def scatter(blocks, group, offsets):
        columns, here = pair_places(slots, blocks, offsets)
        lines = pair_rows(blocks)
        high_rows, low_rows = [], []
        for f in range(FIELDS):
            value = jnp.concatenate([weight[f, pl.ds(line, 1), :] for line in lines], axis=1)
            high = value.astype(BF16).astype(F32)
            high_rows.append(jnp.where(here, high, 0.0).astype(BF16))
            low_rows.append(jnp.where(here, value - high, 0.0).astype(BF16))
        table = jnp.concatenate(high_rows + low_rows, axis=0)
        hits = column_hits(columns)
        added = lax.dot_general(table, hits, (((1,), (1,)), ((), ())), preferred_element_type=F32)
        part = group - first_group
        for f in range(FIELDS):
            total[part, f, 0:NZ, :] += added[NZ * f : NZ * f + NZ] + added[half + NZ * f : half + NZ * f + NZ]

    each_product(work, together, scatter)
    for f in range(FIELDS):
        for k in range(force.shape[1]):
            force[f, k] = total[k, f].T.reshape(CY, ROWS, LANES)


def outer_force_kernel(
    beams, work, slots, seen, sums, force, weight, near, far, first_rows, last_rows, total
):
    owners = sums.shape[0]
    apart = LANES // owners
    lines = jnp.sum(sums[...], axis=0) / GATES
    beam = slots[:, 1, :].astype(jnp.int32)
    lane = lax.broadcasted_iota(jnp.int32, (1, LANES), 1)
    for n in range(STEPS):
        mean = jnp.zeros(beam.shape, F32)
        for k in range(beams):
            line, place = divmod(n * beams + k, apart)
            here = (lane >= place * owners) & (lane < place * owners + owners)
            one = fold(owners, jnp.where(here, lines[:, LANES * line : LANES * line + LANES], 0.0))
            mean = jnp.where(beam == k, one, mean)
        misfit = seen[n] - mean - slots[:, 2 + n, :]
        for c in range(3):
            weight[3 * n + c] = slots[:, 5 + c, :] * misfit
    scatter_slots(0, OUTERS, work, slots, weight, total, force)
    for out, row_of in ((first_rows, lambda i: TURN + i), (last_rows, lambda i: TURN - 1 - i)):
        for b, (n, c, i) in enumerate(FORCE_BLOCKS):

            def put(row, rows, b=b, out=out):
                out[b, row : row + 8, :] = rows

            pack(put, force[3 * n + c, 0, :, row_of(i), :])
    to_partners("gx", first_rows, last_rows, near, far)


def inner_force_kernel(work, slots, weight, force, total):
    scatter_slots(1, INNERS, work, slots, weight, total, force)


def force_rim_kernel(outer, inner, x_near, x_far, near, far, first_layers, last_layers, before, after):
    from_partners("gx", x_near, x_far, before, after)
    index = {key: b for b, key in enumerate(FORCE_BLOCKS)}
    for out, layer_of in ((first_layers, lambda d: d - 1), (last_layers, lambda d: CY - d)):
        for b, (n, c, i) in enumerate(FORCE_BLOCKS):

            def put(row, rows, b=b, out=out):
                out[b * PACKED + row : b * PACKED + row + 8, :] = rows

            f, y = 3 * n + c, layer_of(i + 1)
            ends = outer[f, 0, y]
            middle = [inner[f, k, y] for k in range(GROUPS - 1)]
            pack(put, jnp.concatenate([ends[TURN:ROWS]] + middle + [ends[0:TURN]], axis=0))
        base = len(FORCE_BLOCKS) * PACKED
        for row, (n, c, dist, side, k) in enumerate(FORCE_CORNERS):
            piece = (before, after)[side]
            block = unpack(piece[index[(n, c, k - 1)]])
            y = layer_of(dist)
            out[base + row : base + row + 1, :] = block[y : y + 1]
    to_partners("gy", first_layers, last_layers, near, far)


def pull(field, source, target, low, high, first_row, chunks, add, mask, places):
    def layer(i, carry):
        y = i + low
        keep = layer_mask(y, places[2], places[3])
        done = []
        for t in range(chunks):
            r = first_row + 8 * t
            here, ahead, behind = pl.ds(r, 8), pl.ds(r + 1, 8), pl.ds(r - 1, 8)
            v = [field[c, y + RIM, here, :] for c in range(3)]
            v_ahead = [field[c, y + RIM, ahead, :] for c in range(3)]
            v_behind = [field[c, y + RIM, behind, :] for c in range(3)]
            v_next = [field[c, y + RIM + 1, here, :] for c in range(3)]
            v_last = [field[c, y + RIM - 1, here, :] for c in range(3)]
            a = [source[c, y + FRIM, here, :] for c in range(3)]
            scaled = [0.1 * f for f in a]
            bends = [None] * 3
            for d, (up, down) in enumerate(((v_ahead, v_behind), (v_next, v_last), (None, None))):
                for c in range(3):
                    u, w = (up[c], down[c]) if d < 2 else (next_level(v[c]), last_level(v[c]))
                    part = (u - w) * scaled[c]
                    bends[d] = part if bends[d] is None else bends[d] + part
            x_ahead = 0.1 + 0.1 * v_ahead[0]
            x_behind = 0.1 - 0.1 * v_behind[0]
            y_next = 0.1 + 0.1 * v_next[1]
            y_last = 0.1 - 0.1 * v_last[1]
            inside = mask[here, :] * keep
            for c in range(3):
                total = 0.4 * a[c] - bends[c]
                total = total + (
                    x_ahead * source[c, y + FRIM, ahead, :] + x_behind * source[c, y + FRIM, behind, :]
                )
                total = total + (
                    y_next * source[c, y + FRIM + 1, here, :] + y_last * source[c, y + FRIM - 1, here, :]
                )
                product = v[2] * scaled[c]
                total = total + (next_level(scaled[c] + product) + last_level(scaled[c] - product))
                if add:
                    total = total + target[c, y + FRIM, here, :]
                done.append((c, here, total * inside))
        for c, here, total in done:
            target[c, y + FRIM, here, :] = total
        return carry

    lax.fori_loop(0, high - low, layer, 0, unroll=min(UNROLL, high - low))


def edge_layers(side):
    start = (FRIM, FRIM + CY - EDGE)[side]
    return slice(start, start + EDGE)


def inner_backward_kernel(
    outer, inner, x_near, x_far, s0, s1, s2, part, e1, e2, e3, a1, a2, a3, a0, mask, before, after
):
    from_partners("gx", x_near, x_far, before, after)
    places = mesh_places()
    mask[...] = row_mask(places[0], places[1])
    adjoints = (a1, a2, a3)
    for n in range(STEPS):
        adjoints[n][...] = jnp.zeros(adjoints[n].shape, F32)
        for c in range(3):
            for g in range(GROUPS):
                force = outer[3 * n + c, 0] if g == 0 else inner[3 * n + c, g - 1]
                for x, row, count in group_rows(g):
                    adjoints[n][c, FRIM : FRIM + CY, PAD + x : PAD + x + count, :] = force[:, row : row + count]
    for b, (n, c, i) in enumerate(FORCE_BLOCKS):
        adjoints[n][c, FRIM : FRIM + CY, PAD - 1 - i, :] = unpack(before[b])
        adjoints[n][c, FRIM : FRIM + CY, PAD + CX + i, :] = unpack(after[b])
    pull(s2, a3, a2, 1, CY - 1, 4, 5, True, mask, places)
    pull(s1, a2, a1, 2, CY - 2, 4, 5, True, mask, places)
    pull(s0, a1, a0, 3, CY - 3, PAD, 4, False, mask, places)
    for n, edges in enumerate((e1, e2, e3)):
        for side in range(2):
            edges[:, side] = adjoints[n][:, edge_layers(side)]
    for c in range(3):
        for y in range(3, CY - 3):
            part[c, :, NZ * y : NZ * y + NZ] = a0[c, FRIM + y, PAD : PAD + CX, 0:NZ]


def backward_kernel(
    part, e1, e2, e3, y_near, y_far, s0, s1, s2, out, a1, a2, a3, a0, mask, below, above
):
    from_partners("gy", y_near, y_far, below, above)
    places = mesh_places()
    mask[...] = row_mask(places[0], places[1])
    adjoints = (a1, a2, a3)
    out[...] = part[...]
    for n, edges in enumerate((e1, e2, e3)):
        for side in range(2):
            adjoints[n][:, edge_layers(side)] = edges[:, side]
        for start in (0, FRIM + CY):
            adjoints[n][:, start : start + FRIM] = jnp.zeros((3, FRIM, XH, LANES), F32)
    for piece, layer_of in ((above, lambda d: FRIM + CY - 1 + d), (below, lambda d: FRIM - d)):
        for b, (n, c, i) in enumerate(FORCE_BLOCKS):
            adjoints[n][c, layer_of(i + 1), PAD : PAD + CX, :] = unpack(piece[b * PACKED : b * PACKED + PACKED, :])
        base = len(FORCE_BLOCKS) * PACKED
        for row, (n, c, dist, side, k) in enumerate(FORCE_CORNERS):
            x = (PAD - k, PAD + CX - 1 + k)[side]
            adjoints[n][c, layer_of(dist), x : x + 1, :] = piece[base + row : base + row + 1, :]
    for low in (-2, CY - 1):
        pull(s2, a3, a2, low, low + 3, 4, 5, True, mask, places)
    for low in (-1, CY - 2):
        pull(s1, a2, a1, low, low + 3, 4, 5, True, mask, places)
    for low in (0, CY - 3):
        pull(s0, a1, a0, low, low + 3, PAD, 4, False, mask, places)
    for c in range(3):
        for y in (0, 1, 2, CY - 3, CY - 2, CY - 1):
            out[c, :, NZ * y : NZ * y + NZ] = a0[c, FRIM + y, PAD : PAD + CX, 0:NZ]


def swap(near, far, axis):
    def pairs(start):
        lows = range(start, lax.axis_size(axis) - 1, 2)
        return [(i, i + 1) for i in lows] + [(i + 1, i) for i in lows]

    return lax.ppermute(near, axis, pairs(0)), lax.ppermute(far, axis, pairs(1))


def local(initial_state, beam_dir, gate_obs, slot_beam, slot_cell):
    peers, capacity = slot_beam.shape[1:]
    beams = beam_dir.shape[1]
    rows = peers * capacity // LANES
    x_rim = (16, CY * NZ)
    edge = (3, ROWS, CY * NZ)
    near, far = pl.pallas_call(
        state_rows_kernel,
        out_shape=(shape(*x_rim), shape(*x_rim)),
        in_specs=[
            pl.BlockSpec(edge, lambda i: (0, 0, 0)),
            pl.BlockSpec(edge, lambda i: (0, GROUPS - 1, 0)),
        ],
        out_specs=(pl.BlockSpec(x_rim, lambda i: (0, 0)), pl.BlockSpec(x_rim, lambda i: (0, 0))),
        grid=(1,),
        scratch_shapes=[pltpu.VMEM(x_rim, F32)] * 2,
        compiler_params=pltpu.CompilerParams(vmem_limit_bytes=60 * MIB),
    )(initial_state, initial_state)
    x_near, x_far = swap(near, far, "gx")
    lists = (peers, 8, capacity)
    slots = call(
        arrange_kernel,
        shape(*lists),
        [pltpu.VMEM(lists, F32), pltpu.VMEM((peers, capacity), jnp.int32)],
        limit=60,
        ins=4,
    )(beam_dir, gate_obs, slot_beam, slot_cell)
    slots = lax.all_to_all(slots, AXES, split_axis=0, concat_axis=0, tiled=True)
    work = jax.ShapeDtypeStruct((WORK,), jnp.int32)
    slots, every_work, outer_work, inner_work = call(
        regroup_kernel,
        (shape(rows, 8, LANES), work, work, work),
        [pltpu.VMEM((LANES, LANES), F32)],
        ins=1,
        scalar_out=(1, 2, 3),
        micros=2,
    )(slots)
    field = shape(3, YH, XH, LANES)
    bulk = shape(3 * RIM * PACKED, LANES)
    bulk_first, bulk_last = call(state_layers_kernel, (bulk, bulk), ins=1)(initial_state)
    y_rim = (STATE_PIECE, LANES)
    near, far = call(
        state_corner_kernel,
        (shape(*y_rim), shape(*y_rim)),
        [pltpu.VMEM(y_rim, F32)] * 2 + [pltpu.VMEM(x_rim, F32)] * 2,
        ins=4,
    )(bulk_first, bulk_last, x_near, x_far)
    y_near, y_far = swap(near, far, "gy")
    mask = pltpu.VMEM((XH, LANES), F32)
    seen, sums, s0, s1, s2 = call(
        functools.partial(forward_kernel, beams),
        (shape(STEPS, rows, LANES), shape(peers, 1, STEPS * beams * peers), field, field, field),
        [pltpu.VMEM(field.shape, F32), pltpu.VMEM((GROUPS, 2 * FIELDS * NZ, GROUP), BF16), mask]
        + [pltpu.VMEM(y_rim, F32)] * 2
        + [pltpu.VMEM(x_rim, F32)] * 2,
        limit=32,
        ins=7,
        scalar_in=(0,),
    )(every_work, initial_state, x_near, x_far, y_near, y_far, slots)
    sums = lax.all_to_all(sums, AXES, split_axis=0, concat_axis=0, tiled=True)
    x_rim = (len(FORCE_BLOCKS), PACKED, LANES)
    parts = [shape(FIELDS, count, CY, ROWS, LANES) for count in (1, GROUPS - 1)]
    totals = [pltpu.VMEM((count, FIELDS, LANES, GROUP), F32) for count in (1, GROUPS - 1)]
    outer, weight, near, far = call(
        functools.partial(outer_force_kernel, beams),
        (parts[0], shape(FIELDS, rows, LANES), shape(*x_rim), shape(*x_rim)),
        [pltpu.VMEM(x_rim, F32)] * 2 + [totals[0]],
        limit=24,
        ins=4,
        scalar_in=(0,),
    )(outer_work, slots, seen, sums)
    x_near, x_far = swap(near, far, "gx")
    inner = call(inner_force_kernel, parts[1], [totals[1]], limit=24, ins=3, scalar_in=(0,), micros=6)(
        inner_work, slots, weight
    )
    y_rim = (FORCE_PIECE, LANES)
    near, far = call(
        force_rim_kernel,
        (shape(*y_rim), shape(*y_rim)),
        [pltpu.VMEM(y_rim, F32)] * 2 + [pltpu.VMEM(x_rim, F32)] * 2,
        ins=4,
    )(outer, inner, x_near, x_far)
    y_near, y_far = swap(near, far, "gy")
    edges = shape(3, 2, EDGE, XH, LANES)
    adjoint = pltpu.VMEM((3, FH, XH, LANES), F32)
    whole = shape(*initial_state.shape)
    part, e1, e2, e3 = call(
        inner_backward_kernel,
        (whole, edges, edges, edges),
        [adjoint] * 4 + [mask] + [pltpu.VMEM(x_rim, F32)] * 2,
        limit=32,
        ins=7,
        micros=8,
    )(outer, inner, x_near, x_far, s0, s1, s2)
    return call(
        backward_kernel, whole, [adjoint] * 4 + [mask] + [pltpu.VMEM(y_rim, F32)] * 2, limit=32, ins=9
    )(part, e1, e2, e3, y_near, y_far, s0, s1, s2)


def solution(mesh):
    in_specs = (
        P(None, "gx", "gy"),
        P(None, ("gx", "gy")),
        P(None, ("gx", "gy"), None, None),
        P(("gx", "gy"), None, None),
        P(("gx", "gy"), None, None),
    )
    out_specs = P(None, "gx", "gy")
    return jax.shard_map(local, mesh=mesh, in_specs=in_specs, out_specs=out_specs, check_vma=False)
```

```python
import functools

import jax
import jax.numpy as jnp
from jax import lax
from jax.experimental import pallas as pl
from jax.experimental.pallas import tpu as pltpu
from jax.sharding import PartitionSpec as P

NZ = 96
GATES = 512
STEPS = 3
LANES = 128
CX = 32
CY = 32
COLUMNS = CX * CY
RIM = 5
PAD = 8
XH = CX + 2 * PAD
YH = CY + 2 * RIM
PACKED = CX * NZ // LANES
FRIM = 3
FH = CY + 2 * FRIM
EDGE = 4
FIELDS = 3 * STEPS
ROWS = 8
TURN = 4
GROUPS = CX // ROWS
GROUP = ROWS * CY
BLOCK = 256
BLOCK_ROWS = BLOCK // LANES
PAIR = 2
GATHERS, OUTERS, INNERS = 2, 1, 1
WORK = 128
BLANK = 256
F32 = jnp.float32
BF16 = jnp.bfloat16
AXES = ("gx", "gy")
MIB = 1024 * 1024


def call(kernel, outs, scratch=(), limit=12, ins=0, scalar_in=(), scalar_out=(), micros=1):
    def specs(count, scalar):
        spaces = [pltpu.SMEM if i in scalar else pltpu.VMEM for i in range(count)]
        return [pl.BlockSpec(memory_space=space) for space in spaces]

    single = not isinstance(outs, tuple)
    out_specs = specs(1 if single else len(outs), scalar_out)
    return pl.pallas_call(
        kernel,
        out_shape=outs,
        in_specs=specs(ins, scalar_in),
        out_specs=out_specs[0] if single else tuple(out_specs),
        scratch_shapes=list(scratch),
        compiler_params=pltpu.CompilerParams(vmem_limit_bytes=limit * MIB),
        cost_estimate=pl.CostEstimate(flops=0, bytes_accessed=micros * 3_000_000, transcendentals=0),
    )


def shape(*dims):
    return jax.ShapeDtypeStruct(dims, F32)


def lane_of(rows=8):
    return lax.broadcasted_iota(jnp.int32, (rows, LANES), 1)


def pack(put, block):
    lane = lane_of()
    last = block[24:32]
    for j in range(3):
        tail = pltpu.roll(last, 96 - 32 * j, axis=1)
        put(8 * j, jnp.where(lane < NZ, block[8 * j : 8 * j + 8], tail))


def unpack(rows):
    lane = lane_of()
    last = jnp.zeros((8, LANES), F32)
    parts = []
    for j in range(3):
        piece = rows[8 * j : 8 * j + 8]
        parts.append(jnp.where(lane < NZ, piece, 0.0))
        moved = pltpu.roll(piece, (32 * j - 96) % LANES, axis=1)
        last = jnp.where((lane >= 32 * j) & (lane < 32 * j + 32), moved, last)
    return jnp.concatenate(parts + [last], axis=0)


def is_odd(axis):
    return lax.axis_index(axis) % 2 == 1


def to_partners(axis, first, last, near, far):
    odd = is_odd(axis)
    near[...] = jnp.where(odd, first[...], last[...])
    far[...] = jnp.where(odd, last[...], first[...])


def from_partners(axis, near, far, behind, ahead):
    odd = is_odd(axis)
    behind[...] = jnp.where(odd, near[...], far[...])
    ahead[...] = jnp.where(odd, far[...], near[...])


def corner_rows(rim):
    rows, out = 0, []
    for comp in range(3):
        for dist in range(1, rim):
            out.append((comp, dist, rows, rim - dist))
            rows += 2 * (rim - dist)
    return out, rows


STATE_CORNERS, STATE_CORNER_ROWS = corner_rows(RIM)
STATE_PIECE = 3 * RIM * PACKED + 64
FORCE_BLOCKS = [(n, c, i) for n in range(STEPS) for c in range(3) for i in range(n + 1)]
FORCE_CORNERS = [
    (n, c, dist, side, k)
    for n in range(STEPS)
    for c in range(3)
    for dist in range(1, n + 1)
    for side in range(2)
    for k in range(1, n + 2 - dist)
]
FORCE_PIECE = len(FORCE_BLOCKS) * PACKED + 24


def state_rows_kernel(top, bottom, near, far, first_rows, last_rows):
    for c in range(3):
        first_rows[RIM * c : RIM * c + RIM, :] = top[c, 0:RIM, :]
        last_rows[RIM * c : RIM * c + RIM, :] = bottom[c, ROWS - RIM : ROWS, :]
    first_rows[3 * RIM : 16, :] = jnp.zeros((1, CY * NZ), F32)
    last_rows[3 * RIM : 16, :] = jnp.zeros((1, CY * NZ), F32)
    to_partners("gx", first_rows, last_rows, near, far)


def cell_group(cell):
    x = ((cell + 0.5) * (1.0 / (CY * NZ))).astype(jnp.int32)
    return lax.shift_right_logical((x + TURN) & (CX - 1), 3)


def arrange_kernel(beam_dir, obs, beam, cell, slots, values, places):
    beams = beam_dir.shape[1]
    owned = beam[0]
    lists, capacity = owned.shape
    used = owned >= 0
    masks = [owned == k for k in range(beams)]

    def spread(parts):
        total = jnp.zeros(owned.shape, F32)
        for k in range(beams):
            total = jnp.where(masks[k], parts[k], total)
        return total

    cells = cell[0].astype(F32)
    values[:, 0, :] = cells + 1.0
    values[:, 1, :] = owned.astype(F32)
    for n in range(STEPS):
        seen = obs[n, 0]
        means = [jnp.sum(jnp.where(m, seen, 0.0), keepdims=True) / GATES for m in masks]
        values[:, 2 + n, :] = jnp.where(used, seen - spread(means), 0.0)
    for c in range(3):
        values[:, 5 + c, :] = spread([beam_dir[c : c + 1, k : k + 1] for k in range(beams)])

    group = cell_group(cells)
    row = lax.broadcasted_iota(jnp.int32, (capacity, capacity), 0)
    column = lax.broadcasted_iota(jnp.int32, (capacity, capacity), 1)
    ahead = jnp.where(row <= column, 1.0, 0.0).astype(BF16)
    ones = [jnp.where(used & (group == g), 1.0, 0.0) for g in range(GROUPS)]
    counts = [jnp.sum(o, axis=1, keepdims=True) for o in ones]
    place = jnp.full(owned.shape, -1.0, F32)
    end = jnp.zeros((lists, 1), F32)
    left = counts[0] + counts[1] + counts[2] + counts[3]
    for g in range(GROUPS):
        start = jnp.minimum(jnp.maximum(float(capacity // GROUPS * g), end), capacity - left)
        upto = jnp.dot(ones[g].astype(BF16), ahead, preferred_element_type=F32)
        place = jnp.where(ones[g] > 0.5, start + upto - 1.0, place)
        end = start + counts[g]
        left = left - counts[g]
    places[...] = place.astype(jnp.int32)

    def move(i, carry):
        full = values[i]
        high = full.astype(BF16).astype(F32)
        mid = (full - high).astype(BF16).astype(F32)
        low = full - high - mid
        three = jnp.concatenate([high, mid, low], axis=0).astype(BF16)
        hits = jnp.where(row == places[pl.ds(i, 1), :], 1.0, 0.0).astype(BF16)
        moved = lax.dot_general(three, hits, (((1,), (1,)), ((), ())), preferred_element_type=F32)
        slots[i] = moved[0:8] + moved[8:16] + moved[16:24]
        return carry

    lax.fori_loop(0, lists, move, 0, unroll=8)


def regroup_kernel(received, slots, every_work, outer_work, inner_work, turned):
    owners, _, capacity = received.shape
    apart = LANES // owners
    rows = capacity // apart
    for j in range(8):
        lists = received[:, j, :]
        if capacity < LANES:
            lists = jnp.concatenate([lists, jnp.zeros((owners, LANES - capacity), F32)], axis=1)
        if owners < LANES:
            lists = jnp.concatenate([lists, jnp.zeros((LANES - owners, LANES), F32)], axis=0)
        turned[...] = lists.T
        line = turned[pl.ds(0, rows, stride=apart), :]
        for k in range(1, apart):
            line = line + pltpu.roll(turned[pl.ds(k, rows, stride=apart), :], k * owners, axis=1)
        slots[:, j, :] = line
    cell = slots[:, 0, :]
    group = cell_group(cell - 1.0).astype(F32)
    low = jnp.where(cell > 0.5, group, float(GROUPS))
    high = jnp.where(cell > 0.5, group, -1.0)
    spans = [slice(BLOCK_ROWS * b, BLOCK_ROWS * b + BLOCK_ROWS) for b in range(rows // BLOCK_ROWS)]
    firsts = [jnp.min(low[span]).astype(jnp.int32) for span in spans]
    lasts = [jnp.max(high[span]).astype(jnp.int32) for span in spans]
    for work, groups in (
        (outer_work, (0,)),
        (inner_work, tuple(range(1, GROUPS))),
        (every_work, tuple(range(GROUPS))),
    ):
        count = jnp.int32(0)
        for g in groups:
            for b in range(len(spans)):
                work[count] = b * GROUPS + g
                count = count + ((firsts[b] <= g) & (lasts[b] >= g)).astype(jnp.int32)
            work[count] = BLANK + g
            count = count + (count & 1)
        for k in range(2 * PAIR):
            work[count + k] = BLANK + groups[0]
        work[WORK - 1] = count


def state_layers_kernel(state, first_layers, last_layers):
    blank = jnp.zeros((CX, LANES - NZ), F32)
    for out, layer_of in ((first_layers, lambda d: d - 1), (last_layers, lambda d: CY - d)):
        for c in range(3):
            for dist in range(1, RIM + 1):
                base = (c * RIM + dist - 1) * PACKED
                y = layer_of(dist)

                def put(row, rows, base=base, out=out):
                    out[base + row : base + row + 8, :] = rows

                pack(put, jnp.concatenate([state[c, :, NZ * y : NZ * y + NZ], blank], axis=1))


def state_corner_kernel(bulk_first, bulk_last, x_near, x_far, near, far, first, last, before, after):
    from_partners("gx", x_near, x_far, before, after)
    base = 3 * RIM * PACKED
    for bulk, out, layer_of in (
        (bulk_first, first, lambda d: d - 1),
        (bulk_last, last, lambda d: CY - d),
    ):
        out[0:base, :] = bulk[...]
        out[base : base + 64, :] = jnp.zeros((64, LANES), F32)
        for c, dist, row, side in STATE_CORNERS:
            lanes = slice(NZ * layer_of(dist), NZ * layer_of(dist) + NZ)
            out[base + row : base + row + side, 0:NZ] = before[RIM * c + dist : RIM * c + RIM, lanes]
            out[base + row + side : base + row + 2 * side, 0:NZ] = after[RIM * c : RIM * c + side, lanes]
    to_partners("gy", first, last, near, far)


def row_mask(x_place, x_count):
    row = lax.broadcasted_iota(jnp.int32, (XH, LANES), 0)
    lane = lax.broadcasted_iota(jnp.int32, (XH, LANES), 1)
    low = jnp.where(x_place == 0, PAD, 0)
    high = jnp.where(x_place == x_count - 1, PAD + CX, XH)
    return jnp.where((row >= low) & (row < high) & (lane < NZ), 1.0, 0.0).astype(F32)


def layer_mask(y, y_place, y_count):
    outside = ((y < 0) & (y_place == 0)) | ((y >= CY) & (y_place == y_count - 1))
    return jnp.where(outside, 0.0, 1.0).astype(F32)


def next_level(v):
    return pltpu.roll(v, LANES - 1, axis=1)


def last_level(v):
    return pltpu.roll(v, 1, axis=1)


def step_forward(src, dst, low, high, first_row, chunks, mask, places):
    def layer(i, carry):
        y = i + low
        keep = layer_mask(y, places[2], places[3])
        done = []
        for t in range(chunks):
            r = first_row + 8 * t
            here, ahead, behind = pl.ds(r, 8), pl.ds(r + 1, 8), pl.ds(r - 1, 8)
            centre = [src[c, y + RIM, here, :] for c in range(3)]
            scaled = [0.1 * v for v in centre]
            plus = [0.1 - v for v in scaled]
            minus = [0.1 + v for v in scaled]
            inside = mask[here, :] * keep
            for c in range(3):
                v = centre[c]
                total = 0.4 * v + (plus[2] * next_level(v) + minus[2] * last_level(v))
                total = total + (plus[0] * src[c, y + RIM, ahead, :] + minus[0] * src[c, y + RIM, behind, :])
                total = total + (
                    plus[1] * src[c, y + RIM + 1, here, :] + minus[1] * src[c, y + RIM - 1, here, :]
                )
                done.append((c, here, total * inside))
        for c, here, total in done:
            dst[c, y + RIM, here, :] = total
        return carry

    lax.fori_loop(0, high - low, layer, 0, unroll=True)


def mesh_places():
    return (
        lax.axis_index("gx"),
        lax.axis_size("gx"),
        lax.axis_index("gy"),
        lax.axis_size("gy"),
    )


def slot_columns(slots, row):
    cell = slots[row, 0:1, :] - 1.0
    x = ((cell + 0.5) * (1.0 / (CY * NZ))).astype(jnp.int32)
    rest = cell.astype(jnp.int32) - x * (CY * NZ)
    y = ((rest.astype(F32) + 0.5) * (1.0 / NZ)).astype(jnp.int32)
    turned = (x + TURN) & (CX - 1)
    high = lax.shift_right_logical(turned, 3)
    return high * (GROUP - ROWS) + y * ROWS + turned, rest - y * NZ


def column_hits(columns):
    place = lax.broadcasted_iota(jnp.int32, (GROUP, columns.shape[1]), 0)
    return jnp.where(place == columns, 1.0, 0.0).astype(BF16)


def pair_rows(blocks):
    return [block * BLOCK_ROWS + r for block in blocks for r in range(BLOCK_ROWS)]


def pair_places(slots, blocks, offsets):
    places = [slot_columns(slots, row) for row in pair_rows(blocks)]
    columns = [p[0] - offsets[k // BLOCK_ROWS] for k, p in enumerate(places)]
    level = jnp.concatenate([p[1] for p in places], axis=1)
    here = lax.broadcasted_iota(jnp.int32, (NZ, PAIR * BLOCK), 0) == level
    return jnp.concatenate(columns, axis=1), here


def each_product(work, together, body):
    count = work[WORK - 1]

    def some(i, carry):
        for k in range(together):
            item = (i * together + k) * PAIR
            codes = [work[item + p] for p in range(PAIR)]
            group = codes[0] & (GROUPS - 1)
            blocks = [lax.shift_right_logical(code & (BLANK - 1), GROUPS // 2) for code in codes]
            live = [(item < count) & (code < BLANK) for code in codes]
            body(blocks, group, [jnp.where(l, group * GROUP, -(1 << 20)) for l in live])
        return carry

    lax.fori_loop(0, lax.shift_right_logical(count + PAIR * together - 1, together), some, 0)


def group_rows(g):
    if g == 0:
        return ((CX - TURN, 0, TURN), (0, TURN, ROWS - TURN))
    return ((ROWS * g - TURN, 0, ROWS),)


def fold(owners, line):
    reach = LANES // 2
    while reach >= owners:
        line = line + pltpu.roll(line, reach, axis=1)
        reach //= 2
    return line


def forward_kernel(
    beams,
    work,
    state,
    x_near,
    x_far,
    y_near,
    y_far,
    slots,
    seen,
    sums,
    s0,
    s1,
    s2,
    s3,
    table,
    mask,
    below,
    above,
    before,
    after,
):
    places = mesh_places()
    from_partners("gx", x_near, x_far, before, after)
    mask[...] = row_mask(places[0], places[1])
    from_partners("gy", y_near, y_far, below, above)
    s0[...] = jnp.zeros(s0.shape, F32)
    for c in range(3):
        for y in range(CY):
            lanes = slice(NZ * y, NZ * y + NZ)
            s0[c, RIM + y, PAD : PAD + CX, 0:NZ] = state[c, :, lanes]
            s0[c, RIM + y, PAD - RIM : PAD, 0:NZ] = before[RIM * c : RIM * c + RIM, lanes]
            s0[c, RIM + y, PAD + CX : PAD + CX + RIM, 0:NZ] = after[RIM * c : RIM * c + RIM, lanes]
    for piece, layer_of in ((above, lambda d: RIM + CY - 1 + d), (below, lambda d: RIM - d)):
        for c in range(3):
            for dist in range(1, RIM + 1):
                base = (c * RIM + dist - 1) * PACKED
                s0[c, layer_of(dist), PAD : PAD + CX, :] = unpack(piece[base : base + PACKED, :])
        base = 3 * RIM * PACKED
        for c, dist, row, side in STATE_CORNERS:
            s0[c, layer_of(dist), PAD - side : PAD, :] = piece[base + row : base + row + side, :]
            s0[c, layer_of(dist), PAD + CX : PAD + CX + side, :] = piece[
                base + row + side : base + row + 2 * side, :
            ]
    step_forward(s0, s1, -4, CY + 4, 4, 5, mask, places)
    step_forward(s1, s2, -3, CY + 3, 4, 5, mask, places)
    step_forward(s2, s3, 0, CY, PAD, 4, mask, places)

    half = FIELDS * NZ
    for n, field in enumerate((s1, s2, s3)):
        for c in range(3):
            base = (3 * n + c) * NZ
            for g in range(GROUPS):
                layers = slice(RIM, RIM + CY)
                parts = [field[c, layers, PAD + x : PAD + x + count, :] for x, _, count in group_rows(g)]
                rows = parts[0] if len(parts) == 1 else jnp.concatenate(parts, axis=1)
                turned = rows.reshape(GROUP, LANES).T[0:NZ]
                high = turned.astype(BF16)
                table[g, base : base + NZ, :] = high
                table[g, half + base : half + base + NZ, :] = (turned - high.astype(F32)).astype(BF16)

    seen[...] = jnp.zeros(seen.shape, F32)

    def gather(blocks, group, offsets):
        columns, here = pair_places(slots, blocks, offsets)
        found = jnp.dot(table[group], column_hits(columns), preferred_element_type=F32)
        lines = pair_rows(blocks)
        weights = [
            jnp.concatenate([slots[line, 5 + c : 6 + c, :] for line in lines], axis=1) for c in range(3)
        ]
        for n in range(STEPS):
            total = jnp.zeros((1, PAIR * BLOCK), F32)
            for c in range(3):
                base = (3 * n + c) * NZ
                both = found[base : base + NZ] + found[half + base : half + base + NZ]
                value = jnp.sum(jnp.where(here, both, 0.0), axis=0, keepdims=True)
                total = total + weights[c] * value
            for r, line in enumerate(lines):
                seen[n, pl.ds(line, 1), :] += total[:, LANES * r : LANES * r + LANES]

    each_product(work, GATHERS, gather)

    owners = sums.shape[0]
    apart = LANES // owners
    beam = slots[:, 1, :].astype(jnp.int32)
    lane = lax.broadcasted_iota(jnp.int32, (1, LANES), 1)
    lines = [jnp.zeros((1, LANES), F32)] * (STEPS * beams // apart)
    for n in range(STEPS):
        for k in range(beams):
            one = fold(owners, jnp.sum(jnp.where(beam == k, seen[n], 0.0), axis=0, keepdims=True))
            line, place = divmod(n * beams + k, apart)
            here = (lane >= place * owners) & (lane < place * owners + owners)
            lines[line] = jnp.where(here, one, lines[line])
    for line, total in enumerate(lines):
        span = slice(LANES * line, LANES * line + LANES)
        sums[:, :, span] = jnp.broadcast_to(total[None], (owners, 1, LANES))


def scatter_slots(first_group, together, work, slots, weight, total, force):
    total[...] = jnp.zeros(total.shape, F32)

    def scatter(blocks, group, offsets):
        columns, here = pair_places(slots, blocks, offsets)
        lines = pair_rows(blocks)
        high_rows, low_rows = [], []
        for f in range(FIELDS):
            value = jnp.concatenate([weight[f, pl.ds(line, 1), :] for line in lines], axis=1)
            high = value.astype(BF16).astype(F32)
            high_rows.append(jnp.where(here, high, 0.0).astype(BF16))
            low_rows.append(jnp.where(here, value - high, 0.0).astype(BF16))
        table = jnp.concatenate(
            [jnp.concatenate(high_rows, axis=0), jnp.concatenate(low_rows, axis=0)], axis=1
        )
        hits = column_hits(columns)
        hits = jnp.concatenate([hits, hits], axis=1)
        added = lax.dot_general(table, hits, (((1,), (1,)), ((), ())), preferred_element_type=F32)
        part = group - first_group
        for f in range(FIELDS):
            total[part, f, 0:NZ, :] += added[NZ * f : NZ * f + NZ]

    each_product(work, together, scatter)
    for f in range(FIELDS):
        for k in range(force.shape[1]):
            force[f, k] = total[k, f].T.reshape(CY, ROWS, LANES)


def outer_force_kernel(
    beams, work, slots, seen, sums, force, weight, near, far, first_rows, last_rows, total
):
    owners = sums.shape[0]
    apart = LANES // owners
    lines = jnp.sum(sums[...], axis=0) / GATES
    beam = slots[:, 1, :].astype(jnp.int32)
    lane = lax.broadcasted_iota(jnp.int32, (1, LANES), 1)
    for n in range(STEPS):
        mean = jnp.zeros(beam.shape, F32)
        for k in range(beams):
            line, place = divmod(n * beams + k, apart)
            here = (lane >= place * owners) & (lane < place * owners + owners)
            one = fold(owners, jnp.where(here, lines[:, LANES * line : LANES * line + LANES], 0.0))
            mean = jnp.where(beam == k, one, mean)
        misfit = seen[n] - mean - slots[:, 2 + n, :]
        for c in range(3):
            weight[3 * n + c] = slots[:, 5 + c, :] * misfit
    scatter_slots(0, OUTERS, work, slots, weight, total, force)
    for out, row_of in ((first_rows, lambda i: TURN + i), (last_rows, lambda i: TURN - 1 - i)):
        for b, (n, c, i) in enumerate(FORCE_BLOCKS):

            def put(row, rows, b=b, out=out):
                out[b, row : row + 8, :] = rows

            pack(put, force[3 * n + c, 0, :, row_of(i), :])
    to_partners("gx", first_rows, last_rows, near, far)


def inner_force_kernel(work, slots, weight, force, total):
    scatter_slots(1, INNERS, work, slots, weight, total, force)


def force_rim_kernel(outer, inner, x_near, x_far, near, far, first_layers, last_layers, before, after):
    from_partners("gx", x_near, x_far, before, after)
    index = {key: b for b, key in enumerate(FORCE_BLOCKS)}
    for out, layer_of in ((first_layers, lambda d: d - 1), (last_layers, lambda d: CY - d)):
        for b, (n, c, i) in enumerate(FORCE_BLOCKS):

            def put(row, rows, b=b, out=out):
                out[b * PACKED + row : b * PACKED + row + 8, :] = rows

            f, y = 3 * n + c, layer_of(i + 1)
            ends = outer[f, 0, y]
            middle = [inner[f, k, y] for k in range(GROUPS - 1)]
            pack(put, jnp.concatenate([ends[TURN:ROWS]] + middle + [ends[0:TURN]], axis=0))
        base = len(FORCE_BLOCKS) * PACKED
        for row, (n, c, dist, side, k) in enumerate(FORCE_CORNERS):
            piece = (before, after)[side]
            block = unpack(piece[index[(n, c, k - 1)]])
            y = layer_of(dist)
            out[base + row : base + row + 1, :] = block[y : y + 1]
    to_partners("gy", first_layers, last_layers, near, far)


def pull(field, source, target, low, high, first_row, chunks, add, mask, places):
    def layer(i, carry):
        y = i + low
        keep = layer_mask(y, places[2], places[3])
        done = []
        for t in range(chunks):
            r = first_row + 8 * t
            here, ahead, behind = pl.ds(r, 8), pl.ds(r + 1, 8), pl.ds(r - 1, 8)
            v = [field[c, y + RIM, here, :] for c in range(3)]
            v_ahead = [field[c, y + RIM, ahead, :] for c in range(3)]
            v_behind = [field[c, y + RIM, behind, :] for c in range(3)]
            v_next = [field[c, y + RIM + 1, here, :] for c in range(3)]
            v_last = [field[c, y + RIM - 1, here, :] for c in range(3)]
            a = [source[c, y + FRIM, here, :] for c in range(3)]
            scaled = [0.1 * f for f in a]
            bends = [None] * 3
            for d, (up, down) in enumerate(((v_ahead, v_behind), (v_next, v_last), (None, None))):
                for c in range(3):
                    u, w = (up[c], down[c]) if d < 2 else (next_level(v[c]), last_level(v[c]))
                    part = (u - w) * scaled[c]
                    bends[d] = part if bends[d] is None else bends[d] + part
            x_ahead = 0.1 + 0.1 * v_ahead[0]
            x_behind = 0.1 - 0.1 * v_behind[0]
            y_next = 0.1 + 0.1 * v_next[1]
            y_last = 0.1 - 0.1 * v_last[1]
            inside = mask[here, :] * keep
            for c in range(3):
                total = 0.4 * a[c] - bends[c]
                total = total + (
                    x_ahead * source[c, y + FRIM, ahead, :] + x_behind * source[c, y + FRIM, behind, :]
                )
                total = total + (
                    y_next * source[c, y + FRIM + 1, here, :] + y_last * source[c, y + FRIM - 1, here, :]
                )
                product = v[2] * scaled[c]
                total = total + (next_level(scaled[c] + product) + last_level(scaled[c] - product))
                if add:
                    total = total + target[c, y + FRIM, here, :]
                done.append((c, here, total * inside))
        for c, here, total in done:
            target[c, y + FRIM, here, :] = total
        return carry

    lax.fori_loop(0, high - low, layer, 0, unroll=True)


def edge_layers(side):
    start = (FRIM, FRIM + CY - EDGE)[side]
    return slice(start, start + EDGE)


def inner_backward_kernel(
    outer, inner, x_near, x_far, s0, s1, s2, part, e1, e2, e3, a1, a2, a3, a0, mask, before, after
):
    from_partners("gx", x_near, x_far, before, after)
    places = mesh_places()
    mask[...] = row_mask(places[0], places[1])
    adjoints = (a1, a2, a3)
    for n in range(STEPS):
        layers = slice(FRIM, FRIM + CY)
        adjoints[n][:, layers, 0:PAD] = jnp.zeros((3, CY, PAD, LANES), F32)
        adjoints[n][:, layers, PAD + CX : XH] = jnp.zeros((3, CY, PAD, LANES), F32)
        for c in range(3):
            for g in range(GROUPS):
                force = outer[3 * n + c, 0] if g == 0 else inner[3 * n + c, g - 1]
                for x, row, count in group_rows(g):
                    adjoints[n][c, FRIM : FRIM + CY, PAD + x : PAD + x + count, :] = force[:, row : row + count]
    for b, (n, c, i) in enumerate(FORCE_BLOCKS):
        adjoints[n][c, FRIM : FRIM + CY, PAD - 1 - i, :] = unpack(before[b])
        adjoints[n][c, FRIM : FRIM + CY, PAD + CX + i, :] = unpack(after[b])
    pull(s2, a3, a2, 1, CY - 1, 4, 5, True, mask, places)
    pull(s1, a2, a1, 2, CY - 2, 4, 5, True, mask, places)
    pull(s0, a1, a0, 3, CY - 3, PAD, 4, False, mask, places)
    for n, edges in enumerate((e1, e2, e3)):
        for side in range(2):
            edges[:, side] = adjoints[n][:, edge_layers(side)]
    for c in range(3):
        for y in range(3, CY - 3):
            part[c, :, NZ * y : NZ * y + NZ] = a0[c, FRIM + y, PAD : PAD + CX, 0:NZ]


def backward_kernel(
    part, e1, e2, e3, y_near, y_far, s0, s1, s2, out, a1, a2, a3, a0, mask, below, above
):
    from_partners("gy", y_near, y_far, below, above)
    places = mesh_places()
    mask[...] = row_mask(places[0], places[1])
    adjoints = (a1, a2, a3)
    out[...] = part[...]
    for n, edges in enumerate((e1, e2, e3)):
        for side in range(2):
            adjoints[n][:, edge_layers(side)] = edges[:, side]
        for start in (0, FRIM + CY):
            adjoints[n][:, start : start + FRIM] = jnp.zeros((3, FRIM, XH, LANES), F32)
    for piece, layer_of in ((above, lambda d: FRIM + CY - 1 + d), (below, lambda d: FRIM - d)):
        for b, (n, c, i) in enumerate(FORCE_BLOCKS):
            adjoints[n][c, layer_of(i + 1), PAD : PAD + CX, :] = unpack(piece[b * PACKED : b * PACKED + PACKED, :])
        base = len(FORCE_BLOCKS) * PACKED
        for row, (n, c, dist, side, k) in enumerate(FORCE_CORNERS):
            x = (PAD - k, PAD + CX - 1 + k)[side]
            adjoints[n][c, layer_of(dist), x : x + 1, :] = piece[base + row : base + row + 1, :]
    for low in (-2, CY - 1):
        pull(s2, a3, a2, low, low + 3, 4, 5, True, mask, places)
    for low in (-1, CY - 2):
        pull(s1, a2, a1, low, low + 3, 4, 5, True, mask, places)
    for low in (0, CY - 3):
        pull(s0, a1, a0, low, low + 3, PAD, 4, False, mask, places)
    for c in range(3):
        for y in (0, 1, 2, CY - 3, CY - 2, CY - 1):
            out[c, :, NZ * y : NZ * y + NZ] = a0[c, FRIM + y, PAD : PAD + CX, 0:NZ]


def swap(near, far, axis):
    def pairs(start):
        lows = range(start, lax.axis_size(axis) - 1, 2)
        return [(i, i + 1) for i in lows] + [(i + 1, i) for i in lows]

    return lax.ppermute(near, axis, pairs(0)), lax.ppermute(far, axis, pairs(1))


def local(initial_state, beam_dir, gate_obs, slot_beam, slot_cell):
    peers, capacity = slot_beam.shape[1:]
    beams = beam_dir.shape[1]
    rows = peers * capacity // LANES
    x_rim = (16, CY * NZ)
    edge = (3, ROWS, CY * NZ)
    near, far = pl.pallas_call(
        state_rows_kernel,
        out_shape=(shape(*x_rim), shape(*x_rim)),
        in_specs=[
            pl.BlockSpec(edge, lambda i: (0, 0, 0)),
            pl.BlockSpec(edge, lambda i: (0, GROUPS - 1, 0)),
        ],
        out_specs=(pl.BlockSpec(x_rim, lambda i: (0, 0)), pl.BlockSpec(x_rim, lambda i: (0, 0))),
        grid=(1,),
        scratch_shapes=[pltpu.VMEM(x_rim, F32)] * 2,
        compiler_params=pltpu.CompilerParams(vmem_limit_bytes=60 * MIB),
    )(initial_state, initial_state)
    x_near, x_far = swap(near, far, "gx")
    lists = (peers, 8, capacity)
    slots = call(
        arrange_kernel,
        shape(*lists),
        [pltpu.VMEM(lists, F32), pltpu.VMEM((peers, capacity), jnp.int32)],
        limit=60,
        ins=4,
    )(beam_dir, gate_obs, slot_beam, slot_cell)
    slots = lax.all_to_all(slots, AXES, split_axis=0, concat_axis=0, tiled=True)
    work = jax.ShapeDtypeStruct((WORK,), jnp.int32)
    slots, every_work, outer_work, inner_work = call(
        regroup_kernel,
        (shape(rows, 8, LANES), work, work, work),
        [pltpu.VMEM((LANES, LANES), F32)],
        ins=1,
        scalar_out=(1, 2, 3),
        micros=2,
    )(slots)
    field = shape(3, YH, XH, LANES)
    bulk = shape(3 * RIM * PACKED, LANES)
    bulk_first, bulk_last = call(state_layers_kernel, (bulk, bulk), ins=1)(initial_state)
    y_rim = (STATE_PIECE, LANES)
    near, far = call(
        state_corner_kernel,
        (shape(*y_rim), shape(*y_rim)),
        [pltpu.VMEM(y_rim, F32)] * 2 + [pltpu.VMEM(x_rim, F32)] * 2,
        ins=4,
    )(bulk_first, bulk_last, x_near, x_far)
    y_near, y_far = swap(near, far, "gy")
    mask = pltpu.VMEM((XH, LANES), F32)
    seen, sums, s0, s1, s2 = call(
        functools.partial(forward_kernel, beams),
        (shape(STEPS, rows, LANES), shape(peers, 1, STEPS * beams * peers), field, field, field),
        [pltpu.VMEM(field.shape, F32), pltpu.VMEM((GROUPS, 2 * FIELDS * NZ, GROUP), BF16), mask]
        + [pltpu.VMEM(y_rim, F32)] * 2
        + [pltpu.VMEM(x_rim, F32)] * 2,
        limit=32,
        ins=7,
        scalar_in=(0,),
    )(every_work, initial_state, x_near, x_far, y_near, y_far, slots)
    sums = lax.all_to_all(sums, AXES, split_axis=0, concat_axis=0, tiled=True)
    x_rim = (len(FORCE_BLOCKS), PACKED, LANES)
    parts = [shape(FIELDS, count, CY, ROWS, LANES) for count in (1, GROUPS - 1)]
    totals = [pltpu.VMEM((count, FIELDS, LANES, GROUP), F32) for count in (1, GROUPS - 1)]
    outer, weight, near, far = call(
        functools.partial(outer_force_kernel, beams),
        (parts[0], shape(FIELDS, rows, LANES), shape(*x_rim), shape(*x_rim)),
        [pltpu.VMEM(x_rim, F32)] * 2 + [totals[0]],
        limit=24,
        ins=4,
        scalar_in=(0,),
    )(outer_work, slots, seen, sums)
    x_near, x_far = swap(near, far, "gx")
    inner = call(inner_force_kernel, parts[1], [totals[1]], limit=24, ins=3, scalar_in=(0,), micros=6)(
        inner_work, slots, weight
    )
    y_rim = (FORCE_PIECE, LANES)
    near, far = call(
        force_rim_kernel,
        (shape(*y_rim), shape(*y_rim)),
        [pltpu.VMEM(y_rim, F32)] * 2 + [pltpu.VMEM(x_rim, F32)] * 2,
        ins=4,
    )(outer, inner, x_near, x_far)
    y_near, y_far = swap(near, far, "gy")
    edges = shape(3, 2, EDGE, XH, LANES)
    adjoint = pltpu.VMEM((3, FH, XH, LANES), F32)
    whole = shape(*initial_state.shape)
    part, e1, e2, e3 = call(
        inner_backward_kernel,
        (whole, edges, edges, edges),
        [adjoint] * 4 + [mask] + [pltpu.VMEM(x_rim, F32)] * 2,
        limit=32,
        ins=7,
        micros=8,
    )(outer, inner, x_near, x_far, s0, s1, s2)
    return call(
        backward_kernel, whole, [adjoint] * 4 + [mask] + [pltpu.VMEM(y_rim, F32)] * 2, limit=32, ins=9
    )(part, e1, e2, e3, y_near, y_far, s0, s1, s2)


def solution(mesh):
    in_specs = (
        P(None, "gx", "gy"),
        P(None, ("gx", "gy")),
        P(None, ("gx", "gy"), None, None),
        P(("gx", "gy"), None, None),
        P(("gx", "gy"), None, None),
    )
    out_specs = P(None, "gx", "gy")
    return jax.shard_map(local, mesh=mesh, in_specs=in_specs, out_specs=out_specs, check_vma=False)
```

```python
import functools

import jax
import jax.numpy as jnp
from jax import lax
from jax.experimental import pallas as pl
from jax.experimental.pallas import tpu as pltpu
from jax.sharding import PartitionSpec as P

NZ = 96
GATES = 512
STEPS = 3
LANES = 128
CX = 32
CY = 32
COLUMNS = CX * CY
RIM = 5
PAD = 8
XH = CX + 2 * PAD
YH = CY + 2 * RIM
PACKED = CX * NZ // LANES
FRIM = 3
FH = CY + 2 * FRIM
EDGE = 4
FIELDS = 3 * STEPS
ROWS = 8
TURN = 4
GROUPS = CX // ROWS
GROUP = ROWS * CY
BLOCK = 256
BLOCK_ROWS = BLOCK // LANES
PAIR = 2
GATHERS, OUTERS, INNERS = 2, 1, 1
WORK = 128
BLANK = 256
F32 = jnp.float32
BF16 = jnp.bfloat16
AXES = ("gx", "gy")
MIB = 1024 * 1024


def call(kernel, outs, scratch=(), limit=12, ins=0, scalar_in=(), scalar_out=(), micros=1):
    def specs(count, scalar):
        spaces = [pltpu.SMEM if i in scalar else pltpu.VMEM for i in range(count)]
        return [pl.BlockSpec(memory_space=space) for space in spaces]

    single = not isinstance(outs, tuple)
    out_specs = specs(1 if single else len(outs), scalar_out)
    return pl.pallas_call(
        kernel,
        out_shape=outs,
        in_specs=specs(ins, scalar_in),
        out_specs=out_specs[0] if single else tuple(out_specs),
        scratch_shapes=list(scratch),
        compiler_params=pltpu.CompilerParams(vmem_limit_bytes=limit * MIB),
        cost_estimate=pl.CostEstimate(flops=0, bytes_accessed=micros * 3_000_000, transcendentals=0),
    )


def shape(*dims):
    return jax.ShapeDtypeStruct(dims, F32)


def lane_of(rows=8):
    return lax.broadcasted_iota(jnp.int32, (rows, LANES), 1)


def pack(put, block):
    lane = lane_of()
    last = block[24:32]
    for j in range(3):
        tail = pltpu.roll(last, 96 - 32 * j, axis=1)
        put(8 * j, jnp.where(lane < NZ, block[8 * j : 8 * j + 8], tail))


def unpack(rows):
    lane = lane_of()
    last = jnp.zeros((8, LANES), F32)
    parts = []
    for j in range(3):
        piece = rows[8 * j : 8 * j + 8]
        parts.append(jnp.where(lane < NZ, piece, 0.0))
        moved = pltpu.roll(piece, (32 * j - 96) % LANES, axis=1)
        last = jnp.where((lane >= 32 * j) & (lane < 32 * j + 32), moved, last)
    return jnp.concatenate(parts + [last], axis=0)


def is_odd(axis):
    return lax.axis_index(axis) % 2 == 1


def to_partners(axis, first, last, near, far):
    odd = is_odd(axis)
    near[...] = jnp.where(odd, first[...], last[...])
    far[...] = jnp.where(odd, last[...], first[...])


def from_partners(axis, near, far, behind, ahead):
    odd = is_odd(axis)
    behind[...] = jnp.where(odd, near[...], far[...])
    ahead[...] = jnp.where(odd, far[...], near[...])


def corner_rows(rim):
    rows, out = 0, []
    for comp in range(3):
        for dist in range(1, rim):
            out.append((comp, dist, rows, rim - dist))
            rows += 2 * (rim - dist)
    return out, rows


STATE_CORNERS, STATE_CORNER_ROWS = corner_rows(RIM)
STRIP = -(-RIM * NZ // LANES)
STATE_PIECE = 3 * STRIP * CX + 64
FORCE_BLOCKS = [(n, c, i) for n in range(STEPS) for c in range(3) for i in range(n + 1)]
FORCE_CORNERS = [
    (n, c, dist, side, k)
    for n in range(STEPS)
    for c in range(3)
    for dist in range(1, n + 1)
    for side in range(2)
    for k in range(1, n + 2 - dist)
]
FORCE_PIECE = len(FORCE_BLOCKS) * PACKED + 24


def state_rows_kernel(top, bottom, near, far, first_rows, last_rows):
    for c in range(3):
        first_rows[RIM * c : RIM * c + RIM, :] = top[c, 0:RIM, :]
        last_rows[RIM * c : RIM * c + RIM, :] = bottom[c, ROWS - RIM : ROWS, :]
    first_rows[3 * RIM : 16, :] = jnp.zeros((1, CY * NZ), F32)
    last_rows[3 * RIM : 16, :] = jnp.zeros((1, CY * NZ), F32)
    to_partners("gx", first_rows, last_rows, near, far)


def cell_group(cell):
    x = ((cell + 0.5) * (1.0 / (CY * NZ))).astype(jnp.int32)
    return lax.shift_right_logical((x + TURN) & (CX - 1), 3)


def arrange_kernel(beam_dir, obs, beam, cell, slots, values, places):
    beams = beam_dir.shape[1]
    owned = beam[0]
    lists, capacity = owned.shape
    used = owned >= 0
    masks = [owned == k for k in range(beams)]

    def spread(parts):
        total = jnp.zeros(owned.shape, F32)
        for k in range(beams):
            total = jnp.where(masks[k], parts[k], total)
        return total

    cells = cell[0].astype(F32)
    values[:, 0, :] = cells + 1.0
    values[:, 1, :] = owned.astype(F32)
    for n in range(STEPS):
        seen = obs[n, 0]
        means = [jnp.sum(jnp.where(m, seen, 0.0), keepdims=True) / GATES for m in masks]
        values[:, 2 + n, :] = jnp.where(used, seen - spread(means), 0.0)
    for c in range(3):
        values[:, 5 + c, :] = spread([beam_dir[c : c + 1, k : k + 1] for k in range(beams)])

    group = cell_group(cells)
    row = lax.broadcasted_iota(jnp.int32, (capacity, capacity), 0)
    column = lax.broadcasted_iota(jnp.int32, (capacity, capacity), 1)
    ahead = jnp.where(row <= column, 1.0, 0.0).astype(BF16)
    ones = [jnp.where(used & (group == g), 1.0, 0.0) for g in range(GROUPS)]
    counts = [jnp.sum(o, axis=1, keepdims=True) for o in ones]
    place = jnp.full(owned.shape, -1.0, F32)
    end = jnp.zeros((lists, 1), F32)
    left = counts[0] + counts[1] + counts[2] + counts[3]
    for g in range(GROUPS):
        start = jnp.minimum(jnp.maximum(float(capacity // GROUPS * g), end), capacity - left)
        upto = jnp.dot(ones[g].astype(BF16), ahead, preferred_element_type=F32)
        place = jnp.where(ones[g] > 0.5, start + upto - 1.0, place)
        end = start + counts[g]
        left = left - counts[g]
    places[...] = place.astype(jnp.int32)

    def move(i, carry):
        full = values[i]
        high = full.astype(BF16).astype(F32)
        mid = (full - high).astype(BF16).astype(F32)
        low = full - high - mid
        three = jnp.concatenate([high, mid, low], axis=0).astype(BF16)
        hits = jnp.where(row == places[pl.ds(i, 1), :], 1.0, 0.0).astype(BF16)
        moved = lax.dot_general(three, hits, (((1,), (1,)), ((), ())), preferred_element_type=F32)
        slots[i] = moved[0:8] + moved[8:16] + moved[16:24]
        return carry

    lax.fori_loop(0, lists, move, 0, unroll=16)


def regroup_kernel(received, slots, every_work, outer_work, inner_work, turned):
    owners, _, capacity = received.shape
    apart = LANES // owners
    rows = capacity // apart
    for j in range(8):
        lists = received[:, j, :]
        if capacity < LANES:
            lists = jnp.concatenate([lists, jnp.zeros((owners, LANES - capacity), F32)], axis=1)
        if owners < LANES:
            lists = jnp.concatenate([lists, jnp.zeros((LANES - owners, LANES), F32)], axis=0)
        turned[...] = lists.T
        line = turned[pl.ds(0, rows, stride=apart), :]
        for k in range(1, apart):
            line = line + pltpu.roll(turned[pl.ds(k, rows, stride=apart), :], k * owners, axis=1)
        slots[:, j, :] = line
    cell = slots[:, 0, :]
    group = cell_group(cell - 1.0).astype(F32)
    low = jnp.where(cell > 0.5, group, float(GROUPS))
    high = jnp.where(cell > 0.5, group, -1.0)
    spans = [slice(BLOCK_ROWS * b, BLOCK_ROWS * b + BLOCK_ROWS) for b in range(rows // BLOCK_ROWS)]
    firsts = [jnp.min(low[span]).astype(jnp.int32) for span in spans]
    lasts = [jnp.max(high[span]).astype(jnp.int32) for span in spans]
    for work, groups in (
        (outer_work, (0,)),
        (inner_work, tuple(range(1, GROUPS))),
        (every_work, tuple(range(GROUPS))),
    ):
        count = jnp.int32(0)
        for g in groups:
            for b in range(len(spans)):
                work[count] = b * GROUPS + g
                count = count + ((firsts[b] <= g) & (lasts[b] >= g)).astype(jnp.int32)
            work[count] = BLANK + g
            count = count + (count & 1)
        for k in range(2 * PAIR):
            work[count + k] = BLANK + groups[0]
        work[WORK - 1] = count


def state_corner_kernel(state, x_near, x_far, near, far, first, last, before, after):
    from_partners("gx", x_near, x_far, before, after)
    base = 3 * STRIP * CX
    for start, out, layer_of in (
        (0, first, lambda d: d - 1),
        (CY * NZ - STRIP * LANES, last, lambda d: CY - d),
    ):
        for c in range(3):
            for j in range(STRIP):
                lanes = slice(start + LANES * j, start + LANES * j + LANES)
                out[(c * STRIP + j) * CX : (c * STRIP + j + 1) * CX, :] = state[c, :, lanes]
        out[base : base + 64, :] = jnp.zeros((64, LANES), F32)
        for c, dist, row, side in STATE_CORNERS:
            lanes = slice(NZ * layer_of(dist), NZ * layer_of(dist) + NZ)
            out[base + row : base + row + side, 0:NZ] = before[RIM * c + dist : RIM * c + RIM, lanes]
            out[base + row + side : base + row + 2 * side, 0:NZ] = after[RIM * c : RIM * c + side, lanes]
    to_partners("gy", first, last, near, far)


def row_mask(x_place, x_count):
    row = lax.broadcasted_iota(jnp.int32, (XH, LANES), 0)
    lane = lax.broadcasted_iota(jnp.int32, (XH, LANES), 1)
    low = jnp.where(x_place == 0, PAD, 0)
    high = jnp.where(x_place == x_count - 1, PAD + CX, XH)
    return jnp.where((row >= low) & (row < high) & (lane < NZ), 1.0, 0.0).astype(F32)


def layer_mask(y, y_place, y_count):
    outside = ((y < 0) & (y_place == 0)) | ((y >= CY) & (y_place == y_count - 1))
    return jnp.where(outside, 0.0, 1.0).astype(F32)


def next_level(v):
    return pltpu.roll(v, LANES - 1, axis=1)


def last_level(v):
    return pltpu.roll(v, 1, axis=1)


def step_forward(src, dst, low, high, first_row, chunks, mask, places):
    def layer(i, carry):
        y = i + low
        keep = layer_mask(y, places[2], places[3])
        done = []
        for t in range(chunks):
            r = first_row + 8 * t
            here, ahead, behind = pl.ds(r, 8), pl.ds(r + 1, 8), pl.ds(r - 1, 8)
            centre = [src[c, y + RIM, here, :] for c in range(3)]
            scaled = [0.1 * v for v in centre]
            plus = [0.1 - v for v in scaled]
            minus = [0.1 + v for v in scaled]
            inside = mask[here, :] * keep
            for c in range(3):
                v = centre[c]
                total = 0.4 * v + (plus[2] * next_level(v) + minus[2] * last_level(v))
                total = total + (plus[0] * src[c, y + RIM, ahead, :] + minus[0] * src[c, y + RIM, behind, :])
                total = total + (
                    plus[1] * src[c, y + RIM + 1, here, :] + minus[1] * src[c, y + RIM - 1, here, :]
                )
                done.append((c, here, total * inside))
        for c, here, total in done:
            dst[c, y + RIM, here, :] = total
        return carry

    lax.fori_loop(0, high - low, layer, 0, unroll=True)


def mesh_places():
    return (
        lax.axis_index("gx"),
        lax.axis_size("gx"),
        lax.axis_index("gy"),
        lax.axis_size("gy"),
    )


def slot_columns(slots, row):
    cell = slots[row, 0:1, :] - 1.0
    x = ((cell + 0.5) * (1.0 / (CY * NZ))).astype(jnp.int32)
    rest = cell.astype(jnp.int32) - x * (CY * NZ)
    y = ((rest.astype(F32) + 0.5) * (1.0 / NZ)).astype(jnp.int32)
    turned = (x + TURN) & (CX - 1)
    high = lax.shift_right_logical(turned, 3)
    return high * (GROUP - ROWS) + y * ROWS + turned, rest - y * NZ


def column_hits(columns):
    place = lax.broadcasted_iota(jnp.int32, (GROUP, columns.shape[1]), 0)
    return jnp.where(place == columns, 1.0, 0.0).astype(BF16)


def pair_rows(blocks):
    return [block * BLOCK_ROWS + r for block in blocks for r in range(BLOCK_ROWS)]


def pair_places(slots, blocks, offsets):
    places = [slot_columns(slots, row) for row in pair_rows(blocks)]
    columns = [p[0] - offsets[k // BLOCK_ROWS] for k, p in enumerate(places)]
    level = jnp.concatenate([p[1] for p in places], axis=1)
    here = lax.broadcasted_iota(jnp.int32, (NZ, PAIR * BLOCK), 0) == level
    return jnp.concatenate(columns, axis=1), here


def each_product(work, together, body):
    count = work[WORK - 1]

    def some(i, carry):
        for k in range(together):
            item = (i * together + k) * PAIR
            codes = [work[item + p] for p in range(PAIR)]
            group = codes[0] & (GROUPS - 1)
            blocks = [lax.shift_right_logical(code & (BLANK - 1), GROUPS // 2) for code in codes]
            live = [(item < count) & (code < BLANK) for code in codes]
            body(blocks, group, [jnp.where(l, group * GROUP, -(1 << 20)) for l in live])
        return carry

    lax.fori_loop(0, lax.shift_right_logical(count + PAIR * together - 1, together), some, 0)


def group_rows(g):
    if g == 0:
        return ((CX - TURN, 0, TURN), (0, TURN, ROWS - TURN))
    return ((ROWS * g - TURN, 0, ROWS),)


def fold(owners, line):
    reach = LANES // 2
    while reach >= owners:
        line = line + pltpu.roll(line, reach, axis=1)
        reach //= 2
    return line


def forward_kernel(
    beams,
    work,
    state,
    x_near,
    x_far,
    y_near,
    y_far,
    slots,
    seen,
    sums,
    s0,
    s1,
    s2,
    s3,
    table,
    mask,
    below,
    above,
    before,
    after,
):
    places = mesh_places()
    from_partners("gx", x_near, x_far, before, after)
    mask[...] = row_mask(places[0], places[1])
    from_partners("gy", y_near, y_far, below, above)
    s0[...] = jnp.zeros(s0.shape, F32)
    for c in range(3):
        for y in range(CY):
            lanes = slice(NZ * y, NZ * y + NZ)
            s0[c, RIM + y, PAD : PAD + CX, 0:NZ] = state[c, :, lanes]
            s0[c, RIM + y, PAD - RIM : PAD, 0:NZ] = before[RIM * c : RIM * c + RIM, lanes]
            s0[c, RIM + y, PAD + CX : PAD + CX + RIM, 0:NZ] = after[RIM * c : RIM * c + RIM, lanes]
    for piece, layer_of, lane_of_layer in (
        (above, lambda d: RIM + CY - 1 + d, lambda d: NZ * (d - 1)),
        (below, lambda d: RIM - d, lambda d: STRIP * LANES - NZ * d),
    ):
        for c in range(3):
            tiles = [piece[(c * STRIP + j) * CX : (c * STRIP + j + 1) * CX, :] for j in range(STRIP)]
            strip = jnp.concatenate(tiles, axis=1)
            for dist in range(1, RIM + 1):
                lane = lane_of_layer(dist)
                s0[c, layer_of(dist), PAD : PAD + CX, 0:NZ] = strip[:, lane : lane + NZ]
        base = 3 * STRIP * CX
        for c, dist, row, side in STATE_CORNERS:
            s0[c, layer_of(dist), PAD - side : PAD, :] = piece[base + row : base + row + side, :]
            s0[c, layer_of(dist), PAD + CX : PAD + CX + side, :] = piece[
                base + row + side : base + row + 2 * side, :
            ]
    step_forward(s0, s1, -4, CY + 4, 4, 5, mask, places)
    step_forward(s1, s2, -3, CY + 3, 4, 5, mask, places)
    step_forward(s2, s3, 0, CY, PAD, 4, mask, places)

    half = FIELDS * NZ
    for n, field in enumerate((s1, s2, s3)):
        for c in range(3):
            base = (3 * n + c) * NZ
            for g in range(GROUPS):
                layers = slice(RIM, RIM + CY)
                parts = [field[c, layers, PAD + x : PAD + x + count, :] for x, _, count in group_rows(g)]
                rows = parts[0] if len(parts) == 1 else jnp.concatenate(parts, axis=1)
                turned = rows.reshape(GROUP, LANES).T[0:NZ]
                high = turned.astype(BF16)
                table[g, base : base + NZ, :] = high
                table[g, half + base : half + base + NZ, :] = (turned - high.astype(F32)).astype(BF16)

    seen[...] = jnp.zeros(seen.shape, F32)

    def gather(blocks, group, offsets):
        columns, here = pair_places(slots, blocks, offsets)
        found = jnp.dot(table[group], column_hits(columns), preferred_element_type=F32)
        lines = pair_rows(blocks)
        weights = [
            jnp.concatenate([slots[line, 5 + c : 6 + c, :] for line in lines], axis=1) for c in range(3)
        ]
        for n in range(STEPS):
            total = jnp.zeros((1, PAIR * BLOCK), F32)
            for c in range(3):
                base = (3 * n + c) * NZ
                both = found[base : base + NZ] + found[half + base : half + base + NZ]
                value = jnp.sum(jnp.where(here, both, 0.0), axis=0, keepdims=True)
                total = total + weights[c] * value
            for r, line in enumerate(lines):
                seen[n, pl.ds(line, 1), :] += total[:, LANES * r : LANES * r + LANES]

    each_product(work, GATHERS, gather)

    owners = sums.shape[0]
    apart = LANES // owners
    beam = slots[:, 1, :].astype(jnp.int32)
    lane = lax.broadcasted_iota(jnp.int32, (1, LANES), 1)
    lines = [jnp.zeros((1, LANES), F32)] * (STEPS * beams // apart)
    for n in range(STEPS):
        for k in range(beams):
            one = fold(owners, jnp.sum(jnp.where(beam == k, seen[n], 0.0), axis=0, keepdims=True))
            line, place = divmod(n * beams + k, apart)
            here = (lane >= place * owners) & (lane < place * owners + owners)
            lines[line] = jnp.where(here, one, lines[line])
    for line, total in enumerate(lines):
        span = slice(LANES * line, LANES * line + LANES)
        sums[:, :, span] = jnp.broadcast_to(total[None], (owners, 1, LANES))


def scatter_slots(first_group, together, work, slots, weight, total, force):
    total[...] = jnp.zeros(total.shape, F32)

    def scatter(blocks, group, offsets):
        columns, here = pair_places(slots, blocks, offsets)
        lines = pair_rows(blocks)
        high_rows, low_rows = [], []
        for f in range(FIELDS):
            value = jnp.concatenate([weight[f, pl.ds(line, 1), :] for line in lines], axis=1)
            high = value.astype(BF16).astype(F32)
            high_rows.append(jnp.where(here, high, 0.0).astype(BF16))
            low_rows.append(jnp.where(here, value - high, 0.0).astype(BF16))
        table = jnp.concatenate(
            [jnp.concatenate(high_rows, axis=0), jnp.concatenate(low_rows, axis=0)], axis=1
        )
        hits = column_hits(columns)
        hits = jnp.concatenate([hits, hits], axis=1)
        added = lax.dot_general(table, hits, (((1,), (1,)), ((), ())), preferred_element_type=F32)
        part = group - first_group
        for f in range(FIELDS):
            total[part, f, 0:NZ, :] += added[NZ * f : NZ * f + NZ]

    each_product(work, together, scatter)
    for f in range(FIELDS):
        for k in range(force.shape[1]):
            force[f, k] = total[k, f].T.reshape(CY, ROWS, LANES)


def outer_force_kernel(
    beams, work, slots, seen, sums, force, weight, near, far, first_rows, last_rows, total
):
    owners = sums.shape[0]
    apart = LANES // owners
    lines = jnp.sum(sums[...], axis=0) / GATES
    beam = slots[:, 1, :].astype(jnp.int32)
    lane = lax.broadcasted_iota(jnp.int32, (1, LANES), 1)
    for n in range(STEPS):
        mean = jnp.zeros(beam.shape, F32)
        for k in range(beams):
            line, place = divmod(n * beams + k, apart)
            here = (lane >= place * owners) & (lane < place * owners + owners)
            one = fold(owners, jnp.where(here, lines[:, LANES * line : LANES * line + LANES], 0.0))
            mean = jnp.where(beam == k, one, mean)
        misfit = seen[n] - mean - slots[:, 2 + n, :]
        for c in range(3):
            weight[3 * n + c] = slots[:, 5 + c, :] * misfit
    scatter_slots(0, OUTERS, work, slots, weight, total, force)
    for out, row_of in ((first_rows, lambda i: TURN + i), (last_rows, lambda i: TURN - 1 - i)):
        for b, (n, c, i) in enumerate(FORCE_BLOCKS):

            def put(row, rows, b=b, out=out):
                out[b, row : row + 8, :] = rows

            pack(put, force[3 * n + c, 0, :, row_of(i), :])
    to_partners("gx", first_rows, last_rows, near, far)


def inner_force_kernel(work, slots, weight, force, total):
    scatter_slots(1, INNERS, work, slots, weight, total, force)


def force_rim_kernel(outer, inner, x_near, x_far, near, far, first_layers, last_layers, before, after):
    from_partners("gx", x_near, x_far, before, after)
    index = {key: b for b, key in enumerate(FORCE_BLOCKS)}
    for out, layer_of in ((first_layers, lambda d: d - 1), (last_layers, lambda d: CY - d)):
        for b, (n, c, i) in enumerate(FORCE_BLOCKS):

            def put(row, rows, b=b, out=out):
                out[b * PACKED + row : b * PACKED + row + 8, :] = rows

            f, y = 3 * n + c, layer_of(i + 1)
            ends = outer[f, 0, y]
            middle = [inner[f, k, y] for k in range(GROUPS - 1)]
            pack(put, jnp.concatenate([ends[TURN:ROWS]] + middle + [ends[0:TURN]], axis=0))
        base = len(FORCE_BLOCKS) * PACKED
        for row, (n, c, dist, side, k) in enumerate(FORCE_CORNERS):
            piece = (before, after)[side]
            block = unpack(piece[index[(n, c, k - 1)]])
            y = layer_of(dist)
            out[base + row : base + row + 1, :] = block[y : y + 1]
    to_partners("gy", first_layers, last_layers, near, far)


def pull(field, source, target, low, high, first_row, chunks, add, mask, places):
    def layer(i, carry):
        y = i + low
        keep = layer_mask(y, places[2], places[3])
        done = []
        for t in range(chunks):
            r = first_row + 8 * t
            here, ahead, behind = pl.ds(r, 8), pl.ds(r + 1, 8), pl.ds(r - 1, 8)
            v = [field[c, y + RIM, here, :] for c in range(3)]
            v_ahead = [field[c, y + RIM, ahead, :] for c in range(3)]
            v_behind = [field[c, y + RIM, behind, :] for c in range(3)]
            v_next = [field[c, y + RIM + 1, here, :] for c in range(3)]
            v_last = [field[c, y + RIM - 1, here, :] for c in range(3)]
            a = [source[c, y + FRIM, here, :] for c in range(3)]
            scaled = [0.1 * f for f in a]
            bends = [None] * 3
            for d, (up, down) in enumerate(((v_ahead, v_behind), (v_next, v_last), (None, None))):
                for c in range(3):
                    u, w = (up[c], down[c]) if d < 2 else (next_level(v[c]), last_level(v[c]))
                    part = (u - w) * scaled[c]
                    bends[d] = part if bends[d] is None else bends[d] + part
            x_ahead = 0.1 + 0.1 * v_ahead[0]
            x_behind = 0.1 - 0.1 * v_behind[0]
            y_next = 0.1 + 0.1 * v_next[1]
            y_last = 0.1 - 0.1 * v_last[1]
            inside = mask[here, :] * keep
            for c in range(3):
                total = 0.4 * a[c] - bends[c]
                total = total + (
                    x_ahead * source[c, y + FRIM, ahead, :] + x_behind * source[c, y + FRIM, behind, :]
                )
                total = total + (
                    y_next * source[c, y + FRIM + 1, here, :] + y_last * source[c, y + FRIM - 1, here, :]
                )
                product = v[2] * scaled[c]
                total = total + (next_level(scaled[c] + product) + last_level(scaled[c] - product))
                if add:
                    total = total + target[c, y + FRIM, here, :]
                done.append((c, here, total * inside))
        for c, here, total in done:
            target[c, y + FRIM, here, :] = total
        return carry

    lax.fori_loop(0, high - low, layer, 0, unroll=True)


def edge_layers(side):
    start = (FRIM, FRIM + CY - EDGE)[side]
    return slice(start, start + EDGE)


def inner_backward_kernel(
    outer, inner, x_near, x_far, s0, s1, s2, part, e1, e2, e3, a1, a2, a3, a0, mask, before, after
):
    from_partners("gx", x_near, x_far, before, after)
    places = mesh_places()
    mask[...] = row_mask(places[0], places[1])
    adjoints = (a1, a2, a3)
    for n in range(STEPS):
        layers = slice(FRIM, FRIM + CY)
        adjoints[n][:, layers, 0:PAD] = jnp.zeros((3, CY, PAD, LANES), F32)
        adjoints[n][:, layers, PAD + CX : XH] = jnp.zeros((3, CY, PAD, LANES), F32)
        for c in range(3):
            for g in range(GROUPS):
                force = outer[3 * n + c, 0] if g == 0 else inner[3 * n + c, g - 1]
                for x, row, count in group_rows(g):
                    adjoints[n][c, FRIM : FRIM + CY, PAD + x : PAD + x + count, :] = force[:, row : row + count]
    for b, (n, c, i) in enumerate(FORCE_BLOCKS):
        adjoints[n][c, FRIM : FRIM + CY, PAD - 1 - i, :] = unpack(before[b])
        adjoints[n][c, FRIM : FRIM + CY, PAD + CX + i, :] = unpack(after[b])
    pull(s2, a3, a2, 1, CY - 1, 4, 5, True, mask, places)
    pull(s1, a2, a1, 2, CY - 2, 4, 5, True, mask, places)
    pull(s0, a1, a0, 3, CY - 3, PAD, 4, False, mask, places)
    for n, edges in enumerate((e1, e2, e3)):
        for side in range(2):
            edges[:, side] = adjoints[n][:, edge_layers(side)]
    for c in range(3):
        for y in range(3, CY - 3):
            part[c, :, NZ * y : NZ * y + NZ] = a0[c, FRIM + y, PAD : PAD + CX, 0:NZ]


def backward_kernel(
    part, e1, e2, e3, y_near, y_far, s0, s1, s2, out, a1, a2, a3, a0, mask, below, above
):
    from_partners("gy", y_near, y_far, below, above)
    places = mesh_places()
    mask[...] = row_mask(places[0], places[1])
    adjoints = (a1, a2, a3)
    out[...] = part[...]
    for n, edges in enumerate((e1, e2, e3)):
        for side in range(2):
            adjoints[n][:, edge_layers(side)] = edges[:, side]
        for start in (0, FRIM + CY):
            adjoints[n][:, start : start + FRIM] = jnp.zeros((3, FRIM, XH, LANES), F32)
    for piece, layer_of in ((above, lambda d: FRIM + CY - 1 + d), (below, lambda d: FRIM - d)):
        for b, (n, c, i) in enumerate(FORCE_BLOCKS):
            adjoints[n][c, layer_of(i + 1), PAD : PAD + CX, :] = unpack(piece[b * PACKED : b * PACKED + PACKED, :])
        base = len(FORCE_BLOCKS) * PACKED
        for row, (n, c, dist, side, k) in enumerate(FORCE_CORNERS):
            x = (PAD - k, PAD + CX - 1 + k)[side]
            adjoints[n][c, layer_of(dist), x : x + 1, :] = piece[base + row : base + row + 1, :]
    for low in (-2, CY - 1):
        pull(s2, a3, a2, low, low + 3, 4, 5, True, mask, places)
    for low in (-1, CY - 2):
        pull(s1, a2, a1, low, low + 3, 4, 5, True, mask, places)
    for low in (0, CY - 3):
        pull(s0, a1, a0, low, low + 3, PAD, 4, False, mask, places)
    for c in range(3):
        for y in (0, 1, 2, CY - 3, CY - 2, CY - 1):
            out[c, :, NZ * y : NZ * y + NZ] = a0[c, FRIM + y, PAD : PAD + CX, 0:NZ]


def swap(near, far, axis):
    def pairs(start):
        lows = range(start, lax.axis_size(axis) - 1, 2)
        return [(i, i + 1) for i in lows] + [(i + 1, i) for i in lows]

    return lax.ppermute(near, axis, pairs(0)), lax.ppermute(far, axis, pairs(1))


def local(initial_state, beam_dir, gate_obs, slot_beam, slot_cell):
    peers, capacity = slot_beam.shape[1:]
    beams = beam_dir.shape[1]
    rows = peers * capacity // LANES
    x_rim = (16, CY * NZ)
    edge = (3, ROWS, CY * NZ)
    near, far = pl.pallas_call(
        state_rows_kernel,
        out_shape=(shape(*x_rim), shape(*x_rim)),
        in_specs=[
            pl.BlockSpec(edge, lambda i: (0, 0, 0)),
            pl.BlockSpec(edge, lambda i: (0, GROUPS - 1, 0)),
        ],
        out_specs=(pl.BlockSpec(x_rim, lambda i: (0, 0)), pl.BlockSpec(x_rim, lambda i: (0, 0))),
        grid=(1,),
        scratch_shapes=[pltpu.VMEM(x_rim, F32)] * 2,
        compiler_params=pltpu.CompilerParams(vmem_limit_bytes=8 * MIB),
    )(initial_state, initial_state)
    x_near, x_far = swap(near, far, "gx")
    lists = (peers, 8, capacity)
    slots = call(
        arrange_kernel,
        shape(*lists),
        [pltpu.VMEM(lists, F32), pltpu.VMEM((peers, capacity), jnp.int32)],
        limit=60,
        ins=4,
    )(beam_dir, gate_obs, slot_beam, slot_cell)
    slots = lax.all_to_all(slots, AXES, split_axis=0, concat_axis=0, tiled=True)
    work = jax.ShapeDtypeStruct((WORK,), jnp.int32)
    slots, every_work, outer_work, inner_work = call(
        regroup_kernel,
        (shape(rows, 8, LANES), work, work, work),
        [pltpu.VMEM((LANES, LANES), F32)],
        ins=1,
        scalar_out=(1, 2, 3),
        micros=2,
    )(slots)
    field = shape(3, YH, XH, LANES)
    y_rim = (STATE_PIECE, LANES)
    near, far = call(
        state_corner_kernel,
        (shape(*y_rim), shape(*y_rim)),
        [pltpu.VMEM(y_rim, F32)] * 2 + [pltpu.VMEM(x_rim, F32)] * 2,
        ins=3,
    )(initial_state, x_near, x_far)
    y_near, y_far = swap(near, far, "gy")
    mask = pltpu.VMEM((XH, LANES), F32)
    seen, sums, s0, s1, s2 = call(
        functools.partial(forward_kernel, beams),
        (shape(STEPS, rows, LANES), shape(peers, 1, STEPS * beams * peers), field, field, field),
        [pltpu.VMEM(field.shape, F32), pltpu.VMEM((GROUPS, 2 * FIELDS * NZ, GROUP), BF16), mask]
        + [pltpu.VMEM(y_rim, F32)] * 2
        + [pltpu.VMEM(x_rim, F32)] * 2,
        limit=32,
        ins=7,
        scalar_in=(0,),
    )(every_work, initial_state, x_near, x_far, y_near, y_far, slots)
    sums = lax.all_to_all(sums, AXES, split_axis=0, concat_axis=0, tiled=True)
    x_rim = (len(FORCE_BLOCKS), PACKED, LANES)
    parts = [shape(FIELDS, count, CY, ROWS, LANES) for count in (1, GROUPS - 1)]
    totals = [pltpu.VMEM((count, FIELDS, LANES, GROUP), F32) for count in (1, GROUPS - 1)]
    outer, weight, near, far = call(
        functools.partial(outer_force_kernel, beams),
        (parts[0], shape(FIELDS, rows, LANES), shape(*x_rim), shape(*x_rim)),
        [pltpu.VMEM(x_rim, F32)] * 2 + [totals[0]],
        limit=24,
        ins=4,
        scalar_in=(0,),
    )(outer_work, slots, seen, sums)
    x_near, x_far = swap(near, far, "gx")
    inner = call(inner_force_kernel, parts[1], [totals[1]], limit=24, ins=3, scalar_in=(0,), micros=6)(
        inner_work, slots, weight
    )
    y_rim = (FORCE_PIECE, LANES)
    near, far = call(
        force_rim_kernel,
        (shape(*y_rim), shape(*y_rim)),
        [pltpu.VMEM(y_rim, F32)] * 2 + [pltpu.VMEM(x_rim, F32)] * 2,
        ins=4,
    )(outer, inner, x_near, x_far)
    y_near, y_far = swap(near, far, "gy")
    edges = shape(3, 2, EDGE, XH, LANES)
    adjoint = pltpu.VMEM((3, FH, XH, LANES), F32)
    whole = shape(*initial_state.shape)
    part, e1, e2, e3 = call(
        inner_backward_kernel,
        (whole, edges, edges, edges),
        [adjoint] * 4 + [mask] + [pltpu.VMEM(x_rim, F32)] * 2,
        limit=32,
        ins=7,
        micros=8,
    )(outer, inner, x_near, x_far, s0, s1, s2)
    return call(
        backward_kernel, whole, [adjoint] * 4 + [mask] + [pltpu.VMEM(y_rim, F32)] * 2, limit=32, ins=9
    )(part, e1, e2, e3, y_near, y_far, s0, s1, s2)


def solution(mesh):
    in_specs = (
        P(None, "gx", "gy"),
        P(None, ("gx", "gy")),
        P(None, ("gx", "gy"), None, None),
        P(("gx", "gy"), None, None),
        P(("gx", "gy"), None, None),
    )
    out_specs = P(None, "gx", "gy")
    return jax.shard_map(local, mesh=mesh, in_specs=in_specs, out_specs=out_specs, check_vma=False)
```

```python
import functools

import jax
import jax.numpy as jnp
from jax import lax
from jax.experimental import pallas as pl
from jax.experimental.pallas import tpu as pltpu
from jax.sharding import PartitionSpec as P

NZ = 96
GATES = 512
STEPS = 3
LANES = 128
CX = 32
CY = 32
COLUMNS = CX * CY
RIM = 5
PAD = 8
XH = CX + 2 * PAD
YH = CY + 2 * RIM
PACKED = CX * NZ // LANES
FRIM = 3
FH = CY + 2 * FRIM
EDGE = 4
FIELDS = 3 * STEPS
ROWS = 8
TURN = 4
GROUPS = CX // ROWS
GROUP = ROWS * CY
BLOCK = 256
BLOCK_ROWS = BLOCK // LANES
PAIR = 2
GATHERS, OUTERS, INNERS = 2, 1, 1
WORK = 128
BLANK = 256
F32 = jnp.float32
BF16 = jnp.bfloat16
AXES = ("gx", "gy")
MIB = 1024 * 1024


def call(kernel, outs, scratch=(), limit=12, ins=0, scalar_in=(), scalar_out=(), micros=1):
    def specs(count, scalar):
        spaces = [pltpu.SMEM if i in scalar else pltpu.VMEM for i in range(count)]
        return [pl.BlockSpec(memory_space=space) for space in spaces]

    single = not isinstance(outs, tuple)
    out_specs = specs(1 if single else len(outs), scalar_out)
    return pl.pallas_call(
        kernel,
        out_shape=outs,
        in_specs=specs(ins, scalar_in),
        out_specs=out_specs[0] if single else tuple(out_specs),
        scratch_shapes=list(scratch),
        compiler_params=pltpu.CompilerParams(vmem_limit_bytes=limit * MIB),
        cost_estimate=pl.CostEstimate(flops=0, bytes_accessed=micros * 3_000_000, transcendentals=0),
    )


def shape(*dims):
    return jax.ShapeDtypeStruct(dims, F32)


def lane_of(rows=8):
    return lax.broadcasted_iota(jnp.int32, (rows, LANES), 1)


def pack(put, block):
    lane = lane_of()
    last = block[24:32]
    for j in range(3):
        tail = pltpu.roll(last, 96 - 32 * j, axis=1)
        put(8 * j, jnp.where(lane < NZ, block[8 * j : 8 * j + 8], tail))


def unpack(rows):
    lane = lane_of()
    last = jnp.zeros((8, LANES), F32)
    parts = []
    for j in range(3):
        piece = rows[8 * j : 8 * j + 8]
        parts.append(jnp.where(lane < NZ, piece, 0.0))
        moved = pltpu.roll(piece, (32 * j - 96) % LANES, axis=1)
        last = jnp.where((lane >= 32 * j) & (lane < 32 * j + 32), moved, last)
    return jnp.concatenate(parts + [last], axis=0)


def is_odd(axis):
    return lax.axis_index(axis) % 2 == 1


def to_partners(axis, first, last, near, far):
    odd = is_odd(axis)
    near[...] = jnp.where(odd, first[...], last[...])
    far[...] = jnp.where(odd, last[...], first[...])


def from_partners(axis, near, far, behind, ahead):
    odd = is_odd(axis)
    behind[...] = jnp.where(odd, near[...], far[...])
    ahead[...] = jnp.where(odd, far[...], near[...])


def corner_rows(rim):
    rows, out = 0, []
    for comp in range(3):
        for dist in range(1, rim):
            out.append((comp, dist, rows, rim - dist))
            rows += 2 * (rim - dist)
    return out, rows


STATE_CORNERS, STATE_CORNER_ROWS = corner_rows(RIM)
STRIP = -(-RIM * NZ // LANES)
STATE_PIECE = 3 * STRIP * CX + 64
FORCE_BLOCKS = [(n, c, i) for n in range(STEPS) for c in range(3) for i in range(n + 1)]
FORCE_CORNERS = [
    (n, c, dist, side, k)
    for n in range(STEPS)
    for c in range(3)
    for dist in range(1, n + 1)
    for side in range(2)
    for k in range(1, n + 2 - dist)
]
FORCE_PIECE = len(FORCE_BLOCKS) * PACKED + 24


def state_rows_kernel(top, bottom, near, far, first_rows, last_rows):
    for c in range(3):
        first_rows[RIM * c : RIM * c + RIM, :] = top[c, 0:RIM, :]
        last_rows[RIM * c : RIM * c + RIM, :] = bottom[c, ROWS - RIM : ROWS, :]
    first_rows[3 * RIM : 16, :] = jnp.zeros((1, CY * NZ), F32)
    last_rows[3 * RIM : 16, :] = jnp.zeros((1, CY * NZ), F32)
    to_partners("gx", first_rows, last_rows, near, far)


def cell_group(cell):
    x = ((cell + 0.5) * (1.0 / (CY * NZ))).astype(jnp.int32)
    return lax.shift_right_logical((x + TURN) & (CX - 1), 3)


def arrange_kernel(beam_dir, obs, beam, cell, slots, values, places):
    beams = beam_dir.shape[1]
    owned = beam[0]
    lists, capacity = owned.shape
    used = owned >= 0
    masks = [owned == k for k in range(beams)]

    def spread(parts):
        total = jnp.zeros(owned.shape, F32)
        for k in range(beams):
            total = jnp.where(masks[k], parts[k], total)
        return total

    cells = cell[0].astype(F32)
    values[:, 0, :] = cells + 1.0
    values[:, 1, :] = owned.astype(F32)
    for n in range(STEPS):
        seen = obs[n, 0]
        means = [jnp.sum(jnp.where(m, seen, 0.0), keepdims=True) / GATES for m in masks]
        values[:, 2 + n, :] = jnp.where(used, seen - spread(means), 0.0)
    for c in range(3):
        values[:, 5 + c, :] = spread([beam_dir[c : c + 1, k : k + 1] for k in range(beams)])

    group = cell_group(cells)
    row = lax.broadcasted_iota(jnp.int32, (capacity, capacity), 0)
    column = lax.broadcasted_iota(jnp.int32, (capacity, capacity), 1)
    ahead = jnp.where(row <= column, 1.0, 0.0).astype(BF16)
    ones = [jnp.where(used & (group == g), 1.0, 0.0) for g in range(GROUPS)]
    counts = [jnp.sum(o, axis=1, keepdims=True) for o in ones]
    place = jnp.full(owned.shape, -1.0, F32)
    end = jnp.zeros((lists, 1), F32)
    left = counts[0] + counts[1] + counts[2] + counts[3]
    for g in range(GROUPS):
        start = jnp.minimum(jnp.maximum(float(capacity // GROUPS * g), end), capacity - left)
        upto = jnp.dot(ones[g].astype(BF16), ahead, preferred_element_type=F32)
        place = jnp.where(ones[g] > 0.5, start + upto - 1.0, place)
        end = start + counts[g]
        left = left - counts[g]
    places[...] = place.astype(jnp.int32)

    def move(i, carry):
        full = values[i]
        high = full.astype(BF16).astype(F32)
        mid = (full - high).astype(BF16).astype(F32)
        low = full - high - mid
        three = jnp.concatenate([high, mid, low], axis=0).astype(BF16)
        hits = jnp.where(row == places[pl.ds(i, 1), :], 1.0, 0.0).astype(BF16)
        moved = lax.dot_general(three, hits, (((1,), (1,)), ((), ())), preferred_element_type=F32)
        slots[i] = moved[0:8] + moved[8:16] + moved[16:24]
        return carry

    lax.fori_loop(0, lists, move, 0, unroll=16)


def regroup_kernel(received, slots, every_work, outer_work, inner_work, turned):
    owners, _, capacity = received.shape
    apart = LANES // owners
    rows = capacity // apart
    for j in range(8):
        lists = received[:, j, :]
        if capacity < LANES:
            lists = jnp.concatenate([lists, jnp.zeros((owners, LANES - capacity), F32)], axis=1)
        if owners < LANES:
            lists = jnp.concatenate([lists, jnp.zeros((LANES - owners, LANES), F32)], axis=0)
        turned[...] = lists.T
        line = turned[pl.ds(0, rows, stride=apart), :]
        for k in range(1, apart):
            line = line + pltpu.roll(turned[pl.ds(k, rows, stride=apart), :], k * owners, axis=1)
        slots[:, j, :] = line
    cell = slots[:, 0, :]
    group = cell_group(cell - 1.0).astype(F32)
    low = jnp.where(cell > 0.5, group, float(GROUPS))
    high = jnp.where(cell > 0.5, group, -1.0)
    spans = [slice(BLOCK_ROWS * b, BLOCK_ROWS * b + BLOCK_ROWS) for b in range(rows // BLOCK_ROWS)]
    firsts = [jnp.min(low[span]).astype(jnp.int32) for span in spans]
    lasts = [jnp.max(high[span]).astype(jnp.int32) for span in spans]
    for work, groups in (
        (outer_work, (0,)),
        (inner_work, tuple(range(1, GROUPS))),
        (every_work, tuple(range(GROUPS))),
    ):
        count = jnp.int32(0)
        for g in groups:
            for b in range(len(spans)):
                work[count] = b * GROUPS + g
                count = count + ((firsts[b] <= g) & (lasts[b] >= g)).astype(jnp.int32)
            work[count] = BLANK + g
            count = count + (count & 1)
        for k in range(2 * PAIR):
            work[count + k] = BLANK + groups[0]
        work[WORK - 1] = count


def state_corner_kernel(state, x_near, x_far, near, far, first, last, before, after):
    from_partners("gx", x_near, x_far, before, after)
    base = 3 * STRIP * CX
    for start, out, layer_of in (
        (0, first, lambda d: d - 1),
        (CY * NZ - STRIP * LANES, last, lambda d: CY - d),
    ):
        for c in range(3):
            for j in range(STRIP):
                lanes = slice(start + LANES * j, start + LANES * j + LANES)
                out[(c * STRIP + j) * CX : (c * STRIP + j + 1) * CX, :] = state[c, :, lanes]
        out[base : base + 64, :] = jnp.zeros((64, LANES), F32)
        for c, dist, row, side in STATE_CORNERS:
            lanes = slice(NZ * layer_of(dist), NZ * layer_of(dist) + NZ)
            out[base + row : base + row + side, 0:NZ] = before[RIM * c + dist : RIM * c + RIM, lanes]
            out[base + row + side : base + row + 2 * side, 0:NZ] = after[RIM * c : RIM * c + side, lanes]
    to_partners("gy", first, last, near, far)


def row_mask(x_place, x_count):
    row = lax.broadcasted_iota(jnp.int32, (XH, LANES), 0)
    lane = lax.broadcasted_iota(jnp.int32, (XH, LANES), 1)
    low = jnp.where(x_place == 0, PAD, 0)
    high = jnp.where(x_place == x_count - 1, PAD + CX, XH)
    return jnp.where((row >= low) & (row < high) & (lane < NZ), 1.0, 0.0).astype(F32)


def layer_mask(y, y_place, y_count):
    outside = ((y < 0) & (y_place == 0)) | ((y >= CY) & (y_place == y_count - 1))
    return jnp.where(outside, 0.0, 1.0).astype(F32)


def next_level(v):
    return pltpu.roll(v, LANES - 1, axis=1)


def last_level(v):
    return pltpu.roll(v, 1, axis=1)


def step_forward(src, dst, low, high, first_row, chunks, mask, places):
    def layer(i, carry):
        y = i + low
        keep = layer_mask(y, places[2], places[3])
        done = []
        for t in range(chunks):
            r = first_row + 8 * t
            here, ahead, behind = pl.ds(r, 8), pl.ds(r + 1, 8), pl.ds(r - 1, 8)
            centre = [src[c, y + RIM, here, :] for c in range(3)]
            plus = [1.0 - v for v in centre]
            minus = [1.0 + v for v in centre]
            tenth = mask[here, :] * (0.1 * keep)
            for c in range(3):
                v = centre[c]
                total = 4.0 * v + (plus[2] * next_level(v) + minus[2] * last_level(v))
                total = total + (plus[0] * src[c, y + RIM, ahead, :] + minus[0] * src[c, y + RIM, behind, :])
                total = total + (
                    plus[1] * src[c, y + RIM + 1, here, :] + minus[1] * src[c, y + RIM - 1, here, :]
                )
                done.append((c, here, total * tenth))
        for c, here, total in done:
            dst[c, y + RIM, here, :] = total
        return carry

    lax.fori_loop(0, high - low, layer, 0, unroll=True)


def mesh_places():
    return (
        lax.axis_index("gx"),
        lax.axis_size("gx"),
        lax.axis_index("gy"),
        lax.axis_size("gy"),
    )


def slot_columns(slots, row):
    cell = slots[row, 0:1, :] - 1.0
    x = ((cell + 0.5) * (1.0 / (CY * NZ))).astype(jnp.int32)
    rest = cell.astype(jnp.int32) - x * (CY * NZ)
    y = ((rest.astype(F32) + 0.5) * (1.0 / NZ)).astype(jnp.int32)
    turned = (x + TURN) & (CX - 1)
    high = lax.shift_right_logical(turned, 3)
    return high * (GROUP - ROWS) + y * ROWS + turned, rest - y * NZ


def column_hits(columns):
    place = lax.broadcasted_iota(jnp.int32, (GROUP, columns.shape[1]), 0)
    return jnp.where(place == columns, 1.0, 0.0).astype(BF16)


def pair_rows(blocks):
    return [block * BLOCK_ROWS + r for block in blocks for r in range(BLOCK_ROWS)]


def pair_places(slots, blocks, offsets):
    places = [slot_columns(slots, row) for row in pair_rows(blocks)]
    columns = [p[0] - offsets[k // BLOCK_ROWS] for k, p in enumerate(places)]
    level = jnp.concatenate([p[1] for p in places], axis=1)
    here = lax.broadcasted_iota(jnp.int32, (NZ, PAIR * BLOCK), 0) == level
    return jnp.concatenate(columns, axis=1), here


def each_product(work, together, body):
    count = work[WORK - 1]

    def some(i, carry):
        for k in range(together):
            item = (i * together + k) * PAIR
            codes = [work[item + p] for p in range(PAIR)]
            group = codes[0] & (GROUPS - 1)
            blocks = [lax.shift_right_logical(code & (BLANK - 1), GROUPS // 2) for code in codes]
            live = [(item < count) & (code < BLANK) for code in codes]
            body(blocks, group, [jnp.where(l, group * GROUP, -(1 << 20)) for l in live])
        return carry

    lax.fori_loop(0, lax.shift_right_logical(count + PAIR * together - 1, together), some, 0)


def group_rows(g):
    if g == 0:
        return ((CX - TURN, 0, TURN), (0, TURN, ROWS - TURN))
    return ((ROWS * g - TURN, 0, ROWS),)


def fold(owners, line):
    reach = LANES // 2
    while reach >= owners:
        line = line + pltpu.roll(line, reach, axis=1)
        reach //= 2
    return line


def forward_kernel(
    beams,
    work,
    state,
    x_near,
    x_far,
    y_near,
    y_far,
    slots,
    seen,
    sums,
    s0,
    s1,
    s2,
    s3,
    table,
    mask,
    below,
    above,
    before,
    after,
):
    places = mesh_places()
    from_partners("gx", x_near, x_far, before, after)
    mask[...] = row_mask(places[0], places[1])
    from_partners("gy", y_near, y_far, below, above)
    s0[...] = jnp.zeros(s0.shape, F32)
    for c in range(3):
        for y in range(CY):
            lanes = slice(NZ * y, NZ * y + NZ)
            s0[c, RIM + y, PAD : PAD + CX, 0:NZ] = state[c, :, lanes]
            s0[c, RIM + y, PAD - RIM : PAD, 0:NZ] = before[RIM * c : RIM * c + RIM, lanes]
            s0[c, RIM + y, PAD + CX : PAD + CX + RIM, 0:NZ] = after[RIM * c : RIM * c + RIM, lanes]
    for piece, layer_of, lane_of_layer in (
        (above, lambda d: RIM + CY - 1 + d, lambda d: NZ * (d - 1)),
        (below, lambda d: RIM - d, lambda d: STRIP * LANES - NZ * d),
    ):
        for c in range(3):
            tiles = [piece[(c * STRIP + j) * CX : (c * STRIP + j + 1) * CX, :] for j in range(STRIP)]
            strip = jnp.concatenate(tiles, axis=1)
            for dist in range(1, RIM + 1):
                lane = lane_of_layer(dist)
                s0[c, layer_of(dist), PAD : PAD + CX, 0:NZ] = strip[:, lane : lane + NZ]
        base = 3 * STRIP * CX
        for c, dist, row, side in STATE_CORNERS:
            s0[c, layer_of(dist), PAD - side : PAD, :] = piece[base + row : base + row + side, :]
            s0[c, layer_of(dist), PAD + CX : PAD + CX + side, :] = piece[
                base + row + side : base + row + 2 * side, :
            ]
    step_forward(s0, s1, -4, CY + 4, 4, 5, mask, places)
    step_forward(s1, s2, -3, CY + 3, 4, 5, mask, places)
    step_forward(s2, s3, 0, CY, PAD, 4, mask, places)

    half = FIELDS * NZ
    for n, field in enumerate((s1, s2, s3)):
        for c in range(3):
            base = (3 * n + c) * NZ
            for g in range(GROUPS):
                layers = slice(RIM, RIM + CY)
                parts = [field[c, layers, PAD + x : PAD + x + count, :] for x, _, count in group_rows(g)]
                rows = parts[0] if len(parts) == 1 else jnp.concatenate(parts, axis=1)
                turned = rows.reshape(GROUP, LANES).T[0:NZ]
                high = turned.astype(BF16)
                table[g, base : base + NZ, :] = high
                table[g, half + base : half + base + NZ, :] = (turned - high.astype(F32)).astype(BF16)

    seen[...] = jnp.zeros(seen.shape, F32)

    def gather(blocks, group, offsets):
        columns, here = pair_places(slots, blocks, offsets)
        found = jnp.dot(table[group], column_hits(columns), preferred_element_type=F32)
        lines = pair_rows(blocks)
        weights = [
            jnp.concatenate([slots[line, 5 + c : 6 + c, :] for line in lines], axis=1) for c in range(3)
        ]
        for n in range(STEPS):
            total = jnp.zeros((1, PAIR * BLOCK), F32)
            for c in range(3):
                base = (3 * n + c) * NZ
                both = found[base : base + NZ] + found[half + base : half + base + NZ]
                value = jnp.sum(jnp.where(here, both, 0.0), axis=0, keepdims=True)
                total = total + weights[c] * value
            for r, line in enumerate(lines):
                seen[n, pl.ds(line, 1), :] += total[:, LANES * r : LANES * r + LANES]

    each_product(work, GATHERS, gather)

    owners = sums.shape[0]
    apart = LANES // owners
    beam = slots[:, 1, :].astype(jnp.int32)
    lane = lax.broadcasted_iota(jnp.int32, (1, LANES), 1)
    lines = [jnp.zeros((1, LANES), F32)] * (STEPS * beams // apart)
    for n in range(STEPS):
        for k in range(beams):
            one = fold(owners, jnp.sum(jnp.where(beam == k, seen[n], 0.0), axis=0, keepdims=True))
            line, place = divmod(n * beams + k, apart)
            here = (lane >= place * owners) & (lane < place * owners + owners)
            lines[line] = jnp.where(here, one, lines[line])
    for line, total in enumerate(lines):
        span = slice(LANES * line, LANES * line + LANES)
        sums[:, :, span] = jnp.broadcast_to(total[None], (owners, 1, LANES))


def scatter_slots(first_group, together, work, slots, weight, total, force):
    total[...] = jnp.zeros(total.shape, F32)

    def scatter(blocks, group, offsets):
        columns, here = pair_places(slots, blocks, offsets)
        lines = pair_rows(blocks)
        high_rows, low_rows = [], []
        for f in range(FIELDS):
            value = jnp.concatenate([weight[f, pl.ds(line, 1), :] for line in lines], axis=1)
            high = value.astype(BF16).astype(F32)
            high_rows.append(jnp.where(here, high, 0.0).astype(BF16))
            low_rows.append(jnp.where(here, value - high, 0.0).astype(BF16))
        table = jnp.concatenate(
            [jnp.concatenate(high_rows, axis=0), jnp.concatenate(low_rows, axis=0)], axis=1
        )
        hits = column_hits(columns)
        hits = jnp.concatenate([hits, hits], axis=1)
        added = lax.dot_general(table, hits, (((1,), (1,)), ((), ())), preferred_element_type=F32)
        part = group - first_group
        for f in range(FIELDS):
            total[part, f, 0:NZ, :] += added[NZ * f : NZ * f + NZ]

    each_product(work, together, scatter)
    for f in range(FIELDS):
        for k in range(force.shape[1]):
            force[f, k] = total[k, f].T.reshape(CY, ROWS, LANES)


def outer_force_kernel(
    beams, work, slots, seen, sums, force, weight, near, far, first_rows, last_rows, total
):
    owners = sums.shape[0]
    apart = LANES // owners
    lines = jnp.sum(sums[...], axis=0) / GATES
    beam = slots[:, 1, :].astype(jnp.int32)
    lane = lax.broadcasted_iota(jnp.int32, (1, LANES), 1)
    for n in range(STEPS):
        mean = jnp.zeros(beam.shape, F32)
        for k in range(beams):
            line, place = divmod(n * beams + k, apart)
            here = (lane >= place * owners) & (lane < place * owners + owners)
            one = fold(owners, jnp.where(here, lines[:, LANES * line : LANES * line + LANES], 0.0))
            mean = jnp.where(beam == k, one, mean)
        misfit = seen[n] - mean - slots[:, 2 + n, :]
        for c in range(3):
            weight[3 * n + c] = slots[:, 5 + c, :] * misfit
    scatter_slots(0, OUTERS, work, slots, weight, total, force)
    for out, row_of in ((first_rows, lambda i: TURN + i), (last_rows, lambda i: TURN - 1 - i)):
        for b, (n, c, i) in enumerate(FORCE_BLOCKS):

            def put(row, rows, b=b, out=out):
                out[b, row : row + 8, :] = rows

            pack(put, force[3 * n + c, 0, :, row_of(i), :])
    to_partners("gx", first_rows, last_rows, near, far)


def inner_force_kernel(work, slots, weight, force, total):
    scatter_slots(1, INNERS, work, slots, weight, total, force)


def force_rim_kernel(outer, inner, x_near, x_far, near, far, first_layers, last_layers, before, after):
    from_partners("gx", x_near, x_far, before, after)
    index = {key: b for b, key in enumerate(FORCE_BLOCKS)}
    for out, layer_of in ((first_layers, lambda d: d - 1), (last_layers, lambda d: CY - d)):
        for b, (n, c, i) in enumerate(FORCE_BLOCKS):

            def put(row, rows, b=b, out=out):
                out[b * PACKED + row : b * PACKED + row + 8, :] = rows

            f, y = 3 * n + c, layer_of(i + 1)
            ends = outer[f, 0, y]
            middle = [inner[f, k, y] for k in range(GROUPS - 1)]
            pack(put, jnp.concatenate([ends[TURN:ROWS]] + middle + [ends[0:TURN]], axis=0))
        base = len(FORCE_BLOCKS) * PACKED
        for row, (n, c, dist, side, k) in enumerate(FORCE_CORNERS):
            piece = (before, after)[side]
            block = unpack(piece[index[(n, c, k - 1)]])
            y = layer_of(dist)
            out[base + row : base + row + 1, :] = block[y : y + 1]
    to_partners("gy", first_layers, last_layers, near, far)


def pull(field, source, target, low, high, first_row, chunks, add, mask, places):
    def layer(i, carry):
        y = i + low
        keep = layer_mask(y, places[2], places[3])
        done = []
        for t in range(chunks):
            r = first_row + 8 * t
            here, ahead, behind = pl.ds(r, 8), pl.ds(r + 1, 8), pl.ds(r - 1, 8)
            v = [field[c, y + RIM, here, :] for c in range(3)]
            v_ahead = [field[c, y + RIM, ahead, :] for c in range(3)]
            v_behind = [field[c, y + RIM, behind, :] for c in range(3)]
            v_next = [field[c, y + RIM + 1, here, :] for c in range(3)]
            v_last = [field[c, y + RIM - 1, here, :] for c in range(3)]
            a = [source[c, y + FRIM, here, :] for c in range(3)]
            bends = [None] * 3
            for d, (up, down) in enumerate(((v_ahead, v_behind), (v_next, v_last), (None, None))):
                for c in range(3):
                    u, w = (up[c], down[c]) if d < 2 else (next_level(v[c]), last_level(v[c]))
                    part = (u - w) * a[c]
                    bends[d] = part if bends[d] is None else bends[d] + part
            x_ahead = 1.0 + v_ahead[0]
            x_behind = 1.0 - v_behind[0]
            y_next = 1.0 + v_next[1]
            y_last = 1.0 - v_last[1]
            tenth = mask[here, :] * (0.1 * keep)
            for c in range(3):
                total = 4.0 * a[c] - bends[c]
                total = total + (
                    x_ahead * source[c, y + FRIM, ahead, :] + x_behind * source[c, y + FRIM, behind, :]
                )
                total = total + (
                    y_next * source[c, y + FRIM + 1, here, :] + y_last * source[c, y + FRIM - 1, here, :]
                )
                product = v[2] * a[c]
                total = total + (next_level(a[c] + product) + last_level(a[c] - product))
                total = total * tenth
                if add:
                    total = total + target[c, y + FRIM, here, :]
                done.append((c, here, total))
        for c, here, total in done:
            target[c, y + FRIM, here, :] = total
        return carry

    lax.fori_loop(0, high - low, layer, 0, unroll=True)


def edge_layers(side):
    start = (FRIM, FRIM + CY - EDGE)[side]
    return slice(start, start + EDGE)


def inner_backward_kernel(
    outer, inner, x_near, x_far, s0, s1, s2, part, e1, e2, e3, a1, a2, a3, a0, mask, before, after
):
    from_partners("gx", x_near, x_far, before, after)
    places = mesh_places()
    mask[...] = row_mask(places[0], places[1])
    adjoints = (a1, a2, a3)
    for n in range(STEPS):
        layers = slice(FRIM, FRIM + CY)
        adjoints[n][:, layers, 0:PAD] = jnp.zeros((3, CY, PAD, LANES), F32)
        adjoints[n][:, layers, PAD + CX : XH] = jnp.zeros((3, CY, PAD, LANES), F32)
        for c in range(3):
            for g in range(GROUPS):
                force = outer[3 * n + c, 0] if g == 0 else inner[3 * n + c, g - 1]
                for x, row, count in group_rows(g):
                    adjoints[n][c, FRIM : FRIM + CY, PAD + x : PAD + x + count, :] = force[:, row : row + count]
    for b, (n, c, i) in enumerate(FORCE_BLOCKS):
        adjoints[n][c, FRIM : FRIM + CY, PAD - 1 - i, :] = unpack(before[b])
        adjoints[n][c, FRIM : FRIM + CY, PAD + CX + i, :] = unpack(after[b])
    pull(s2, a3, a2, 1, CY - 1, 4, 5, True, mask, places)
    pull(s1, a2, a1, 2, CY - 2, 4, 5, True, mask, places)
    pull(s0, a1, a0, 3, CY - 3, PAD, 4, False, mask, places)
    for n, edges in enumerate((e1, e2, e3)):
        for side in range(2):
            edges[:, side] = adjoints[n][:, edge_layers(side)]
    for c in range(3):
        for y in range(3, CY - 3):
            part[c, :, NZ * y : NZ * y + NZ] = a0[c, FRIM + y, PAD : PAD + CX, 0:NZ]


def backward_kernel(
    part, e1, e2, e3, y_near, y_far, s0, s1, s2, out, a1, a2, a3, a0, mask, below, above
):
    from_partners("gy", y_near, y_far, below, above)
    places = mesh_places()
    mask[...] = row_mask(places[0], places[1])
    adjoints = (a1, a2, a3)
    out[...] = part[...]
    for n, edges in enumerate((e1, e2, e3)):
        for side in range(2):
            adjoints[n][:, edge_layers(side)] = edges[:, side]
        for start in (0, FRIM + CY):
            adjoints[n][:, start : start + FRIM] = jnp.zeros((3, FRIM, XH, LANES), F32)
    for piece, layer_of in ((above, lambda d: FRIM + CY - 1 + d), (below, lambda d: FRIM - d)):
        for b, (n, c, i) in enumerate(FORCE_BLOCKS):
            adjoints[n][c, layer_of(i + 1), PAD : PAD + CX, :] = unpack(piece[b * PACKED : b * PACKED + PACKED, :])
        base = len(FORCE_BLOCKS) * PACKED
        for row, (n, c, dist, side, k) in enumerate(FORCE_CORNERS):
            x = (PAD - k, PAD + CX - 1 + k)[side]
            adjoints[n][c, layer_of(dist), x : x + 1, :] = piece[base + row : base + row + 1, :]
    for low in (-2, CY - 1):
        pull(s2, a3, a2, low, low + 3, 4, 5, True, mask, places)
    for low in (-1, CY - 2):
        pull(s1, a2, a1, low, low + 3, 4, 5, True, mask, places)
    for low in (0, CY - 3):
        pull(s0, a1, a0, low, low + 3, PAD, 4, False, mask, places)
    for c in range(3):
        for y in (0, 1, 2, CY - 3, CY - 2, CY - 1):
            out[c, :, NZ * y : NZ * y + NZ] = a0[c, FRIM + y, PAD : PAD + CX, 0:NZ]


def swap(near, far, axis):
    def pairs(start):
        lows = range(start, lax.axis_size(axis) - 1, 2)
        return [(i, i + 1) for i in lows] + [(i + 1, i) for i in lows]

    return lax.ppermute(near, axis, pairs(0)), lax.ppermute(far, axis, pairs(1))


def local(initial_state, beam_dir, gate_obs, slot_beam, slot_cell):
    peers, capacity = slot_beam.shape[1:]
    beams = beam_dir.shape[1]
    rows = peers * capacity // LANES
    x_rim = (16, CY * NZ)
    edge = (3, ROWS, CY * NZ)
    near, far = pl.pallas_call(
        state_rows_kernel,
        out_shape=(shape(*x_rim), shape(*x_rim)),
        in_specs=[
            pl.BlockSpec(edge, lambda i: (0, 0, 0)),
            pl.BlockSpec(edge, lambda i: (0, GROUPS - 1, 0)),
        ],
        out_specs=(pl.BlockSpec(x_rim, lambda i: (0, 0)), pl.BlockSpec(x_rim, lambda i: (0, 0))),
        grid=(1,),
        scratch_shapes=[pltpu.VMEM(x_rim, F32)] * 2,
        compiler_params=pltpu.CompilerParams(vmem_limit_bytes=8 * MIB),
    )(initial_state, initial_state)
    x_near, x_far = swap(near, far, "gx")
    lists = (peers, 8, capacity)
    slots = call(
        arrange_kernel,
        shape(*lists),
        [pltpu.VMEM(lists, F32), pltpu.VMEM((peers, capacity), jnp.int32)],
        limit=60,
        ins=4,
    )(beam_dir, gate_obs, slot_beam, slot_cell)
    slots = lax.all_to_all(slots, AXES, split_axis=0, concat_axis=0, tiled=True)
    work = jax.ShapeDtypeStruct((WORK,), jnp.int32)
    slots, every_work, outer_work, inner_work = call(
        regroup_kernel,
        (shape(rows, 8, LANES), work, work, work),
        [pltpu.VMEM((LANES, LANES), F32)],
        ins=1,
        scalar_out=(1, 2, 3),
        micros=2,
    )(slots)
    field = shape(3, YH, XH, LANES)
    y_rim = (STATE_PIECE, LANES)
    near, far = call(
        state_corner_kernel,
        (shape(*y_rim), shape(*y_rim)),
        [pltpu.VMEM(y_rim, F32)] * 2 + [pltpu.VMEM(x_rim, F32)] * 2,
        ins=3,
    )(initial_state, x_near, x_far)
    y_near, y_far = swap(near, far, "gy")
    mask = pltpu.VMEM((XH, LANES), F32)
    seen, sums, s0, s1, s2 = call(
        functools.partial(forward_kernel, beams),
        (shape(STEPS, rows, LANES), shape(peers, 1, STEPS * beams * peers), field, field, field),
        [pltpu.VMEM(field.shape, F32), pltpu.VMEM((GROUPS, 2 * FIELDS * NZ, GROUP), BF16), mask]
        + [pltpu.VMEM(y_rim, F32)] * 2
        + [pltpu.VMEM(x_rim, F32)] * 2,
        limit=32,
        ins=7,
        scalar_in=(0,),
    )(every_work, initial_state, x_near, x_far, y_near, y_far, slots)
    sums = lax.all_to_all(sums, AXES, split_axis=0, concat_axis=0, tiled=True)
    x_rim = (len(FORCE_BLOCKS), PACKED, LANES)
    parts = [shape(FIELDS, count, CY, ROWS, LANES) for count in (1, GROUPS - 1)]
    totals = [pltpu.VMEM((count, FIELDS, LANES, GROUP), F32) for count in (1, GROUPS - 1)]
    outer, weight, near, far = call(
        functools.partial(outer_force_kernel, beams),
        (parts[0], shape(FIELDS, rows, LANES), shape(*x_rim), shape(*x_rim)),
        [pltpu.VMEM(x_rim, F32)] * 2 + [totals[0]],
        limit=24,
        ins=4,
        scalar_in=(0,),
    )(outer_work, slots, seen, sums)
    x_near, x_far = swap(near, far, "gx")
    inner = call(inner_force_kernel, parts[1], [totals[1]], limit=24, ins=3, scalar_in=(0,), micros=6)(
        inner_work, slots, weight
    )
    y_rim = (FORCE_PIECE, LANES)
    near, far = call(
        force_rim_kernel,
        (shape(*y_rim), shape(*y_rim)),
        [pltpu.VMEM(y_rim, F32)] * 2 + [pltpu.VMEM(x_rim, F32)] * 2,
        ins=4,
    )(outer, inner, x_near, x_far)
    y_near, y_far = swap(near, far, "gy")
    edges = shape(3, 2, EDGE, XH, LANES)
    adjoint = pltpu.VMEM((3, FH, XH, LANES), F32)
    whole = shape(*initial_state.shape)
    part, e1, e2, e3 = call(
        inner_backward_kernel,
        (whole, edges, edges, edges),
        [adjoint] * 4 + [mask] + [pltpu.VMEM(x_rim, F32)] * 2,
        limit=32,
        ins=7,
        micros=8,
    )(outer, inner, x_near, x_far, s0, s1, s2)
    return call(
        backward_kernel, whole, [adjoint] * 4 + [mask] + [pltpu.VMEM(y_rim, F32)] * 2, limit=32, ins=9
    )(part, e1, e2, e3, y_near, y_far, s0, s1, s2)


def solution(mesh):
    in_specs = (
        P(None, "gx", "gy"),
        P(None, ("gx", "gy")),
        P(None, ("gx", "gy"), None, None),
        P(("gx", "gy"), None, None),
        P(("gx", "gy"), None, None),
    )
    out_specs = P(None, "gx", "gy")
    return jax.shard_map(local, mesh=mesh, in_specs=in_specs, out_specs=out_specs, check_vma=False)
```
